32 devices in a mesh: dp: 8 (over z, core), mp: 4 (over y, x).
Axes of the slice: x: 2, y: 2, z: 4, core: 2. Of those that a mesh axis runs over, the one named last changes fastest.
Arguments:
- tokens: bfloat16 [20480, 1024], P('dp'), may hold values from -6 to 6
- lengths: int32 [8, 9], P('dp'), may hold values from 1 to 1024, 2560 in all within a row
- cotangent: bfloat16 [20480, 1024], P('dp'), may hold values from -6 to 6
- norm1_gain: float32 [1024], replicated, may hold values from 0.5 to 1.5
- norm1_bias: float32 [1024], replicated, may hold values from -3 to 3
- w_query: bfloat16 [1024, 1024], P(None, 'mp'), may hold values from -0.25 to 0.25
- w_key: bfloat16 [1024, 1024], P(None, 'mp'), may hold values from -0.25 to 0.25
- w_value: bfloat16 [1024, 1024], P(None, 'mp'), may hold values from -0.1875 to 0.1875
- w_output: bfloat16 [1024, 1024], P('mp'), may hold values from -0.75 to 0.75
- norm2_gain: float32 [1024], replicated, may hold values from 0.5 to 1.5
- norm2_bias: float32 [1024], replicated, may hold values from -3 to 3
- w_gate: bfloat16 [1024, 4096], P(None, 'mp'), may hold values from -0.1875 to 0.1875
- w_up: bfloat16 [1024, 4096], P(None, 'mp'), may hold values from -0.1875 to 0.1875
- w_down: bfloat16 [4096, 1024], P('mp'), may hold values from -0.1875 to 0.1875
Outputs:
- output: bfloat16 [20480, 1024], P(('dp', 'mp'))
- tokens_grad: bfloat16 [20480, 1024], P(('dp', 'mp'))
- query_grad: float32 [1024, 1024], P('dp', 'mp')
- key_grad: float32 [1024, 1024], P('dp', 'mp')
- value_grad: float32 [1024, 1024], P('dp', 'mp')
- output_proj_grad: float32 [1024, 1024], P('mp', 'dp')
- gate_grad: float32 [1024, 4096], P('dp', 'mp')
- up_grad: float32 [1024, 4096], P('dp', 'mp')
- down_grad: float32 [4096, 1024], P('mp', 'dp')
- norm1_gain_grad: float32 [1024], P('dp')
- norm1_bias_grad: float32 [1024], P('dp')
- norm2_gain_grad: float32 [1024], P('dp')
- norm2_bias_grad: float32 [1024], P('dp')
The draws below stay inside these ranges and needn't reach their ends.
Inputs may be any that keep to these rules, and one draw needn't show every extreme that they name: Row i lists the lengths of 8 windows packed in order from the first row of pack i, then the number of padding rows at its end; each row sums to 2560 and its largest entry is exactly 1024.
All inputs are finite; a program needn't handle non-finite values.
Results may differ from the reference program's by a relative error of at most 0.025.
Values may be sent and summed in bfloat16 or wider, within the bound.
A program may use at most 256 MiB of HBM per device.

```python
import math
import jax
import jax.numpy as jnp
import numpy as np
from jax import lax

D = 1024
HEADS = 16
HD = 64
FF = 4096
TOK_DEV = 2560
WINS = 9
MOST = 1024
TOKENS = 20480
N_DP = 8


def levels(own_key, shape, cuts, smallest, largest):
    def one(dim, blocks):
        draws = jax.random.uniform(jax.random.fold_in(jax.random.fold_in(own_key, 6), dim), (blocks,), jnp.float32, smallest / len(cuts), largest / len(cuts))
        return jnp.repeat(jnp.exp(draws), shape[dim] // blocks).reshape((-1,) + (1,) * (len(shape) - dim - 1))

    gain = one(*cuts[0])
    for cut in cuts[1:]:
        gain = gain * one(*cut)
    return gain


def split_up(amount, total, most, skew):
    portions = [(1 << 20) // math.isqrt(grade ** skew) + 1 for grade in range(2, amount + 1)]
    surplus, holding = total - most - (amount - 1), [1] * (amount - 1)
    while surplus > 0:
        candidates = [i for i in range(amount - 1) if holding[i] < most]
        mass, budget = sum([portions[i] for i in candidates]), surplus
        for i in candidates:
            extra = min(most - holding[i], max(1, budget * portions[i] // mass), surplus)
            holding[i] = holding[i] + extra
            surplus = surplus - extra
    return np.array([most] + holding)


def uneven_parts(own_key, count, total, most, lean):
    if count == 2:
        one = jax.random.randint(own_key, (), max(1, total - most), min(most, total - 1) + 1)
        return jnp.stack([one, total - one])
    sizes = jnp.asarray(split_up(count, total, most, lean), jnp.int32)
    pairs = (count - 1) // 2
    giver, receiver = sizes[1:1 + 2 * pairs:2], sizes[2:2 + 2 * pairs:2]
    margin = jnp.minimum(giver - 1, most - receiver)
    shifted = jax.random.randint(jax.random.fold_in(own_key, 1), (pairs,), 0, 1 << 20) % (margin + 1)
    sizes = sizes.at[1:1 + 2 * pairs:2].set(giver - shifted).at[2:2 + 2 * pairs:2].set(receiver + shifted)
    return sizes[jax.random.permutation(jax.random.fold_in(own_key, 2), count)]


def bell_draw(rng, shape, deviation, limit, cuts=(), kind=jnp.bfloat16):
    values = jax.random.normal(rng, shape, jnp.float32) * deviation
    if len(cuts) > 0:
        values = levels(rng, shape, cuts, -0.22, 0.18) * values
    return jnp.clip(values, min=-limit, max=limit).astype(kind)


def setup_inputs(seed: int = 0) -> dict:
    seeds = jax.random.split(jax.random.key(seed), 15)
    tokens = bell_draw(seeds[0], (TOKENS, D), 1.0, 6.0, ((0, 8),))
    lengths = jax.vmap(lambda own: uneven_parts(own, WINS, TOK_DEV, MOST, 2))(jax.random.split(seeds[1], N_DP)).reshape((N_DP, WINS)).astype(jnp.int32)
    cotangent = bell_draw(seeds[2], (TOKENS, D), 1.0, 6.0, ((0, 8),))
    norm1_gain = jnp.clip(1.0 + 0.1 * jax.random.normal(seeds[3], (D,), jnp.float32), 0.5, 1.5)
    norm1_bias = bell_draw(seeds[4], (D,), 0.5, 3.0, (), jnp.float32)
    w_query = bell_draw(seeds[5], (D, D), (D // 2) ** -0.5, 0.25, ((1, 4),))
    w_key = bell_draw(seeds[6], (D, D), (D // 2) ** -0.5, 0.25, ((1, 4),))
    w_value = bell_draw(seeds[7], (D, D), D ** -0.5, 0.1875, ((1, 4),))
    w_output = bell_draw(seeds[8], (D, D), (D // 16) ** -0.5, 0.75, ((0, 4),))
    norm2_gain = jnp.clip(1.0 + 0.1 * jax.random.normal(seeds[9], (D,), jnp.float32), 0.5, 1.5)
    norm2_bias = bell_draw(seeds[10], (D,), 0.5, 3.0, (), jnp.float32)
    w_gate = bell_draw(seeds[11], (D, FF), D ** -0.5, 0.1875, ((1, 4),))
    w_up = bell_draw(seeds[12], (D, FF), D ** -0.5, 0.1875, ((1, 4),))
    w_down = bell_draw(seeds[13], (FF, D), (FF // 4) ** -0.5, 0.1875, ((0, 4),))
    return dict(tokens=tokens, lengths=lengths, cotangent=cotangent, norm1_gain=norm1_gain, norm1_bias=norm1_bias, w_query=w_query, w_key=w_key, w_value=w_value, w_output=w_output, norm2_gain=norm2_gain, norm2_bias=norm2_bias, w_gate=w_gate, w_up=w_up, w_down=w_down)


epsilon = 1e-05
rotary_base = 10000.0
highest = lax.Precision.HIGHEST

@jax.custom_vjp
def low(v):
    return lax.optimization_barrier(v.astype(jnp.bfloat16)).astype(jnp.float32)

@jax.custom_vjp
def low_back(v):
    return v

def low_keep(v):
    return (low(v), None)

def low_pass(kept, grad):
    return (grad,)

def back_keep(v):
    return (v, None)

def back_low(kept, grad):
    return (low(grad),)
low.defvjp(low_keep, low_pass)
low_back.defvjp(back_keep, back_low)

def window_tables(lengths_row, rows_total, head_size):
    window_ends = jnp.cumsum(lengths_row).astype(jnp.int32)
    position = jnp.arange(rows_total, dtype=jnp.int32)
    passed = (position[:, None] >= window_ends[None, :]).astype(jnp.int32)
    segment = lax.optimization_barrier(jnp.sum(passed, axis=1)).astype(jnp.int32)
    window_start = lax.optimization_barrier(jnp.sum(passed * lengths_row[None, :], axis=1)).astype(jnp.int32)
    offset = (position - window_start).astype(jnp.float32)
    half_size = head_size // 2
    frequency = rotary_base ** (-2.0 * jnp.arange(half_size, dtype=jnp.float32) / head_size)
    angles = offset[:, None] * frequency[None, :]
    angles = jnp.concatenate([angles, angles], axis=1)
    return (segment, jnp.cos(angles), jnp.sin(angles))

def layer_norm(row_values, gain_vec, bias_vec):
    row_mean = lax.optimization_barrier(jnp.mean(row_values, axis=-1, keepdims=True))
    centred = row_values - row_mean
    row_scale = lax.rsqrt(lax.optimization_barrier(jnp.mean(centred * centred, axis=-1, keepdims=True)) + epsilon)
    return centred * row_scale * gain_vec + bias_vec

def rotate(field, cosine, sine_table, direction):
    row_count = field.shape[0]
    head_size = cosine.shape[1]
    pieces = field.reshape(row_count, field.shape[1] // head_size, head_size)
    half_size = head_size // 2
    turned = jnp.concatenate([-pieces[..., half_size:], pieces[..., :half_size]], axis=-1)
    result = pieces * cosine[:, None, :] + direction * turned * sine_table[:, None, :]
    return result.reshape(row_count, field.shape[1])

def attend_pack(pack_items):
    queries, keys_rot, values, segment = pack_items
    row_count = queries.shape[0]
    block_rows = min(512, row_count)
    block_count = row_count // block_rows

    def one_block(block_items):
        query_block, segment_block = block_items
        scores = jnp.einsum('qhd,khd->hqk', query_block, keys_rot, precision=highest)
        scores = low_back(scores * HD ** (-0.5))
        same_window = (segment_block[:, None] == segment[None, :])[None]
        scores = jnp.where(same_window, scores, -1e+30)
        row_top = lax.optimization_barrier(jnp.max(scores, axis=-1, keepdims=True))
        exp_scores = jnp.exp(scores - row_top)
        attn_prob = exp_scores / lax.optimization_barrier(jnp.sum(exp_scores, axis=-1, keepdims=True))
        return jnp.einsum('hqk,khd->qhd', low(attn_prob), values, precision=highest)
    mixed_blocks = lax.map(jax.checkpoint(one_block), (queries.reshape(block_count, block_rows, HEADS, HD), segment.reshape(block_count, block_rows)))
    return mixed_blocks.reshape(row_count, HEADS, HD)

def reference(tokens, lengths, cotangent, norm1_gain, norm1_bias, w_query, w_key, w_value, w_output, norm2_gain, norm2_bias, w_gate, w_up, w_down):
    tables = jax.vmap(lambda lengths_row: window_tables(lengths_row, TOK_DEV, HD))(lengths)
    segment = tables[0].reshape(TOKENS)
    cosine = tables[1].reshape(TOKENS, HD)
    sine_table = tables[2].reshape(TOKENS, HD)
    live_rows = (segment < WINS - 1).astype(jnp.float32)

    def forward(tokens_f, gain_first, bias_first, query_w, key_w, value_w, output_w, gain_second, bias_second, gate_w, up_w, down_w):
        inputs_first = low(layer_norm(tokens_f, gain_first, bias_first))
        queries = low_back(jnp.dot(inputs_first, query_w, precision=highest))
        keys_pre = low_back(jnp.dot(inputs_first, key_w, precision=highest))
        values = low(low_back(jnp.dot(inputs_first, value_w, precision=highest)))
        queries_rot = low(rotate(queries, cosine, sine_table, 1.0))
        keys_rot = low(rotate(keys_pre, cosine, sine_table, 1.0))
        shaped = (queries_rot.reshape(N_DP, TOK_DEV, HEADS, HD), keys_rot.reshape(N_DP, TOK_DEV, HEADS, HD), values.reshape(N_DP, TOK_DEV, HEADS, HD), segment.reshape(N_DP, TOK_DEV))
        mixed_heads = lax.map(jax.checkpoint(attend_pack), shaped).reshape(TOKENS, D)
        mixed_low = low(low_back(mixed_heads))
        residual = tokens_f + low_back(jnp.dot(mixed_low, output_w, precision=highest))
        inputs_second = low(layer_norm(residual, gain_second, bias_second))
        gate_pre = low_back(jnp.dot(inputs_second, gate_w, precision=highest))
        up_proj = low_back(jnp.dot(inputs_second, up_w, precision=highest))
        hidden = low(jax.nn.silu(gate_pre) * up_proj)
        return residual + low_back(jnp.dot(hidden, down_w, precision=highest))
    floats = (tokens.astype(jnp.float32), norm1_gain.astype(jnp.float32), norm1_bias.astype(jnp.float32), w_query.astype(jnp.float32), w_key.astype(jnp.float32), w_value.astype(jnp.float32), w_output.astype(jnp.float32), norm2_gain.astype(jnp.float32), norm2_bias.astype(jnp.float32), w_gate.astype(jnp.float32), w_up.astype(jnp.float32), w_down.astype(jnp.float32))
    output, pull_back = jax.vjp(forward, *floats)
    gradients = pull_back(cotangent.astype(jnp.float32) * live_rows[:, None])
    return (output.astype(jnp.bfloat16), gradients[0].astype(jnp.bfloat16), gradients[3], gradients[4], gradients[5], gradients[6], gradients[9], gradients[10], gradients[11], gradients[1], gradients[2], gradients[7], gradients[8])
```

```python
import functools
import math

import jax
import jax.numpy as jnp
import numpy as np
from jax import lax
from jax.experimental import pallas as pl
from jax.experimental.pallas import tpu as pltpu
from jax.sharding import PartitionSpec as P

HD = 64
HALF = HD // 2
PAIR = 2 * HD
QB = 128
KB = 256
EPS = 1e-05
BASE = 10000.0
NEG = -1e30
MOST = 1024
SCALE = HD**-0.5
VMEM = pl.BlockSpec(memory_space=pltpu.VMEM)
SMEM = pl.BlockSpec(memory_space=pltpu.SMEM)
ANY = pl.BlockSpec(memory_space=pl.ANY)
MESH = pl.DeviceIdType.MESH
STEPS = 5
EARLY = 2
PIECES = 4
DIRECT = 1
VMEM_CAP = 62 << 20
F32 = jnp.float32
BF16 = jnp.bfloat16


def mm(a, b):
    return jnp.dot(a, b, preferred_element_type=F32)


def mm_nt(a, b):
    return lax.dot_general(a, b, (((1,), (1,)), ((), ())), preferred_element_type=F32)


def mm_tn(a, b):
    return lax.dot_general(a, b, (((0,), (0,)), ((), ())), preferred_element_type=F32)


def window_bounds(len_ref, position):
    entries = len_ref.shape[1]
    start = jnp.zeros_like(position)
    end = jnp.zeros_like(position)
    edge = jnp.int32(0)
    for entry in range(entries):
        size = len_ref[0, entry]
        inside = position >= edge
        start = jnp.where(inside, edge, start)
        edge = edge + size
        end = jnp.where(inside, edge, end)
    return start, end


def norm_rows(rows):
    mean = jnp.mean(rows, axis=-1, keepdims=True)
    centred = rows - mean
    scale = lax.rsqrt(jnp.mean(centred * centred, axis=-1, keepdims=True) + EPS)
    return centred * scale, scale


def rotate_t(field, cosine, sine, direction):
    parts = []
    for head in range(field.shape[0] // HD):
        first = field[head * HD : head * HD + HALF]
        second = field[head * HD + HALF : (head + 1) * HD]
        parts.append(first * cosine - direction * (second * sine))
        parts.append(second * cosine + direction * (first * sine))
    return jnp.concatenate(parts, axis=0)


def qkv_kernel(
    len_ref, tok_ref, gain_ref, bias_ref, freq_ref, wq_ref, wk_ref, wv_ref,
    a1_ref, k_ref, v_ref, qt_ref, kt_ref, vt_ref, cos_ref, sin_ref,
):
    rows = tok_ref.shape[0]
    position = lax.broadcasted_iota(jnp.int32, (1, rows), 1) + pl.program_id(0) * rows
    start, _ = window_bounds(len_ref, position)
    offset = (position - start).astype(F32)
    theta = freq_ref[...] * offset
    cosine, sine = jnp.cos(theta), jnp.sin(theta)
    cos_ref[...] = cosine
    sin_ref[...] = sine
    hat, _ = norm_rows(tok_ref[...].astype(F32))
    a1 = (hat * gain_ref[...] + bias_ref[...]).astype(BF16)
    a1_ref[...] = a1
    for w_ref, out_ref, out_t_ref, scale in (
        (wq_ref, None, qt_ref, SCALE),
        (wk_ref, k_ref, kt_ref, None),
    ):
        field = rotate_t(mm(a1, w_ref[...]).T, cosine, sine, 1.0).astype(BF16)
        if scale is not None:
            field = field * jnp.asarray(scale, BF16)
        out_t_ref[...] = field
        if out_ref is not None:
            out_ref[...] = field.T
    values = mm(a1, wv_ref[...]).astype(BF16)
    v_ref[...] = values
    vt_ref[...] = values.T


def project(lengths, tokens, gain, bias, wq, wk, wv):
    rows, width = tokens.shape
    feats = wq.shape[1]
    block = min(512, rows)
    freq = np.float32(BASE) ** (np.float32(-2.0 / HD) * np.arange(HALF, dtype=np.float32))
    freq = jnp.asarray(freq[:, None], F32)
    whole = lambda a: pl.BlockSpec(a.shape, lambda i: (0, 0))
    by_row = lambda cols: pl.BlockSpec((block, cols), lambda i: (i, 0))
    by_col = lambda size: pl.BlockSpec((size, block), lambda i: (0, i))
    nat = jax.ShapeDtypeStruct((rows, feats), BF16)
    trans = jax.ShapeDtypeStruct((feats, rows), BF16)
    table = jax.ShapeDtypeStruct((HALF, rows), F32)
    return pl.pallas_call(
        qkv_kernel,
        grid=(rows // block,),
        in_specs=[SMEM, by_row(width)] + [whole(a) for a in (gain, bias, freq, wq, wk, wv)],
        out_specs=[by_row(width)] + [by_row(feats)] * 2 + [by_col(feats)] * 3 + [by_col(HALF)] * 2,
        out_shape=[jax.ShapeDtypeStruct((rows, width), BF16)] + [nat] * 2 + [trans] * 3 + [table] * 2,
        compiler_params=pltpu.CompilerParams(vmem_limit_bytes=VMEM_CAP),
        cost_estimate=pl.CostEstimate(
            flops=6 * rows * width * feats, bytes_accessed=rows * width * 8, transcendentals=0
        ),
        name="qkv",
    )(lengths, tokens, gain, bias, freq, wq, wk, wv)


def block_diagonal_t(pair):
    head = lax.broadcasted_iota(jnp.int32, pair.shape, 0) < HD
    zero = jnp.zeros_like(pair)
    return jnp.concatenate([jnp.where(head, pair, zero), jnp.where(head, zero, pair)], axis=1)


def diagonal_blocks(product):
    return jnp.concatenate([product[:HD, :QB], product[HD:, QB:]], axis=1)


def key_range(len_ref, first):
    low, _ = window_bounds(len_ref, first)
    _, high = window_bounds(len_ref, first + (QB - 1))
    base = low // QB * QB
    return base, (high - base + (KB - 1)) // KB


def key_rows(at, rows):
    return pl.ds(pl.multiple_of(jnp.clip(at, 0, rows - KB), QB), KB)


def inside_window(start, end, at, rows):
    shift = jnp.minimum(at, rows - KB)
    key = lax.broadcasted_iota(jnp.int32, (KB, QB), 0)
    inside = (key >= jnp.maximum(start, at) - shift) & (key < end - shift)
    return jnp.concatenate([inside, inside], axis=1)


def fill_schedule(len_ref, sched, blocks, index_of, rows):
    def nothing(n):
        sched[0, n] = 0
        sched[1, n] = rows

    def one_query(turn, n):
        base, count = key_range(len_ref, index_of(turn) * QB)

        def one_key(kb, _):
            sched[0, n + kb] = turn
            sched[1, n + kb] = base + kb * KB
            return 0

        lax.fori_loop(0, count, one_key, 0)
        return n + count

    nothing(0)
    n = lax.fori_loop(0, blocks, one_query, jnp.int32(1))
    for extra in range(3):
        nothing(n + extra)
    return n - 1


def store_window(len_ref, window, turn, first):
    position = lax.broadcasted_iota(jnp.int32, (1, QB), 1) + first
    window[turn, 0:1], window[turn, 1:2] = window_bounds(len_ref, position)


def run_pipeline(count, scores, soften, mix):
    def two_pairs(turn, _):
        n = 1 + 2 * turn
        mix(n - 1, 1)
        scores(n + 1, 1)
        soften(n, 0)
        mix(n, 0)
        scores(n + 2, 0)
        soften(n + 1, 1)
        return 0

    turns = (count + 1) // 2
    scores(1, 0)
    lax.fori_loop(0, turns, two_pairs, 0)
    mix(2 * turns, 1)


def attend_kernel(begin, steps, len_ref, qt_ref, k_ref, vt_ref, *rest):
    if begin > 0:
        ot_before, lse_before, *rest = rest
    o_ref, ot_ref, lse_ref, sched, window, diag, stat, acc, keep_buf, score_buf, prob_buf = rest
    if begin > 0:
        ot_ref[...] = ot_before[...]
        lse_ref[...] = lse_before[...]
    owners, taken = o_ref.shape[:2]
    feats, rows = qt_ref.shape
    pairs = range(feats // PAIR)
    feat = [pl.ds(p * PAIR, PAIR) for p in pairs]

    def index_of(turn):
        return turn // taken * steps + begin + lax.rem(turn, taken)

    def prepare(turn, _):
        first = index_of(turn) * QB
        cols = pl.ds(pl.multiple_of(first, QB), QB)
        store_window(len_ref, window, turn, first)
        for p in pairs:
            diag[turn, p] = block_diagonal_t(qt_ref[feat[p], cols])
            stat[turn, p : p + 1] = jnp.full((1, 2 * QB), NEG, F32)
            stat[turn, 4 + p : 5 + p] = jnp.zeros((1, 2 * QB), F32)
            acc[turn, p] = jnp.zeros((HD, 2 * QB), F32)
        return 0

    lax.fori_loop(0, owners * taken, prepare, 0)
    count = fill_schedule(len_ref, sched, owners * taken, index_of, rows)

    def scores(n, buf):
        turn, keys = sched[0, n], key_rows(sched[1, n], rows)
        for p in pairs:
            score_buf[buf, p] = mm(k_ref[keys, feat[p]], diag[turn, p])

    def soften(n, buf):
        turn = sched[0, n]
        inside = inside_window(window[turn, 0:1], window[turn, 1:2], sched[1, n], rows)
        for p in pairs:
            top, total = stat[turn, p : p + 1], stat[turn, 4 + p : 5 + p]
            values = jnp.where(inside, score_buf[buf, p], NEG)
            new_top = jnp.maximum(top, jnp.max(values, axis=0, keepdims=True))
            prob = jnp.exp(values - new_top)
            keep = jnp.exp(top - new_top)
            stat[turn, p : p + 1] = new_top
            stat[turn, 4 + p : 5 + p] = keep * total + jnp.sum(prob, axis=0, keepdims=True)
            keep_buf[buf, p : p + 1] = keep
            prob_buf[buf, p] = prob.astype(BF16)

    def mix(n, buf):
        turn, keys = sched[0, n], key_rows(sched[1, n], rows)
        for p in pairs:
            mixed = diagonal_blocks(mm(vt_ref[feat[p], keys], prob_buf[buf, p]))
            acc[turn, p] = acc[turn, p] * keep_buf[buf, p : p + 1] + mixed

    prob_buf[1] = jnp.zeros_like(prob_buf[1])
    keep_buf[1] = jnp.ones_like(keep_buf[1])
    run_pipeline(count, scores, soften, mix)

    def finish(turn, _):
        index = index_of(turn)
        cols = pl.ds(pl.multiple_of(index * QB, QB), QB)
        for p in pairs:
            top, total = stat[turn, p : p + 1], stat[turn, 4 + p : 5 + p]
            mixed = acc[turn, p] / total
            mixed = jnp.concatenate([mixed[:, :QB], mixed[:, QB:]], axis=0).astype(BF16)
            lse_ref[index, p : p + 1] = top + jnp.log(total)
            ot_ref[feat[p], cols] = mixed
            o_ref[turn // taken, lax.rem(turn, taken), :, feat[p]] = mixed.T
        return 0

    lax.fori_loop(0, owners * taken, finish, 0)


def schedule_size(blocks):
    return blocks * ((2 * MOST + 2 * QB) // KB + 1) + 4


def attend(lengths, qt, k, vt, begin, end, steps, before=()):
    feats, rows = qt.shape
    pairs = feats // PAIR
    owners = rows // (steps * QB)
    share = (end - begin) / steps
    blocks = owners * (end - begin)
    return pl.pallas_call(
        functools.partial(attend_kernel, begin, steps),
        in_specs=[SMEM] + [VMEM] * (3 + len(before)),
        out_specs=[VMEM, VMEM, VMEM],
        out_shape=[
            jax.ShapeDtypeStruct((owners, end - begin, QB, feats), BF16),
            jax.ShapeDtypeStruct((feats, rows), BF16),
            jax.ShapeDtypeStruct((rows // QB, pairs, 2 * QB), F32),
        ],
        scratch_shapes=[
            pltpu.SMEM((2, schedule_size(blocks)), jnp.int32),
            pltpu.VMEM((blocks, 8, QB), jnp.int32),
            pltpu.VMEM((blocks, pairs, PAIR, 2 * QB), BF16),
            pltpu.VMEM((blocks, 8, 2 * QB), F32),
            pltpu.VMEM((blocks, pairs, HD, 2 * QB), F32),
            pltpu.VMEM((2, 8, 2 * QB), F32),
            pltpu.VMEM((2, pairs, KB, 2 * QB), F32),
            pltpu.VMEM((2, pairs, KB, 2 * QB), BF16),
        ],
        compiler_params=pltpu.CompilerParams(vmem_limit_bytes=VMEM_CAP),
        cost_estimate=pl.CostEstimate(
            flops=int(8 * share * rows * rows * feats),
            bytes_accessed=rows * feats * 10,
            transcendentals=int(share * rows * rows),
        ),
        name="attend",
    )(lengths, qt, k, vt, *before)


def attend_back_kernel(
    len_ref, qt_ref, k_ref, kt_ref, v_ref, do_ref, ot_ref, lse_ref, cos_ref, sin_ref,
    grad_ref, grad_t_ref, sched, window, q_diag, do_diag, stat, dq_acc, dk_acc, dv_acc,
    score_buf, prob_grad_buf, prob_buf, score_grad_buf,
):
    feats, rows = qt_ref.shape
    pairs = range(feats // PAIR)
    feat = [pl.ds(p * PAIR, PAIR) for p in pairs]
    dk_acc[...] = jnp.zeros_like(dk_acc)
    dv_acc[...] = jnp.zeros_like(dv_acc)
    dq_acc[...] = jnp.zeros_like(dq_acc)

    def prepare(turn, _):
        cols = pl.ds(pl.multiple_of(turn * QB, QB), QB)
        store_window(len_ref, window, turn, turn * QB)
        for p in pairs:
            do_t = do_ref[cols, feat[p]].T
            delta = do_t.astype(F32) * ot_ref[feat[p], cols].astype(F32)
            delta = [jnp.sum(part, axis=0, keepdims=True) for part in (delta[:HD], delta[HD:])]
            q_diag[turn, p] = block_diagonal_t(qt_ref[feat[p], cols])
            do_diag[turn, p] = block_diagonal_t(do_t)
            stat[turn, p : p + 1] = lse_ref[turn, p : p + 1]
            stat[turn, 4 + p : 5 + p] = jnp.concatenate(delta, axis=1)
        return 0

    lax.fori_loop(0, rows // QB, prepare, 0)
    count = fill_schedule(len_ref, sched, rows // QB, lambda turn: turn, rows)

    def scores(n, buf):
        turn, keys = sched[0, n], key_rows(sched[1, n], rows)
        for p in pairs:
            score_buf[buf, p] = mm(k_ref[keys, feat[p]], q_diag[turn, p])
            prob_grad_buf[buf, p] = mm(v_ref[keys, feat[p]], do_diag[turn, p])

    def soften(n, buf):
        turn = sched[0, n]
        inside = inside_window(window[turn, 0:1], window[turn, 1:2], sched[1, n], rows)
        for p in pairs:
            lse, delta = stat[turn, p : p + 1], stat[turn, 4 + p : 5 + p]
            prob = jnp.where(inside, jnp.exp(score_buf[buf, p] - lse), 0.0)
            prob_buf[buf, p] = prob.astype(BF16)
            score_grad_buf[buf, p] = (prob * (prob_grad_buf[buf, p] - delta)).astype(BF16)

    def mix(n, buf):
        turn, keys = sched[0, n], key_rows(sched[1, n], rows)
        for p in pairs:
            dv_acc[feat[p], keys] += mm_nt(do_diag[turn, p], prob_buf[buf, p])
            dk_acc[feat[p], keys] += mm_nt(q_diag[turn, p], score_grad_buf[buf, p])
            dq_acc[turn, p] += diagonal_blocks(mm(kt_ref[feat[p], keys], score_grad_buf[buf, p]))

    prob_buf[1] = jnp.zeros_like(prob_buf[1])
    score_grad_buf[1] = jnp.zeros_like(score_grad_buf[1])
    run_pipeline(count, scores, soften, mix)

    def finish(turn, _):
        cols = pl.ds(pl.multiple_of(turn * QB, QB), QB)
        cosine, sine = cos_ref[:, cols], sin_ref[:, cols]
        for p in pairs:
            dq = jnp.concatenate([dq_acc[turn, p, :, :QB], dq_acc[turn, p, :, QB:]], axis=0) * SCALE
            fields = (
                rotate_t(dq, cosine, sine, -1.0),
                rotate_t(dk_acc[feat[p], cols], cosine, sine, -1.0),
                dv_acc[feat[p], cols],
            )
            for kind, field in enumerate(fields):
                place = pl.ds(kind * feats + p * PAIR, PAIR)
                field = field.astype(BF16)
                grad_t_ref[place, cols] = field
                grad_ref[cols, place] = field.T
        return 0

    lax.fori_loop(0, rows // QB, finish, 0)


def attend_back(lengths, qt, k, kt, v, do, ot, lse, cosine, sine):
    feats, rows = qt.shape
    blocks = rows // QB
    return pl.pallas_call(
        attend_back_kernel,
        in_specs=[SMEM] + [VMEM] * 9,
        out_specs=[VMEM, VMEM],
        out_shape=[
            jax.ShapeDtypeStruct((rows, 3 * feats), BF16),
            jax.ShapeDtypeStruct((3 * feats, rows), BF16),
        ],
        scratch_shapes=[
            pltpu.SMEM((2, schedule_size(blocks)), jnp.int32),
            pltpu.VMEM((blocks, 8, QB), jnp.int32),
            pltpu.VMEM((blocks, feats // PAIR, PAIR, 2 * QB), BF16),
            pltpu.VMEM((blocks, feats // PAIR, PAIR, 2 * QB), BF16),
            pltpu.VMEM((blocks, 8, 2 * QB), F32),
            pltpu.VMEM((blocks, feats // PAIR, HD, 2 * QB), F32),
            pltpu.VMEM((feats, rows), F32),
            pltpu.VMEM((feats, rows), F32),
        ]
        + [pltpu.VMEM((2, feats // PAIR, KB, 2 * QB), kind) for kind in (F32, F32, BF16, BF16)],
        compiler_params=pltpu.CompilerParams(vmem_limit_bytes=VMEM_CAP),
        cost_estimate=pl.CostEstimate(
            flops=10 * rows * rows * feats, bytes_accessed=rows * feats * 28, transcendentals=rows * rows
        ),
        name="attend_back",
    )(lengths, qt, k, kt, v, do, ot, lse, cosine, sine)


def neighbours():
    me = lax.axis_index("mp")
    one = lax.rem(me, 2)
    across = me + 1 - 2 * one
    along = lax.rem(me + 2, 4)
    return me, across, along, lax.rem(across + 2, 4)


def remote(src, dst, sems, kind, step, device):
    send, recv = sems
    return pltpu.make_async_remote_copy(
        src_ref=src,
        dst_ref=dst,
        send_sem=send.at[kind, step],
        recv_sem=recv.at[kind, step],
        device_id={"mp": device},
        device_id_type=MESH,
    )


def pack_neighbours(packs):
    index = lax.axis_index("dp")
    core, chip = lax.rem(index, 2), index // 2
    chips = packs // 2
    return core, chip, index + 1 - 2 * core, [
        lax.rem(index + 2 * shift, packs) for shift in range(1, chips)
    ]


def chip_across(chip, bits):
    low, high = lax.rem(chip, 2), chip // 2
    low = 1 - low if bits % 2 else low
    high = 1 - high if bits // 2 else high
    return low + 2 * high


def remote_pack(src, dst, send, recv, device):
    return pltpu.make_async_remote_copy(
        src_ref=src, dst_ref=dst, send_sem=send, recv_sem=recv,
        device_id={"dp": device}, device_id_type=MESH,
    )


CHIPS = 4
PILES = (((0, 2), 0), ((1, 3), 0), ((0, 1), 2), ((2, 3), 2))
PARTNERS = (1, 2)


def group_barrier(devices, packs=()):
    barrier = pltpu.get_barrier_semaphore()
    for device in devices:
        pl.semaphore_signal(barrier, inc=1, device_id={"mp": device}, device_id_type=MESH)
    for device in packs:
        pl.semaphore_signal(barrier, inc=1, device_id={"dp": device}, device_id_type=MESH)
    pl.semaphore_wait(barrier, len(devices) + len(packs))


def scatter_first(part, slot, from_x, from_y, sems, kind, step):
    me, x, y, d = neighbours()
    return [
        remote(part.at[slot, x, 0], from_x.at[step, 0], sems, kind, step, x),
        remote(part.at[slot, y, 1], from_y.at[step, 0], sems, kind + 1, step, y),
        remote(part.at[slot, d, 0], from_x.at[step, 1], sems, kind + 2, step, x),
        remote(part.at[slot, d, 1], from_y.at[step, 1], sems, kind + 3, step, y),
    ]


def scatter_second(from_x, from_y, last_x, last_y, sems, kind, step):
    me, x, y, d = neighbours()
    return [
        remote(from_x.at[step, 1], last_y.at[step], sems, kind + 4, step, y),
        remote(from_y.at[step, 1], last_x.at[step], sems, kind + 5, step, x),
    ]


def scatter_middle(part, slot, from_x, from_y, last_x, last_y, sems, kind, step):
    me, x, y, d = neighbours()
    first = scatter_first(part, slot, from_x, from_y, sems, kind, step)
    second = scatter_second(from_x, from_y, last_x, last_y, sems, kind, step)
    first[2].wait_recv()
    total = from_x[step, 1].astype(F32) + part[slot, y, 0].astype(F32)
    from_x[step, 1] = total.astype(BF16)
    second[0].start()
    first[3].wait_recv()
    total = from_y[step, 1].astype(F32) + part[slot, x, 1].astype(F32)
    from_y[step, 1] = total.astype(BF16)
    second[1].start()


def scatter_last(part, slot, from_x, from_y, last_x, last_y, sems, kind, step):
    me, x, y, d = neighbours()
    first = scatter_first(part, slot, from_x, from_y, sems, kind, step)
    second = scatter_second(from_x, from_y, last_x, last_y, sems, kind, step)
    first[0].wait_recv()
    first[1].wait_recv()
    second[0].wait_recv()
    second[1].wait_recv()
    upper = part[slot, me, 0].astype(F32) + from_x[step, 0].astype(F32) + last_y[step].astype(F32)
    lower = part[slot, me, 1].astype(F32) + from_y[step, 0].astype(F32) + last_x[step].astype(F32)
    for copy in first + second:
        copy.wait_send()
    return jnp.concatenate([upper, lower], axis=0)


def ffn_kernel(
    packs,
    len_ref, early0, early1, early2, early3, o_hbm, tok_hbm, cot_hbm, wo0, wo1, wo2, wo3, wg_hbm, wu_hbm, wd_hbm, gain_ref, bias_ref,
    h1_ref, dh1_ref, sums_ref, do_hbm, land_hbm, down0_hbm, down1_hbm, down2_hbm, down3_hbm, rows_hbm, *rest,
):
    chips = packs // 2
    piles = rest[: len(PILES)]
    (
        wo, wg, wu, wd, o_all, tok, cot, h1_all, hid, dgate, dup, part, from_x, from_y, last_x, last_y,
        a2_all, acc, stage, do_own, db_own, load_sem, tok_sem, cot_sem, own_sem, early_sem, stage_sem, put_sem, pile_sem,
        core_send, core_recv, send_sem, recv_sem,
    ) = rest[len(PILES) :]
    core, chip, other_core, _ = pack_neighbours(packs)
    steps, owners, block, width = o_all.shape
    share = width // packs
    feats = o_hbm.shape[-1]
    size = owners * block
    cut = dgate.shape[-1] // PIECES
    early = early0.shape[1]
    some = owners // 2
    sems = (send_sem, recv_sem)
    me, x, y, d = neighbours()
    row_total = owners * steps * block
    live_end = row_total - len_ref[0, len_ref.shape[1] - 1]

    loads = [(wg_hbm, wg), (wu_hbm, wu), (wd_hbm, wd)]
    for source, group in ((wo0, me), (wo1, x), (wo2, y), (wo3, d)):
        loads.append((source, wo.at[pl.ds(pl.multiple_of(group * feats, feats), feats)]))
    loads = [pltpu.make_async_copy(a, b, load_sem.at[i]) for i, (a, b) in enumerate(loads)]

    def fetch(step):
        slot = lax.rem(step, 2)
        return (
            pltpu.make_async_copy(tok_hbm.at[:, step], tok.at[slot], tok_sem.at[slot]),
            pltpu.make_async_copy(cot_hbm.at[:, step], cot.at[slot], cot_sem.at[slot]),
        )

    def lanes(group):
        return pl.ds(pl.multiple_of(group * feats, feats), feats)

    def early_copies(step):
        return [
            pltpu.make_async_copy(
                source.at[:, step], o_all.at[step, :, :, lanes(group)], early_sem.at[step, i]
            )
            for i, (source, group) in enumerate(
                ((early0, me), (early1, x), (early2, y), (early3, d))
            )
        ]

    def own_copy(step):
        return pltpu.make_async_copy(
            o_hbm.at[:, step - early], o_all.at[step, :, :, lanes(me)], own_sem.at[step]
        )

    def gather_own(step):
        source, target = o_hbm.at[:, step - early], o_all.at[step, :, :, lanes(me)]
        return [
            remote(source, target, sems, 0, step, x),
            remote(source, target, sems, 1, step, y),
        ]

    halfway = owners // 2

    def gather_relay(step):
        upper = o_all.at[step, pl.ds(0, halfway), :, lanes(x)]
        lower = o_all.at[step, pl.ds(halfway, halfway), :, lanes(y)]
        return [
            remote(upper, upper, sems, 2, step, y),
            remote(lower, lower, sems, 3, step, x),
        ]

    def relay(step):
        for copy, passed in zip(gather_own(step), gather_relay(step)):
            copy.wait_recv()
            passed.start()

    outgoing = (hid, dgate, dup)

    def to_core(kind):
        source = outgoing[kind] if kind < 3 else stage.at[0].reshape(size, width)
        return remote_pack(
            source, land_hbm.at[kind], core_send.at[kind], core_recv.at[kind], other_core
        )

    def landed(kind):
        return pltpu.make_async_copy(
            land_hbm.at[kind], tok.at[kind % 2].reshape(size, width), tok_sem.at[kind % 2]
        )

    def pile_copies(kind):
        summed = cot.at[kind % 2].reshape(size, width)
        return [
            pltpu.make_async_copy(
                summed.at[pl.ds(pl.multiple_of(chip_across(chip, bits) * share, share), share)],
                pile.at[i, kind - first],
                pile_sem.at[kind % 2, bits],
            )
            for pile, (places, first) in zip(piles, PILES)
            for i, bits in enumerate(places)
            if first <= kind < first + 2
        ]

    def sum_kind(kind):
        landed(kind).wait()
        if kind >= 2:
            for copy in pile_copies(kind - 2):
                copy.wait()
        theirs = tok[kind % 2].reshape(size, width)
        if kind < 3:
            mine = [
                acc[kind, pl.ds(pl.multiple_of((2 * z + core) * share, share), share), :]
                for z in range(chips)
            ]
            mine = jnp.concatenate(mine, axis=0)
        else:
            mine = h1_all[...].reshape(size, width)
        total = (mine + theirs.astype(F32)).astype(BF16)
        cot[kind % 2] = total.reshape(owners, block, width)
        for copy in pile_copies(kind):
            copy.start()

    def put_rows(step):
        return [
            remote(
                stage.at[lax.rem(step, 2), target], rows_hbm.at[i, step], sems, 13 + i, step, target
            )
            for i, target in enumerate((x, y, d))
        ]

    def put_do(step):
        return [
            remote(do_own.at[step, target], do_hbm.at[me, step], sems, 10 + i, step, target)
            for i, target in enumerate((x, y, d))
        ]

    def keep_do(step):
        return pltpu.make_async_copy(do_own.at[step, me], do_hbm.at[me, step], put_sem.at[step])

    for copy in fetch(0):
        copy.start()
    for copy in loads:
        copy.start()
    for step in range(early):
        for copy in early_copies(step):
            copy.start()
    group_barrier((x, y, d), (other_core,))

    def begin(step, _):
        for copy in gather_own(step):
            copy.start()
        own_copy(step).start()
        return 0

    lax.fori_loop(early, steps, begin, 0)
    acc[...] = jnp.zeros_like(acc)
    sums_ref[...] = jnp.zeros_like(sums_ref)
    for copy in loads:
        copy.wait()

    def step_body(step, _):
        slot = lax.rem(step, 2)
        now, before, older = [lax.rem(step + lag, 3) for lag in (0, 2, 1)]

        @pl.when(step + 1 < steps)
        def _():
            for copy in fetch(step + 1):
                copy.start()

        @pl.when((step + 1 < steps) & (step + 1 >= early))
        def _():
            relay(step + 1)

        @pl.when(step < early)
        def _():
            for copy in early_copies(step):
                copy.wait()

        @pl.when((step < steps) & (step >= early))
        def _():
            for copy in gather_relay(step):
                copy.wait_recv()
            own_copy(step).wait()

        @pl.when(step < steps)
        def _():
            for copy in fetch(step):
                copy.wait()
            def some_rows(turn, _):
                who, rows = pl.ds(turn * some, some), pl.ds(turn * some * block, some * block)
                position = lax.broadcasted_iota(jnp.int32, (some, block, 1), 1) + step * block
                position = position + (steps * block) * (
                    lax.broadcasted_iota(jnp.int32, (some, block, 1), 0) + turn * some
                )
                eb = jnp.where(position < live_end, cot[slot, who].astype(F32), 0.0).astype(BF16)
                cot[slot, who] = eb
                eb = eb.reshape(some * block, width)
                mixed = mm(o_all[step, who].reshape(some * block, width), wo[...])
                h1 = tok[slot, who].reshape(some * block, width).astype(F32) + mixed
                h1_all[who] = h1.reshape(some, block, width)
                hat, _ = norm_rows(h1)
                a2 = (hat * gain_ref[...] + bias_ref[...]).astype(BF16)
                a2_all[rows] = a2
                for piece in range(PIECES):
                    cols = pl.ds(piece * cut, cut)
                    gate = mm(a2, wg[:, cols])
                    up = mm(a2, wu[:, cols])
                    back = mm_nt(eb, wd[cols, :])
                    sig = 0.5 * jnp.tanh(0.5 * gate) + 0.5
                    act = gate * sig
                    hid[rows, cols] = (act * up).astype(BF16)
                    dgate[rows, cols] = (back * up * (sig + act * (1.0 - sig))).astype(BF16)
                    dup[rows, cols] = (back * act).astype(BF16)
                dc = mm_nt(dgate[rows, :], wg[...]) + mm_nt(dup[rows, :], wu[...])
                part[now, who] = dc.astype(BF16).reshape(some, 2, block // 2, width)
                return 0

            lax.fori_loop(0, owners // some, some_rows, 0)
            h1_ref[step] = h1_all[me]
            dh1_ref[step] = cot[slot, me].astype(F32)
            for copy in scatter_first(part, now, from_x, from_y, sems, 4, step):
                copy.start()

        @pl.when(step == steps)
        def _():
            for kind in range(3):
                for z in range(chips):
                    rows = pl.ds(pl.multiple_of((2 * z + 1 - core) * share, share), share)
                    outgoing[kind][z * share : (z + 1) * share, :] = acc[kind, rows, :].astype(BF16)
                to_core(kind).start()

        @pl.when((step >= 1) & (step <= steps))
        def _():
            scatter_middle(
                part, before, from_x, from_y, last_x, last_y, sems, 4, step - 1
            )

        @pl.when(step == steps)
        def _():
            for kind in range(2):
                to_core(kind).wait_recv()
                landed(kind).start()
            sum_kind(0)
            to_core(2).wait_recv()
            landed(2).start()
            sum_kind(1)
            sum_kind(2)

        def stage_copies(at, direct):
            slot = lax.rem(at, 2)
            places = [(me, down0_hbm.at[at])]
            if not direct:
                places += [(x, down1_hbm), (y, down2_hbm), (d, down3_hbm)]
                places[1:] = [(who, out.at[at - DIRECT]) for who, out in places[1:]]
            return [
                pltpu.make_async_copy(stage.at[slot, who], out, stage_sem.at[i, slot])
                for i, (who, out) in enumerate(places)
            ]

        @pl.when(step < steps)
        def _():
            @pl.when((step >= 2) & (step - 2 < DIRECT))
            def _():
                for copy in stage_copies(step - 2, True):
                    copy.wait()
                for copy in put_rows(step - 2):
                    copy.wait_send()

            @pl.when((step >= 2) & (step - 2 >= DIRECT))
            def _():
                for copy in stage_copies(step - 2, False):
                    copy.wait()

            stage[slot] = mm(hid[...], wd[...]).astype(BF16).reshape(owners, block, width)

            @pl.when(step < DIRECT)
            def _():
                for copy in stage_copies(step, True) + put_rows(step):
                    copy.start()

            @pl.when(step >= DIRECT)
            def _():
                for copy in stage_copies(step, False):
                    copy.start()

            a2_t = a2_all[...].T
            eb_t = cot[slot].reshape(size, width).T
            acc[0] += mm(a2_t, dgate[...])
            acc[1] += mm(a2_t, dup[...])
            acc[2] += mm(eb_t, hid[...])

        @pl.when(step == steps)
        def _():
            for copy in stage_copies(steps - 2, False) + stage_copies(steps - 1, False):
                copy.wait()

        @pl.when(step >= 2)
        def _():
            prev = step - 2
            dc = scatter_last(part, older, from_x, from_y, last_x, last_y, sems, 4, prev)
            hat, scale = norm_rows(h1_ref[prev])
            sums_ref[0:1] += jnp.sum(dc * hat, axis=0, keepdims=True)
            sums_ref[1:2] += jnp.sum(dc, axis=0, keepdims=True)
            inner = dc * gain_ref[...]
            inner = inner - jnp.mean(inner, axis=-1, keepdims=True) - hat * jnp.mean(
                inner * hat, axis=-1, keepdims=True
            )
            dh1 = dh1_ref[prev] + scale * inner
            dh1_ref[prev] = dh1
            db = dh1.astype(BF16)
            db_own[prev] = db
            back = mm_nt(db, wo[...]).astype(BF16)
            for group in range(owners):
                do_own[prev, group] = back[:, group * feats : (group + 1) * feats]
            for copy in put_do(prev):
                copy.start()
            keep_do(prev).start()

        return 0

    lax.fori_loop(0, steps + 2, step_body, 0)

    o_mine = jnp.concatenate([o_all[step, me] for step in range(steps)], axis=0)
    for turn, which in enumerate((1 - core, core)):
        columns = [
            db_own[:, :, pl.ds(pl.multiple_of((2 * z + which) * share, share), share)].reshape(
                steps * block, share
            )
            for z in range(chips)
        ]
        values = mm_tn(jnp.concatenate(columns, axis=1), o_mine)
        if turn == 0:
            stage[0] = values.astype(BF16).reshape(owners, block, width)
            to_core(3).start()
        else:
            h1_all[...] = values.reshape(owners, block, width)

    to_core(3).wait_recv()
    landed(3).start()
    sum_kind(3)
    for kind in range(4):
        to_core(kind).wait_send()
    for copy in pile_copies(2) + pile_copies(3):
        copy.wait()

    def sent(step, _):
        for copy in gather_own(step) + gather_relay(step):
            copy.wait_send()
        return 0

    lax.fori_loop(early, steps, sent, 0)

    for step in range(DIRECT):
        for copy in put_rows(step):
            copy.wait_recv()

    def finish(step, _):
        for copy in put_do(step):
            copy.wait()
        keep_do(step).wait()
        return 0

    lax.fori_loop(0, steps, finish, 0)


def ffn(lengths, early, o, tokens, cotangent, wo, wg, wu, wd, gain, bias, steps, packs):
    rows, width = tokens.shape
    feats = o.shape[-1]
    owners = width // feats
    block = rows // (owners * steps)
    hidden = wg.shape[1]
    size = owners * block
    chips = packs // 2
    by_owner = lambda a: a.reshape(owners, steps, block, a.shape[1])
    own = jax.ShapeDtypeStruct((steps, block, width), F32)
    half = (steps, 2, block // 2, width)
    dma = pltpu.SemaphoreType.DMA
    flops = 2 * rows * width * (width + 9 * hidden)
    h1, dh1, sums, do, _, *rest = pl.pallas_call(
        functools.partial(ffn_kernel, packs),
        in_specs=[SMEM] + [ANY] * 14 + [VMEM, VMEM],
        out_specs=[VMEM, VMEM, VMEM] + [ANY] * (7 + len(PILES)),
        out_shape=[
            own,
            own,
            jax.ShapeDtypeStruct((2, width), F32),
            jax.ShapeDtypeStruct((owners, steps, block, feats), BF16),
            jax.ShapeDtypeStruct((4, size, width), BF16),
        ]
        + [jax.ShapeDtypeStruct((steps, block, width), BF16)]
        + [jax.ShapeDtypeStruct((steps - DIRECT, block, width), BF16)] * 3
        + [jax.ShapeDtypeStruct((3, DIRECT, block, width), BF16)]
        + [jax.ShapeDtypeStruct((2, 2, width // packs, width), BF16)] * len(PILES),
        scratch_shapes=[
            pltpu.VMEM((width, width), BF16),
            pltpu.VMEM((width, hidden), BF16),
            pltpu.VMEM((width, hidden), BF16),
            pltpu.VMEM((hidden, width), BF16),
            pltpu.VMEM((steps, owners, block, width), BF16),
            pltpu.VMEM((2, owners, block, width), BF16),
            pltpu.VMEM((2, owners, block, width), BF16),
            pltpu.VMEM((owners, block, width), F32),
            pltpu.VMEM((size, hidden), BF16),
            pltpu.VMEM((size, hidden), BF16),
            pltpu.VMEM((size, hidden), BF16),
            pltpu.VMEM((3, owners, 2, block // 2, width), BF16),
            pltpu.VMEM(half, BF16),
            pltpu.VMEM(half, BF16),
            pltpu.VMEM((steps, block // 2, width), BF16),
            pltpu.VMEM((steps, block // 2, width), BF16),
            pltpu.VMEM((size, width), BF16),
            pltpu.VMEM((3, width, hidden), F32),
            pltpu.VMEM((2, owners, block, width), BF16),
            pltpu.VMEM((steps, owners, block, feats), BF16),
            pltpu.VMEM((steps, block, width), BF16),
            dma((7,)),
            dma((2,)),
            dma((2,)),
            dma((steps,)),
            dma((early[0].shape[1], 4)),
            dma((4, 2)),
            dma((steps,)),
            dma((2, chips)),
            dma((4,)),
            dma((4,)),
            dma((16, steps)),
            dma((16, steps)),
        ],
        compiler_params=pltpu.CompilerParams(
            collective_id=0, has_side_effects=True, vmem_limit_bytes=VMEM_CAP
        ),
        cost_estimate=pl.CostEstimate(flops=flops, bytes_accessed=rows * width * 14, transcendentals=0),
        name="ffn",
    )(lengths, *early, o, by_owner(tokens), by_owner(cotangent), *wo, wg, wu, wd, gain, bias)
    return h1, dh1, sums, do.reshape(rows, feats), rest[:5], rest[5:]


def last_kernel(
    packs,
    grad_hbm, grad_t_hbm, a1_hbm, tok_hbm, dh1_ref, h1_hbm, wq_ref, wk_ref, wv_ref, gain_ref, sums2_ref, *rest,
):
    chips = packs // 2
    downs, rest = rest[:5], rest[5:]
    piles, rest = rest[: len(PILES)], rest[len(PILES) :]
    (
        out_ref, tg_ref, gq_ref, gk_ref, gv_ref, gate_ref, up_ref, down_ref, proj_ref, norm_ref,
        grad, grad_t, a1, tok, part, from_x, from_y, last_x, last_y, h1, down, pile, pile_out, pile_in, sums1,
        full, core_out, core_in, chip_out, chip_in, proj_out, proj_in, norm_out, norm_in,
        grad_sem, tok_sem, load_sem, core_send, core_recv, chip_send, chip_recv, pile_send, pile_recv,
        small_send, small_recv, send_sem, recv_sem,
    ) = rest
    steps, owners, _, half, width = part.shape
    feats = wq_ref.shape[1]
    size = owners * 2 * half
    share = width // packs
    tall = 3 * feats
    sems = (send_sem, recv_sem)
    me, x, y, d = neighbours()
    core, chip, other_core, next_chips = pack_neighbours(packs)

    def fetch(step):
        return [
            pltpu.make_async_copy(grad_hbm.at[:, step], grad.at[step], grad_sem.at[step]),
            pltpu.make_async_copy(tok_hbm.at[:, step], tok.at[step], tok_sem.at[step]),
        ]

    later = [(grad_t_hbm, grad_t), (a1_hbm, a1)]
    later += [(piles[i], pile.at[i]) for i in range(len(PILES))]
    later += [(h1_hbm, h1), (downs[0], down.at[0])]
    later += [(downs[i], down.at[i, pl.ds(DIRECT, steps - DIRECT)]) for i in range(1, 4)]
    later += [(downs[4], down.at[pl.ds(1, 3), pl.ds(0, DIRECT)])]
    later = [pltpu.make_async_copy(a, b, load_sem.at[i]) for i, (a, b) in enumerate(later)]

    def to_core():
        return remote_pack(core_out, core_in, core_send, core_recv, other_core)

    def to_chips():
        return [
            remote_pack(
                chip_out.at[lax.rem(chip + i + 1, chips)], chip_in.at[i],
                chip_send.at[i], chip_recv.at[i], device,
            )
            for i, device in enumerate(next_chips)
        ]

    def pile_copies():
        index = lax.axis_index("dp")
        return [
            remote_pack(
                pile_out.at[i], pile_in.at[i], pile_send.at[i], pile_recv.at[i],
                index + 2 * (chip_across(chip, bits) - chip),
            )
            for i, bits in enumerate(reversed(PARTNERS))
        ]

    def small(kind, source, target):
        return [
            remote(source(device), target.at[i], (small_send, small_recv), kind, i, device)
            for i, device in enumerate((x, y, d))
        ]

    def proj_copies():
        return small(0, lambda device: proj_out.at[device], proj_in)

    def norm_copies():
        return small(1, lambda device: norm_out, norm_in)

    def begin(step, _):
        for copy in fetch(step):
            copy.start()
        return 0

    lax.fori_loop(0, steps, begin, 0)
    for copy in later:
        copy.start()
    group_barrier((x, y, d), [other_core] + next_chips)
    sums1[...] = jnp.zeros_like(sums1)

    def first(step, _):
        for copy in fetch(step):
            copy.wait()
        rows = grad[step].reshape(size, tall)
        da = mm_nt(rows[:, :feats], wq_ref[...])
        da = da + mm_nt(rows[:, feats : 2 * feats], wk_ref[...])
        da = da + mm_nt(rows[:, 2 * feats :], wv_ref[...])
        part[step] = da.astype(BF16).reshape(owners, 2, half, width)
        for copy in scatter_first(part, step, from_x, from_y, sems, 0, step):
            copy.start()

        @pl.when(step == 0)
        def _():
            for copy in later[2 : 2 + len(PILES)]:
                copy.wait()
            for i in range(2):
                total = pile[2 * i, 1].astype(F32) + pile[2 * i + 1, 1].astype(F32)
                pile_out[i] = total.astype(BF16)
            for copy in pile_copies():
                copy.start()

        hat, _ = norm_rows(tok[step].reshape(size, width).astype(F32))
        sums1[0:1] += jnp.sum(da * hat, axis=0, keepdims=True)
        sums1[1:2] += jnp.sum(da, axis=0, keepdims=True)
        return 0

    lax.fori_loop(0, steps, first, 0)
    later[0].wait()
    later[1].wait()
    for kind in range(3):
        rows = pl.ds(kind * feats, feats)
        full[rows, :] = mm(grad_t[rows, :], a1[...])
    full[pl.ds(tall, 16), :] = jnp.concatenate(
        [sums1[...], sums2_ref[...], jnp.zeros((12, width), F32)], axis=0
    )
    for z in range(chips):
        columns = pl.ds(pl.multiple_of((2 * z + 1 - core) * share, share), share)
        core_out[z] = full[:, columns].astype(BF16)
    to_core().start()

    to_core().wait_recv()
    for z in range(chips):
        columns = pl.ds(pl.multiple_of((2 * z + core) * share, share), share)
        chip_out[z] = (full[:, columns] + core_in[z].astype(F32)).astype(BF16)
    for copy in to_chips():
        copy.start()
    for copy in later[2 + len(PILES) :]:
        copy.wait()

    def sum_piles():
        for copy in pile_copies():
            copy.wait_recv()
        for kind in range(4):
            half, at = kind // 2, kind % 2
            total = pile[2 * half, 0, at].astype(F32) + pile[2 * half + 1, 0, at].astype(F32)
            total = total + pile_in[half, at].astype(F32)
            if kind < 2:
                (gate_ref, up_ref)[kind][...] = total
            elif kind == 2:
                down_ref[...] = total.T
            else:
                for group in range(owners):
                    proj_out[group] = total[:, group * feats : (group + 1) * feats].astype(BF16)
                for copy in proj_copies():
                    copy.start()

    def finish(step):
        da = scatter_last(part, step, from_x, from_y, last_x, last_y, sems, 0, step)
        hat, scale = norm_rows(tok[step, me].astype(F32))
        inner = da * gain_ref[...]
        inner = inner - jnp.mean(inner, axis=-1, keepdims=True) - hat * jnp.mean(
            inner * hat, axis=-1, keepdims=True
        )
        tg_ref[step] = (dh1_ref[step] + scale * inner).astype(BF16)

    def second(step, _):
        scatter_middle(part, step, from_x, from_y, last_x, last_y, sems, 0, step)
        total = h1[step]
        for i in range(4):
            total = total + down[i, step].astype(F32)
        out_ref[step] = total.astype(BF16)
        return 0

    def third(step, _):
        finish(step)
        return 0

    lax.fori_loop(0, steps, second, 0)
    sum_piles()
    lax.fori_loop(0, steps - 2, third, 0)
    total = chip_out[chip].astype(F32)
    for i, copy in enumerate(to_chips()):
        copy.wait_recv()
        total = total + chip_in[i].astype(F32)
    norm_out[...] = total[tall : tall + 8]
    for copy in norm_copies():
        copy.start()
    finish(steps - 2)
    for kind, ref in enumerate((gq_ref, gk_ref, gv_ref)):
        ref[...] = total[kind * feats : (kind + 1) * feats].T
    total = proj_out[me].astype(F32)
    for i, copy in enumerate(proj_copies()):
        copy.wait_recv()
        total = total + proj_in[i].astype(F32)
    proj_ref[...] = total.T
    finish(steps - 1)
    total = norm_out[...]
    for i, copy in enumerate(norm_copies()):
        copy.wait_recv()
        total = total + norm_in[i]
    norm_ref[...] = total
    for copy in [to_core()] + to_chips() + pile_copies() + proj_copies() + norm_copies():
        copy.wait_send()


def last(grads, grads_t, a1, tokens, dh1, h1, wq, wk, wv, gain, sums2, downs, piles, packs):
    rows, width = tokens.shape
    steps, block, _ = dh1.shape
    owners = rows // (steps * block)
    feats = wq.shape[1]
    hidden = piles[0].shape[-1]
    chips = packs // 2
    share = width // packs
    tall = 3 * feats + 16
    by_owner = lambda a: a.reshape(owners, steps, block, a.shape[1])
    half = (steps, 2, block // 2, width)
    dma = pltpu.SemaphoreType.DMA
    own = jax.ShapeDtypeStruct((steps, block, width), BF16)
    f32 = lambda *shape: jax.ShapeDtypeStruct(shape, F32)
    return pl.pallas_call(
        functools.partial(last_kernel, packs),
        in_specs=[ANY] * 4 + [VMEM, ANY] + [VMEM] * 5 + [ANY] * (5 + len(piles)),
        out_specs=[VMEM] * 10,
        out_shape=[own, own]
        + [f32(share, feats)] * 3
        + [f32(share, hidden), f32(share, hidden), f32(hidden, share), f32(feats, share), f32(8, share)],
        scratch_shapes=[
            pltpu.VMEM((steps, owners, block, 3 * feats), BF16),
            pltpu.VMEM((3 * feats, rows), BF16),
            pltpu.VMEM((rows, width), BF16),
            pltpu.VMEM((steps, owners, block, width), BF16),
            pltpu.VMEM((steps, owners, 2, block // 2, width), BF16),
            pltpu.VMEM(half, BF16),
            pltpu.VMEM(half, BF16),
            pltpu.VMEM((steps, block // 2, width), BF16),
            pltpu.VMEM((steps, block // 2, width), BF16),
            pltpu.VMEM((steps, block, width), F32),
            pltpu.VMEM((4, steps, block, width), BF16),
            pltpu.VMEM((len(PILES), 2, 2, share, hidden), BF16),
            pltpu.VMEM((2, 2, share, hidden), BF16),
            pltpu.VMEM((2, 2, share, hidden), BF16),
            pltpu.VMEM((2, width), F32),
            pltpu.VMEM((tall, width), F32),
            pltpu.VMEM((chips, tall, share), BF16),
            pltpu.VMEM((chips, tall, share), BF16),
            pltpu.VMEM((chips, tall, share), BF16),
            pltpu.VMEM((chips - 1, tall, share), BF16),
            pltpu.VMEM((owners, share, feats), BF16),
            pltpu.VMEM((owners - 1, share, feats), BF16),
            pltpu.VMEM((8, share), F32),
            pltpu.VMEM((owners - 1, 8, share), F32),
            dma((steps,)),
            dma((steps,)),
            dma((8 + len(piles),)),
            dma,
            dma,
            dma((chips - 1,)),
            dma((chips - 1,)),
            dma((2,)),
            dma((2,)),
            dma((2, owners - 1)),
            dma((2, owners - 1)),
            dma((6, steps)),
            dma((6, steps)),
        ],
        compiler_params=pltpu.CompilerParams(
            collective_id=1, has_side_effects=True, vmem_limit_bytes=VMEM_CAP
        ),
        cost_estimate=pl.CostEstimate(
            flops=12 * rows * width * feats, bytes_accessed=rows * width * 20, transcendentals=0
        ),
        name="last",
    )(
        by_owner(grads), grads_t, a1, by_owner(tokens), dh1, h1, wq, wk, wv, gain, sums2, *downs, *piles
    )


def hand_out_kernel(count, *refs):
    sources, outs, held = refs[:count], refs[count : 2 * count], refs[2 * count : 3 * count]
    in_sem, out_sem = refs[3 * count :]
    loads = [pltpu.make_async_copy(sources[i], held[i], in_sem.at[i]) for i in range(count)]
    stores = [pltpu.make_async_copy(held[i], outs[i], out_sem.at[i]) for i in range(count)]
    for copy in loads:
        copy.start()
    for load, store in zip(loads, stores):
        load.wait()
        store.start()
    for store in stores:
        store.wait()


def hand_out(arrays):
    count = len(arrays)
    return pl.pallas_call(
        functools.partial(hand_out_kernel, count),
        in_specs=[ANY] * count,
        out_specs=[ANY] * count,
        out_shape=[jax.ShapeDtypeStruct(a.shape, a.dtype) for a in arrays],
        scratch_shapes=[pltpu.VMEM(a.shape, a.dtype) for a in arrays]
        + [pltpu.SemaphoreType.DMA((count,))] * 2,
        compiler_params=pltpu.CompilerParams(vmem_limit_bytes=VMEM_CAP),
        name="hand_out",
    )(*arrays)


def local_square(
    tokens, lengths, cotangent, norm1_gain, norm1_bias, w_query, w_key, w_value, w_output,
    norm2_gain, norm2_bias, w_gate, w_up, w_down,
):
    rows, width = tokens.shape
    groups = lax.axis_size("mp")
    packs = lax.axis_size("dp")
    gain1, bias1 = norm1_gain[None, :], norm1_bias[None, :]
    exchange = lambda a, shift: lax.ppermute(a, "mp", [(i, i ^ shift) for i in range(groups)])
    w_outputs = [w_output] + [exchange(w_output, shift) for shift in range(1, groups)]
    a1, k, v, qt, kt, vt, cosine, sine = project(
        lengths, tokens, gain1, bias1, w_query, w_key, w_value
    )
    early, mixed_t, lse = attend(lengths, qt, k, vt, 0, EARLY, STEPS)
    early = [early] + [exchange(early, shift) for shift in range(1, groups)]
    mixed, mixed_t, lse = attend(lengths, qt, k, vt, EARLY, STEPS, STEPS, (mixed_t, lse))
    h1, dh1, sums2, mixed_grad, downs, piles = ffn(
        lengths, early, mixed, tokens, cotangent, w_outputs, w_gate, w_up, w_down,
        norm2_gain[None, :], norm2_bias[None, :], STEPS, packs,
    )
    downs[1:4] = [exchange(downs[shift], shift) for shift in range(1, groups)]
    for i, bits in enumerate(PARTNERS):
        perm = [(j, j ^ (2 * bits)) for j in range(packs)]
        piles[2 * i + 1] = lax.ppermute(piles[2 * i + 1], "dp", perm)
    grads, grads_t = attend_back(
        lengths, qt, k, kt, v, mixed_grad, mixed_t, lse, cosine, sine
    )
    *results, norms = last(
        grads, grads_t, a1, tokens, dh1, h1, w_query, w_key, w_value, gain1, sums2, downs, piles, packs
    )
    output, tokens_grad, grad_q, grad_k, grad_v, gate, up, down, proj = hand_out(results)
    own_rows = (rows // groups, width)
    return (
        output.reshape(own_rows),
        tokens_grad.reshape(own_rows),
        grad_q,
        grad_k,
        grad_v,
        proj,
        gate,
        up,
        down,
        norms[0],
        norms[1],
        norms[2],
        norms[3],
    )


def layer_stats(row_values, gain_vec, bias_vec):
    normed, row_scale = norm_rows(row_values)
    return (normed * gain_vec + bias_vec, normed, row_scale)


def layer_back(gradient, normed, row_scale, gain_vec):
    inner_grad = gradient * gain_vec
    centred_grad = inner_grad - jnp.mean(inner_grad, axis=-1, keepdims=True)
    return row_scale * (
        centred_grad - normed * jnp.mean(inner_grad * normed, axis=-1, keepdims=True)
    )


def scatter_rows(partial, axis, dim=0):
    return lax.psum_scatter(
        partial.astype(BF16), axis, scatter_dimension=dim, tiled=True
    ).astype(F32)


def local(
    tokens, lengths, cotangent, norm1_gain, norm1_bias, w_query, w_key, w_value, w_output,
    norm2_gain, norm2_bias, w_gate, w_up, w_down,
):
    row_count, width = tokens.shape
    feats = w_query.shape[1]
    gain1, bias1 = norm1_gain[None, :], norm1_bias[None, :]
    a1, k, v, qt, kt, vt, cosine, sine = project(
        lengths, tokens, gain1, bias1, w_query, w_key, w_value
    )
    mixed, mixed_t, lse = attend(lengths, qt, k, vt, 0, 1, 1)
    mixed = mixed.reshape(row_count, feats)

    share_rows = row_count // lax.axis_size("mp")
    own_start = lax.axis_index("mp") * share_rows
    own = lambda a: lax.dynamic_slice_in_dim(a, own_start, share_rows, 0)
    live_end = row_count - lengths[0, lengths.shape[1] - 1]
    live = jnp.arange(row_count, dtype=jnp.int32)[:, None] < live_end
    out_grad = jnp.where(live, cotangent, jnp.zeros_like(cotangent))

    attn_rows = scatter_rows(mm(mixed, w_output), "mp")
    residual = own(tokens).astype(F32) + attn_rows
    normed_second, hat_second, scale_second = layer_stats(residual, norm2_gain, norm2_bias)
    inputs_second = lax.all_gather(normed_second.astype(BF16), "mp", axis=0, tiled=True)
    gate_pre = mm(inputs_second, w_gate)
    up_proj = mm(inputs_second, w_up)
    gate_sig = jax.nn.sigmoid(gate_pre)
    gate_act = gate_pre * gate_sig
    hidden = (gate_act * up_proj).astype(BF16)
    output_own = residual + scatter_rows(mm(hidden, w_down), "mp")
    down_w_grad = mm_tn(hidden, out_grad)
    hidden_grad = mm_nt(out_grad, w_down)
    gate_in_grad = (hidden_grad * up_proj * gate_sig * (1.0 + gate_pre * (1.0 - gate_sig))).astype(BF16)
    up_in_grad = (hidden_grad * gate_act).astype(BF16)
    gate_w_grad = mm_tn(inputs_second, gate_in_grad)
    up_w_grad = mm_tn(inputs_second, up_in_grad)
    ffn_sums = (
        scatter_rows(gate_w_grad, "dp"),
        scatter_rows(up_w_grad, "dp"),
        scatter_rows(down_w_grad, "dp", 1),
    )
    second_grad = scatter_rows(mm_nt(gate_in_grad, w_gate) + mm_nt(up_in_grad, w_up), "mp")
    residual_grad = own(out_grad).astype(F32) + layer_back(
        second_grad, hat_second, scale_second, norm2_gain
    )
    attn_grad = lax.all_gather(residual_grad.astype(BF16), "mp", axis=0, tiled=True)
    gain_second_grad = jnp.sum(second_grad * hat_second, axis=0)
    bias_second_grad = jnp.sum(second_grad, axis=0)
    output_w_grad = mm_tn(mixed, attn_grad)
    mixed_grad = mm_nt(attn_grad, w_output).astype(BF16)

    grads, grads_t = attend_back(
        lengths, qt, k, kt, v, mixed_grad, mixed_t, lse, cosine, sine
    )
    w_qkv = jnp.concatenate([w_query, w_key, w_value], axis=1)
    qkv_w_grad = mm(grads_t, a1)
    first_grad = scatter_rows(mm_nt(grads, w_qkv), "mp")
    hat_own, scale_own = norm_rows(own(tokens).astype(F32))
    tokens_grad = (residual_grad + layer_back(first_grad, hat_own, scale_own, norm1_gain)).astype(BF16)
    gain_parts = jnp.stack(
        [
            jnp.sum(first_grad * hat_own, axis=0),
            jnp.sum(first_grad, axis=0),
            gain_second_grad,
            bias_second_grad,
        ]
    )
    gain_parts = scatter_rows(lax.psum(gain_parts, "mp"), "dp", 1)
    attn_sums = scatter_rows(jnp.concatenate([qkv_w_grad, output_w_grad], axis=0), "dp", 1)
    return (
        output_own.astype(BF16),
        tokens_grad,
        attn_sums[:feats].T,
        attn_sums[feats : 2 * feats].T,
        attn_sums[2 * feats : 3 * feats].T,
        attn_sums[3 * feats :],
        ffn_sums[0],
        ffn_sums[1],
        ffn_sums[2],
        gain_parts[0],
        gain_parts[1],
        gain_parts[2],
        gain_parts[3],
    )


def solution(mesh):
    square = mesh.shape["mp"] == 4 and mesh.shape["dp"] == 2 * CHIPS
    rows, weight_in, weight_out = P("dp", None), P(None, "mp"), P("mp", None)
    row_out = P(("dp", "mp"), None)
    return jax.shard_map(
        local_square if square else local,
        mesh=mesh,
        in_specs=(rows, rows, rows, P(), P(), weight_in, weight_in, weight_in, weight_out)
        + (P(), P(), weight_in, weight_in, weight_out),
        out_specs=(row_out, row_out)
        + (P("dp", "mp"),) * 3
        + (P("mp", "dp"), P("dp", "mp"), P("dp", "mp"), P("mp", "dp"))
        + (P("dp"),) * 4,
        check_vma=False,
    )
```

```python
import functools
import math

import jax
import jax.numpy as jnp
import numpy as np
from jax import lax
from jax.experimental import pallas as pl
from jax.experimental.pallas import tpu as pltpu
from jax.sharding import PartitionSpec as P

HD = 64
HALF = HD // 2
PAIR = 2 * HD
QB = 128
KB = 256
EPS = 1e-05
BASE = 10000.0
NEG = -1e30
MOST = 1024
SCALE = HD**-0.5
VMEM = pl.BlockSpec(memory_space=pltpu.VMEM)
SMEM = pl.BlockSpec(memory_space=pltpu.SMEM)
ANY = pl.BlockSpec(memory_space=pl.ANY)
MESH = pl.DeviceIdType.MESH
STEPS = 5
EARLY = 2
TILE = 256
VMEM_CAP = 62 << 20
F32 = jnp.float32
BF16 = jnp.bfloat16


def mm(a, b):
    return jnp.dot(a, b, preferred_element_type=F32)


def mm_nt(a, b):
    return lax.dot_general(a, b, (((1,), (1,)), ((), ())), preferred_element_type=F32)


def mm_tn(a, b):
    return lax.dot_general(a, b, (((0,), (0,)), ((), ())), preferred_element_type=F32)


def window_bounds(len_ref, position):
    entries = len_ref.shape[1]
    start = jnp.zeros_like(position)
    end = jnp.zeros_like(position)
    edge = jnp.int32(0)
    for entry in range(entries):
        size = len_ref[0, entry]
        inside = position >= edge
        start = jnp.where(inside, edge, start)
        edge = edge + size
        end = jnp.where(inside, edge, end)
    return start, end


def norm_rows(rows):
    mean = jnp.mean(rows, axis=-1, keepdims=True)
    centred = rows - mean
    scale = lax.rsqrt(jnp.mean(centred * centred, axis=-1, keepdims=True) + EPS)
    return centred * scale, scale


def rotate_t(field, cosine, sine, direction):
    parts = []
    for head in range(field.shape[0] // HD):
        first = field[head * HD : head * HD + HALF]
        second = field[head * HD + HALF : (head + 1) * HD]
        parts.append(first * cosine - direction * (second * sine))
        parts.append(second * cosine + direction * (first * sine))
    return jnp.concatenate(parts, axis=0)


def qkv_kernel(
    len_ref, tok_ref, gain_ref, bias_ref, freq_ref, wq_ref, wk_ref, wv_ref,
    a1_ref, k_ref, v_ref, qt_ref, kt_ref, vt_ref, cos_ref, sin_ref,
):
    rows = tok_ref.shape[0]
    position = lax.broadcasted_iota(jnp.int32, (1, rows), 1) + pl.program_id(0) * rows
    start, _ = window_bounds(len_ref, position)
    offset = (position - start).astype(F32)
    theta = freq_ref[...] * offset
    cosine, sine = jnp.cos(theta), jnp.sin(theta)
    cos_ref[...] = cosine
    sin_ref[...] = sine
    hat, _ = norm_rows(tok_ref[...].astype(F32))
    a1 = (hat * gain_ref[...] + bias_ref[...]).astype(BF16)
    a1_ref[...] = a1
    for w_ref, out_ref, out_t_ref, scale in (
        (wq_ref, None, qt_ref, SCALE),
        (wk_ref, k_ref, kt_ref, None),
    ):
        field = rotate_t(mm(a1, w_ref[...]).T, cosine, sine, 1.0).astype(BF16)
        if scale is not None:
            field = field * jnp.asarray(scale, BF16)
        out_t_ref[...] = field
        if out_ref is not None:
            out_ref[...] = field.T
    values = mm(a1, wv_ref[...]).astype(BF16)
    v_ref[...] = values
    vt_ref[...] = values.T


def project(lengths, tokens, gain, bias, wq, wk, wv):
    rows, width = tokens.shape
    feats = wq.shape[1]
    block = min(512, rows)
    freq = np.float32(BASE) ** (np.float32(-2.0 / HD) * np.arange(HALF, dtype=np.float32))
    freq = jnp.asarray(freq[:, None], F32)
    whole = lambda a: pl.BlockSpec(a.shape, lambda i: (0, 0))
    by_row = lambda cols: pl.BlockSpec((block, cols), lambda i: (i, 0))
    by_col = lambda size: pl.BlockSpec((size, block), lambda i: (0, i))
    nat = jax.ShapeDtypeStruct((rows, feats), BF16)
    trans = jax.ShapeDtypeStruct((feats, rows), BF16)
    table = jax.ShapeDtypeStruct((HALF, rows), F32)
    return pl.pallas_call(
        qkv_kernel,
        grid=(rows // block,),
        in_specs=[SMEM, by_row(width)] + [whole(a) for a in (gain, bias, freq, wq, wk, wv)],
        out_specs=[by_row(width)] + [by_row(feats)] * 2 + [by_col(feats)] * 3 + [by_col(HALF)] * 2,
        out_shape=[jax.ShapeDtypeStruct((rows, width), BF16)] + [nat] * 2 + [trans] * 3 + [table] * 2,
        compiler_params=pltpu.CompilerParams(vmem_limit_bytes=VMEM_CAP),
        cost_estimate=pl.CostEstimate(
            flops=6 * rows * width * feats, bytes_accessed=rows * width * 8, transcendentals=0
        ),
        name="qkv",
    )(lengths, tokens, gain, bias, freq, wq, wk, wv)


def block_diagonal_t(pair):
    head = lax.broadcasted_iota(jnp.int32, pair.shape, 0) < HD
    zero = jnp.zeros_like(pair)
    return jnp.concatenate([jnp.where(head, pair, zero), jnp.where(head, zero, pair)], axis=1)


def diagonal_blocks(product):
    return jnp.concatenate([product[:HD, :QB], product[HD:, QB:]], axis=1)


def key_range(len_ref, first):
    low, _ = window_bounds(len_ref, first)
    _, high = window_bounds(len_ref, first + (QB - 1))
    base = low // QB * QB
    return base, (high - base + (KB - 1)) // KB


def key_rows(at, rows):
    return pl.ds(pl.multiple_of(jnp.clip(at, 0, rows - KB), QB), KB)


def inside_window(start, end, at, rows):
    shift = jnp.minimum(at, rows - KB)
    key = lax.broadcasted_iota(jnp.int32, (KB, QB), 0)
    inside = (key >= jnp.maximum(start, at) - shift) & (key < end - shift)
    return jnp.concatenate([inside, inside], axis=1)


def fill_schedule(len_ref, sched, blocks, index_of, rows):
    def nothing(n):
        sched[0, n] = 0
        sched[1, n] = rows

    def one_query(turn, n):
        base, count = key_range(len_ref, index_of(turn) * QB)

        def one_key(kb, _):
            sched[0, n + kb] = turn
            sched[1, n + kb] = base + kb * KB
            return 0

        lax.fori_loop(0, count, one_key, 0)
        return n + count

    nothing(0)
    n = lax.fori_loop(0, blocks, one_query, jnp.int32(1))
    for extra in range(3):
        nothing(n + extra)
    return n - 1


def store_window(len_ref, window, turn, first):
    position = lax.broadcasted_iota(jnp.int32, (1, QB), 1) + first
    window[turn, 0:1], window[turn, 1:2] = window_bounds(len_ref, position)


def run_pipeline(count, scores, soften, mix):
    def two_pairs(turn, _):
        n = 1 + 2 * turn
        mix(n - 1, 1)
        scores(n + 1, 1)
        soften(n, 0)
        mix(n, 0)
        scores(n + 2, 0)
        soften(n + 1, 1)
        return 0

    turns = (count + 1) // 2
    scores(1, 0)
    lax.fori_loop(0, turns, two_pairs, 0)
    mix(2 * turns, 1)


def attend_kernel(begin, steps, len_ref, qt_ref, k_ref, vt_ref, *rest):
    if begin > 0:
        ot_before, lse_before, *rest = rest
    o_ref, *rest = rest
    first_ref = None
    if begin == 0 and steps > 1:
        first_ref, *rest = rest
    ot_ref, lse_ref, sched, window, diag, stat, acc, keep_buf, score_buf, prob_buf = rest
    if begin > 0:
        ot_ref[...] = ot_before[...]
        lse_ref[...] = lse_before[...]
    owners, taken = o_ref.shape[:2]
    feats, rows = qt_ref.shape
    pairs = range(feats // PAIR)
    feat = [pl.ds(p * PAIR, PAIR) for p in pairs]

    def index_of(turn):
        return turn // taken * steps + begin + lax.rem(turn, taken)

    def prepare(turn, _):
        first = index_of(turn) * QB
        cols = pl.ds(pl.multiple_of(first, QB), QB)
        store_window(len_ref, window, turn, first)
        for p in pairs:
            diag[turn, p] = block_diagonal_t(qt_ref[feat[p], cols])
            stat[turn, p : p + 1] = jnp.full((1, 2 * QB), NEG, F32)
            stat[turn, 4 + p : 5 + p] = jnp.zeros((1, 2 * QB), F32)
            acc[turn, p] = jnp.zeros((HD, 2 * QB), F32)
        return 0

    lax.fori_loop(0, owners * taken, prepare, 0)
    count = fill_schedule(len_ref, sched, owners * taken, index_of, rows)

    def scores(n, buf):
        turn, keys = sched[0, n], key_rows(sched[1, n], rows)
        for p in pairs:
            score_buf[buf, p] = mm(k_ref[keys, feat[p]], diag[turn, p])

    def soften(n, buf):
        turn = sched[0, n]
        inside = inside_window(window[turn, 0:1], window[turn, 1:2], sched[1, n], rows)
        for p in pairs:
            top, total = stat[turn, p : p + 1], stat[turn, 4 + p : 5 + p]
            values = jnp.where(inside, score_buf[buf, p], NEG)
            new_top = jnp.maximum(top, jnp.max(values, axis=0, keepdims=True))
            prob = jnp.exp(values - new_top)
            keep = jnp.exp(top - new_top)
            stat[turn, p : p + 1] = new_top
            stat[turn, 4 + p : 5 + p] = keep * total + jnp.sum(prob, axis=0, keepdims=True)
            keep_buf[buf, p : p + 1] = keep
            prob_buf[buf, p] = prob.astype(BF16)

    def mix(n, buf):
        turn, keys = sched[0, n], key_rows(sched[1, n], rows)
        for p in pairs:
            mixed = diagonal_blocks(mm(vt_ref[feat[p], keys], prob_buf[buf, p]))
            acc[turn, p] = acc[turn, p] * keep_buf[buf, p : p + 1] + mixed

    prob_buf[1] = jnp.zeros_like(prob_buf[1])
    keep_buf[1] = jnp.ones_like(keep_buf[1])
    run_pipeline(count, scores, soften, mix)

    def finish(turn, _):
        index = index_of(turn)
        cols = pl.ds(pl.multiple_of(index * QB, QB), QB)
        for p in pairs:
            top, total = stat[turn, p : p + 1], stat[turn, 4 + p : 5 + p]
            mixed = acc[turn, p] / total
            mixed = jnp.concatenate([mixed[:, :QB], mixed[:, QB:]], axis=0).astype(BF16)
            lse_ref[index, p : p + 1] = top + jnp.log(total)
            ot_ref[feat[p], cols] = mixed
            mixed = mixed.T
            o_ref[turn // taken, lax.rem(turn, taken), :, feat[p]] = mixed
            if first_ref is not None:

                @pl.when(lax.rem(turn, taken) == 0)
                def _():
                    first_ref[turn // taken, 0, :, feat[p]] = mixed

        return 0

    lax.fori_loop(0, owners * taken, finish, 0)


def schedule_size(blocks):
    return blocks * ((2 * MOST + 2 * QB) // KB + 1) + 4


def attend(lengths, qt, k, vt, begin, end, steps, before=()):
    feats, rows = qt.shape
    pairs = feats // PAIR
    owners = rows // (steps * QB)
    share = (end - begin) / steps
    blocks = owners * (end - begin)
    first = []
    if begin == 0 and steps > 1:
        first = [jax.ShapeDtypeStruct((owners, 1, QB, feats), BF16)]
    return pl.pallas_call(
        functools.partial(attend_kernel, begin, steps),
        in_specs=[SMEM] + [VMEM] * (3 + len(before)),
        out_specs=[VMEM] * (3 + len(first)),
        out_shape=[jax.ShapeDtypeStruct((owners, end - begin, QB, feats), BF16)]
        + first
        + [
            jax.ShapeDtypeStruct((feats, rows), BF16),
            jax.ShapeDtypeStruct((rows // QB, pairs, 2 * QB), F32),
        ],
        scratch_shapes=[
            pltpu.SMEM((2, schedule_size(blocks)), jnp.int32),
            pltpu.VMEM((blocks, 8, QB), jnp.int32),
            pltpu.VMEM((blocks, pairs, PAIR, 2 * QB), BF16),
            pltpu.VMEM((blocks, 8, 2 * QB), F32),
            pltpu.VMEM((blocks, pairs, HD, 2 * QB), F32),
            pltpu.VMEM((2, 8, 2 * QB), F32),
            pltpu.VMEM((2, pairs, KB, 2 * QB), F32),
            pltpu.VMEM((2, pairs, KB, 2 * QB), BF16),
        ],
        compiler_params=pltpu.CompilerParams(vmem_limit_bytes=VMEM_CAP),
        cost_estimate=pl.CostEstimate(
            flops=int(8 * share * rows * rows * feats),
            bytes_accessed=rows * feats * 10,
            transcendentals=int(share * rows * rows),
        ),
        name="attend",
    )(lengths, qt, k, vt, *before)


def attend_back_kernel(
    len_ref, qt_ref, k_ref, kt_ref, v_ref, do_ref, ot_ref, lse_ref, cos_ref, sin_ref,
    grad_ref, grad_t_ref, sched, window, q_diag, do_diag, stat, dq_acc, dk_acc, dv_acc,
    score_buf, prob_grad_buf, prob_buf, score_grad_buf,
):
    feats, rows = qt_ref.shape
    pairs = range(feats // PAIR)
    feat = [pl.ds(p * PAIR, PAIR) for p in pairs]
    dk_acc[...] = jnp.zeros_like(dk_acc)
    dv_acc[...] = jnp.zeros_like(dv_acc)
    dq_acc[...] = jnp.zeros_like(dq_acc)

    def prepare(turn, _):
        cols = pl.ds(pl.multiple_of(turn * QB, QB), QB)
        store_window(len_ref, window, turn, turn * QB)
        for p in pairs:
            do_t = do_ref[cols, feat[p]].T
            delta = do_t.astype(F32) * ot_ref[feat[p], cols].astype(F32)
            delta = [jnp.sum(part, axis=0, keepdims=True) for part in (delta[:HD], delta[HD:])]
            q_diag[turn, p] = block_diagonal_t(qt_ref[feat[p], cols])
            do_diag[turn, p] = block_diagonal_t(do_t)
            stat[turn, p : p + 1] = lse_ref[turn, p : p + 1]
            stat[turn, 4 + p : 5 + p] = jnp.concatenate(delta, axis=1)
        return 0

    lax.fori_loop(0, rows // QB, prepare, 0)
    count = fill_schedule(len_ref, sched, rows // QB, lambda turn: turn, rows)

    def scores(n, buf):
        turn, keys = sched[0, n], key_rows(sched[1, n], rows)
        for p in pairs:
            score_buf[buf, p] = mm(k_ref[keys, feat[p]], q_diag[turn, p])
            prob_grad_buf[buf, p] = mm(v_ref[keys, feat[p]], do_diag[turn, p])

    def soften(n, buf):
        turn = sched[0, n]
        inside = inside_window(window[turn, 0:1], window[turn, 1:2], sched[1, n], rows)
        for p in pairs:
            lse, delta = stat[turn, p : p + 1], stat[turn, 4 + p : 5 + p]
            prob = jnp.where(inside, jnp.exp(score_buf[buf, p] - lse), 0.0)
            prob_buf[buf, p] = prob.astype(BF16)
            score_grad_buf[buf, p] = (prob * (prob_grad_buf[buf, p] - delta)).astype(BF16)

    def mix(n, buf):
        turn, keys = sched[0, n], key_rows(sched[1, n], rows)
        for p in pairs:
            dv_acc[feat[p], keys] += mm_nt(do_diag[turn, p], prob_buf[buf, p])
            dk_acc[feat[p], keys] += mm_nt(q_diag[turn, p], score_grad_buf[buf, p])
            dq_acc[turn, p] += diagonal_blocks(mm(kt_ref[feat[p], keys], score_grad_buf[buf, p]))

    prob_buf[1] = jnp.zeros_like(prob_buf[1])
    score_grad_buf[1] = jnp.zeros_like(score_grad_buf[1])
    run_pipeline(count, scores, soften, mix)

    def finish(turn, _):
        cols = pl.ds(pl.multiple_of(turn * QB, QB), QB)
        cosine, sine = cos_ref[:, cols], sin_ref[:, cols]
        for p in pairs:
            dq = jnp.concatenate([dq_acc[turn, p, :, :QB], dq_acc[turn, p, :, QB:]], axis=0) * SCALE
            fields = (
                rotate_t(dq, cosine, sine, -1.0),
                rotate_t(dk_acc[feat[p], cols], cosine, sine, -1.0),
                dv_acc[feat[p], cols],
            )
            for kind, field in enumerate(fields):
                place = pl.ds(kind * feats + p * PAIR, PAIR)
                field = field.astype(BF16)
                grad_t_ref[place, cols] = field
                grad_ref[cols, place] = field.T
        return 0

    lax.fori_loop(0, rows // QB, finish, 0)


def attend_back(lengths, qt, k, kt, v, do, ot, lse, cosine, sine):
    feats, rows = qt.shape
    blocks = rows // QB
    return pl.pallas_call(
        attend_back_kernel,
        in_specs=[SMEM] + [VMEM] * 9,
        out_specs=[VMEM, VMEM],
        out_shape=[
            jax.ShapeDtypeStruct((rows, 3 * feats), BF16),
            jax.ShapeDtypeStruct((3 * feats, rows), BF16),
        ],
        scratch_shapes=[
            pltpu.SMEM((2, schedule_size(blocks)), jnp.int32),
            pltpu.VMEM((blocks, 8, QB), jnp.int32),
            pltpu.VMEM((blocks, feats // PAIR, PAIR, 2 * QB), BF16),
            pltpu.VMEM((blocks, feats // PAIR, PAIR, 2 * QB), BF16),
            pltpu.VMEM((blocks, 8, 2 * QB), F32),
            pltpu.VMEM((blocks, feats // PAIR, HD, 2 * QB), F32),
            pltpu.VMEM((feats, rows), F32),
            pltpu.VMEM((feats, rows), F32),
        ]
        + [pltpu.VMEM((2, feats // PAIR, KB, 2 * QB), kind) for kind in (F32, F32, BF16, BF16)],
        compiler_params=pltpu.CompilerParams(vmem_limit_bytes=VMEM_CAP),
        cost_estimate=pl.CostEstimate(
            flops=10 * rows * rows * feats, bytes_accessed=rows * feats * 28, transcendentals=rows * rows
        ),
        name="attend_back",
    )(lengths, qt, k, kt, v, do, ot, lse, cosine, sine)


def neighbours():
    me = lax.axis_index("mp")
    one = lax.rem(me, 2)
    across = me + 1 - 2 * one
    along = lax.rem(me + 2, 4)
    return me, across, along, lax.rem(across + 2, 4)


def remote(src, dst, sems, kind, step, device):
    send, recv = sems
    return pltpu.make_async_remote_copy(
        src_ref=src,
        dst_ref=dst,
        send_sem=send.at[kind, step],
        recv_sem=recv.at[kind, step],
        device_id={"mp": device},
        device_id_type=MESH,
    )


def pack_neighbours(packs):
    index = lax.axis_index("dp")
    core, chip = lax.rem(index, 2), index // 2
    chips = packs // 2
    return core, chip, index + 1 - 2 * core, [
        lax.rem(index + 2 * shift, packs) for shift in range(1, chips)
    ]


def chip_across(chip, bits):
    low, high = lax.rem(chip, 2), chip // 2
    low = 1 - low if bits % 2 else low
    high = 1 - high if bits // 2 else high
    return low + 2 * high


def remote_pack(src, dst, send, recv, device):
    return pltpu.make_async_remote_copy(
        src_ref=src, dst_ref=dst, send_sem=send, recv_sem=recv,
        device_id={"dp": device}, device_id_type=MESH,
    )


CHIPS = 4
PILES = (((0, 2), 0), ((1, 3), 0), ((0, 1), 2), ((2, 3), 2))
PARTNERS = (1, 2)


def group_barrier(devices, packs=()):
    barrier = pltpu.get_barrier_semaphore()
    for device in devices:
        pl.semaphore_signal(barrier, inc=1, device_id={"mp": device}, device_id_type=MESH)
    for device in packs:
        pl.semaphore_signal(barrier, inc=1, device_id={"dp": device}, device_id_type=MESH)
    pl.semaphore_wait(barrier, len(devices) + len(packs))


def scatter_first(part, slot, from_x, from_y, sems, kind, step):
    me, x, y, d = neighbours()
    return [
        remote(part.at[slot, x, 0], from_x.at[step, 0], sems, kind, step, x),
        remote(part.at[slot, y, 1], from_y.at[step, 0], sems, kind + 1, step, y),
        remote(part.at[slot, d, 0], from_x.at[step, 1], sems, kind + 2, step, x),
        remote(part.at[slot, d, 1], from_y.at[step, 1], sems, kind + 3, step, y),
    ]


def scatter_second(from_x, from_y, last_x, last_y, sems, kind, step):
    me, x, y, d = neighbours()
    return [
        remote(from_x.at[step, 1], last_y.at[step], sems, kind + 4, step, y),
        remote(from_y.at[step, 1], last_x.at[step], sems, kind + 5, step, x),
    ]


def scatter_middle(part, slot, from_x, from_y, last_x, last_y, sems, kind, step):
    me, x, y, d = neighbours()
    first = scatter_first(part, slot, from_x, from_y, sems, kind, step)
    second = scatter_second(from_x, from_y, last_x, last_y, sems, kind, step)
    first[2].wait_recv()
    total = from_x[step, 1].astype(F32) + part[slot, y, 0].astype(F32)
    from_x[step, 1] = total.astype(BF16)
    second[0].start()
    first[3].wait_recv()
    total = from_y[step, 1].astype(F32) + part[slot, x, 1].astype(F32)
    from_y[step, 1] = total.astype(BF16)
    second[1].start()


def scatter_last(part, slot, from_x, from_y, last_x, last_y, sems, kind, step):
    me, x, y, d = neighbours()
    first = scatter_first(part, slot, from_x, from_y, sems, kind, step)
    second = scatter_second(from_x, from_y, last_x, last_y, sems, kind, step)
    first[0].wait_recv()
    first[1].wait_recv()
    second[0].wait_recv()
    second[1].wait_recv()
    upper = part[slot, me, 0].astype(F32) + from_x[step, 0].astype(F32) + last_y[step].astype(F32)
    lower = part[slot, me, 1].astype(F32) + from_y[step, 0].astype(F32) + last_x[step].astype(F32)
    for copy in first + second:
        copy.wait_send()
    return jnp.concatenate([upper, lower], axis=0)


def ffn_kernel(
    packs,
    len_ref, early0, early1, early2, early3, o_hbm, tok_hbm, cot_hbm, wo0, wo1, wo2, wo3, wg_hbm, wu_hbm, wd_hbm, gain_ref, bias_ref,
    h1_ref, dh1_ref, sums_ref, do_hbm, land_hbm, down0_hbm, down1_hbm, down2_hbm, down3_hbm, rows_hbm, *rest,
):
    chips = packs // 2
    piles = rest[: len(PILES)]
    (
        wo, wg, wu, wd, o_all, tok, cot, h1_all, hid, dgate, dup, part, from_x, from_y, last_x, last_y,
        a2_t, eb_t, acc, stage, do_own, db_own, load_sem, tok_sem, cot_sem, own_sem, early_sem, stage_sem, put_sem, pile_sem,
        core_send, core_recv, send_sem, recv_sem,
    ) = rest[len(PILES) :]
    core, chip, other_core, _ = pack_neighbours(packs)
    steps, owners, block, width = o_all.shape
    share = width // packs
    feats = o_hbm.shape[-1]
    size = owners * block
    tiles = [pl.ds(at, TILE) for at in range(0, width, TILE)]
    early = early0.shape[1]
    some = owners
    sems = (send_sem, recv_sem)
    me, x, y, d = neighbours()
    row_total = owners * steps * block
    live_end = row_total - len_ref[0, len_ref.shape[1] - 1]

    loads = [(wg_hbm, wg), (wu_hbm, wu), (wd_hbm, wd)]
    for source, group in ((wo0, me), (wo1, x), (wo2, y), (wo3, d)):
        loads.append((source, wo.at[pl.ds(pl.multiple_of(group * feats, feats), feats)]))
    loads = [pltpu.make_async_copy(a, b, load_sem.at[i]) for i, (a, b) in enumerate(loads)]

    def fetch(step):
        slot = lax.rem(step, 2)
        return (
            pltpu.make_async_copy(tok_hbm.at[:, step], tok.at[slot], tok_sem.at[slot]),
            pltpu.make_async_copy(cot_hbm.at[:, step], cot.at[slot], cot_sem.at[slot]),
        )

    def lanes(group):
        return pl.ds(pl.multiple_of(group * feats, feats), feats)

    def early_copies(step):
        return [
            pltpu.make_async_copy(
                source.at[:, step], o_all.at[step, :, :, lanes(group)], early_sem.at[step, i]
            )
            for i, (source, group) in enumerate(
                ((early0, me), (early1, x), (early2, y), (early3, d))
            )
            if step < source.shape[1]
        ]

    def own_copy(step):
        return pltpu.make_async_copy(
            o_hbm.at[:, step - early], o_all.at[step, :, :, lanes(me)], own_sem.at[step]
        )

    def gather_own(step):
        source, target = o_hbm.at[:, step - early], o_all.at[step, :, :, lanes(me)]
        return [
            remote(source, target, sems, 0, step, x),
            remote(source, target, sems, 1, step, y),
        ]

    halfway = owners // 2

    def gather_relay(step):
        upper = o_all.at[step, pl.ds(0, halfway), :, lanes(x)]
        lower = o_all.at[step, pl.ds(halfway, halfway), :, lanes(y)]
        return [
            remote(upper, upper, sems, 2, step, y),
            remote(lower, lower, sems, 3, step, x),
        ]

    def relay(step):
        for copy, passed in zip(gather_own(step), gather_relay(step)):
            copy.wait_recv()
            passed.start()

    outgoing = (hid, dgate, dup)

    def to_core(kind):
        source = outgoing[kind] if kind < 3 else stage.at[steps % 2].reshape(size, width)
        return remote_pack(
            source, land_hbm.at[kind], core_send.at[kind], core_recv.at[kind], other_core
        )

    def landed(kind):
        return pltpu.make_async_copy(
            land_hbm.at[kind], tok.at[kind % 2].reshape(size, width), tok_sem.at[kind % 2]
        )

    def pile_copies(kind):
        summed = cot.at[kind % 2].reshape(size, width)
        return [
            pltpu.make_async_copy(
                summed.at[pl.ds(pl.multiple_of(chip_across(chip, bits) * share, share), share)],
                pile.at[i, kind - first],
                pile_sem.at[kind % 2, bits],
            )
            for pile, (places, first) in zip(piles, PILES)
            for i, bits in enumerate(places)
            if first <= kind < first + 2
        ]

    def sum_kind(kind):
        landed(kind).wait()
        if kind >= 2:
            for copy in pile_copies(kind - 2):
                copy.wait()
        theirs = tok[kind % 2].reshape(size, width)
        if kind < 3:
            mine = [
                acc[kind, pl.ds(pl.multiple_of((2 * z + core) * share, share), share), :]
                for z in range(chips)
            ]
            mine = jnp.concatenate(mine, axis=0)
        else:
            mine = h1_all[...].reshape(size, width)
        total = (mine + theirs.astype(F32)).astype(BF16)
        cot[kind % 2] = total.reshape(owners, block, width)
        for copy in pile_copies(kind):
            copy.start()

    def put_rows():
        slot = (steps - 1) % 2
        return [
            remote(stage.at[slot, target], rows_hbm.at[i], sems, 13 + i, 0, target)
            for i, target in enumerate((x, y))
        ]

    def put_do(step):
        return [
            remote(do_own.at[step, target], do_hbm.at[me, step], sems, 10 + i, step, target)
            for i, target in enumerate((x, y, d))
        ]

    def keep_do(step):
        return pltpu.make_async_copy(do_own.at[step, me], do_hbm.at[me, step], put_sem.at[step])

    for copy in fetch(0):
        copy.start()
    for copy in loads:
        copy.start()
    for step in range(early):
        for copy in early_copies(step):
            copy.start()
    group_barrier((x, y, d), (other_core,))

    def begin(step, _):
        for copy in gather_own(step):
            copy.start()
        own_copy(step).start()
        return 0

    lax.fori_loop(early, steps, begin, 0)
    acc[...] = jnp.zeros_like(acc)
    sums_ref[...] = jnp.zeros_like(sums_ref)
    for copy in loads:
        copy.wait()

    def step_body(step, _):
        slot = lax.rem(step, 2)
        now, before, older = [lax.rem(step + lag, 3) for lag in (0, 2, 1)]

        @pl.when(step + 1 < steps)
        def _():
            for copy in fetch(step + 1):
                copy.start()

        @pl.when((step + 1 < steps) & (step + 1 >= early))
        def _():
            relay(step + 1)

        for which in range(early):

            @pl.when(step == which)
            def _():
                if which == 0:
                    for copy in early_copies(0):
                        copy.wait()
                    for after in range(1, early):
                        for copy in early_copies(after):
                            copy.wait()
                        for copy in gather_relay(after):
                            copy.start()
                else:
                    for copy in gather_relay(which):
                        copy.wait_recv()

        @pl.when((step < steps) & (step >= early))
        def _():
            for copy in gather_relay(step):
                copy.wait_recv()
            own_copy(step).wait()

        @pl.when(step < steps)
        def _():
            for copy in fetch(step):
                copy.wait()
            def some_rows(turn, _):
                count = some * block
                who = pl.ds(turn * some, some)
                rows = pl.ds(pl.multiple_of(turn * count, count), count)
                position = lax.broadcasted_iota(jnp.int32, (some, block, 1), 1) + step * block
                position = position + (steps * block) * (
                    lax.broadcasted_iota(jnp.int32, (some, block, 1), 0) + turn * some
                )
                eb = jnp.where(position < live_end, cot[slot, who].astype(F32), 0.0).astype(BF16)
                cot[slot, who] = eb
                eb = eb.reshape(count, width)
                mixed = o_all[step, who].reshape(count, width)
                for cols in tiles:
                    h1 = tok[slot, who, :, cols].reshape(count, TILE).astype(F32)
                    h1 = h1 + mm(mixed, wo[:, cols])
                    h1_all[who, :, cols] = h1.reshape(some, block, TILE)
                hat, _ = norm_rows(h1_all[who].reshape(count, width))
                a2 = (hat * gain_ref[...] + bias_ref[...]).astype(BF16)

                def products(cols):
                    return mm(a2, wg[:, cols]), mm(a2, wu[:, cols]), mm_nt(eb, wd[cols, :])

                def hidden(cols, gate, up, back):
                    sig = 0.5 * jnp.tanh(0.5 * gate) + 0.5
                    act = gate * sig
                    hid[rows, cols] = (act * up).astype(BF16)
                    dgate[rows, cols] = (back * up * (sig + act * (1.0 - sig))).astype(BF16)
                    dup[rows, cols] = (back * act).astype(BF16)

                ready = products(tiles[0])
                a2_t[:, rows] = a2.T
                eb_t[:, rows] = eb.T
                for cols, ahead in zip(tiles, tiles[1:] + [None]):
                    coming = products(ahead) if ahead is not None else None
                    hidden(cols, *ready)
                    ready = coming
                for cols in tiles:
                    dc = mm_nt(dgate[rows, :], wg[cols, :]) + mm_nt(dup[rows, :], wu[cols, :])
                    part[now, who, :, :, cols] = dc.astype(BF16).reshape(some, 2, block // 2, TILE)
                return 0

            lax.fori_loop(0, owners // some, some_rows, 0)
            h1_ref[step] = h1_all[me]
            dh1_ref[step] = cot[slot, me].astype(F32)
            for copy in scatter_first(part, now, from_x, from_y, sems, 4, step):
                copy.start()

        @pl.when(step == steps)
        def _():
            for kind in range(3):
                for z in range(chips):
                    rows = pl.ds(pl.multiple_of((2 * z + 1 - core) * share, share), share)
                    outgoing[kind][z * share : (z + 1) * share, :] = acc[kind, rows, :].astype(BF16)
                to_core(kind).start()

        @pl.when((step >= 1) & (step <= steps))
        def _():
            scatter_middle(
                part, before, from_x, from_y, last_x, last_y, sems, 4, step - 1
            )

        @pl.when(step == steps)
        def _():
            for kind in range(2):
                to_core(kind).wait_recv()
                landed(kind).start()
            sum_kind(0)
            to_core(2).wait_recv()
            landed(2).start()
            sum_kind(1)
            sum_kind(2)

        def stage_copies(at, final):
            slot = lax.rem(at, 2)
            places = [(me, down0_hbm), (d, down3_hbm)]
            if not final:
                places += [(x, down1_hbm), (y, down2_hbm)]
            return [
                pltpu.make_async_copy(stage.at[slot, who], out.at[at], stage_sem.at[i, slot])
                for i, (who, out) in enumerate(places)
            ]

        @pl.when(step < steps)
        def _():
            @pl.when(step >= 2)
            def _():
                for copy in stage_copies(step - 2, False):
                    copy.wait()

            def some_output(turn, _):
                count = some * block
                who = pl.ds(turn * some, some)
                rows = pl.ds(pl.multiple_of(turn * count, count), count)
                for cols in tiles:
                    partial = mm(hid[rows, :], wd[:, cols]).astype(BF16)
                    stage[slot, who, :, cols] = partial.reshape(some, block, TILE)
                return 0

            lax.fori_loop(0, owners // some, some_output, 0)

            @pl.when(step < steps - 1)
            def _():
                for copy in stage_copies(step, False):
                    copy.start()

            @pl.when(step == steps - 1)
            def _():
                for copy in stage_copies(step, True):
                    copy.start()

            def some_grads(turn, _):
                rows = pl.ds(pl.multiple_of(turn * size, size), size)
                for cols in tiles:
                    acc[0, rows, cols] += mm(a2_t[rows, :], dgate[:, cols])
                    acc[1, rows, cols] += mm(a2_t[rows, :], dup[:, cols])
                    acc[2, rows, cols] += mm(eb_t[rows, :], hid[:, cols])
                return 0

            lax.fori_loop(0, width // size, some_grads, 0)

        @pl.when(step == steps)
        def _():
            for copy in stage_copies(steps - 2, False) + stage_copies(steps - 1, True):
                copy.wait()

        @pl.when(step >= 2)
        def _():
            prev = step - 2
            dc = scatter_last(part, older, from_x, from_y, last_x, last_y, sems, 4, prev)
            hat, scale = norm_rows(h1_ref[prev])
            sums_ref[0:1] += jnp.sum(dc * hat, axis=0, keepdims=True)
            sums_ref[1:2] += jnp.sum(dc, axis=0, keepdims=True)
            inner = dc * gain_ref[...]
            inner = inner - jnp.mean(inner, axis=-1, keepdims=True) - hat * jnp.mean(
                inner * hat, axis=-1, keepdims=True
            )
            dh1 = dh1_ref[prev] + scale * inner
            dh1_ref[prev] = dh1
            db = dh1.astype(BF16)
            db_own[prev] = db
            back = mm_nt(db, wo[...]).astype(BF16)
            for group in range(owners):
                do_own[prev, group] = back[:, group * feats : (group + 1) * feats]
            for copy in put_do(prev):
                copy.start()
            keep_do(prev).start()

        @pl.when(step == steps)
        def _():
            for copy in put_rows():
                copy.start()

        return 0

    lax.fori_loop(0, steps + 2, step_body, 0)

    o_mine = jnp.concatenate([o_all[step, me] for step in range(steps)], axis=0)
    for turn, which in enumerate((1 - core, core)):
        columns = [
            db_own[:, :, pl.ds(pl.multiple_of((2 * z + which) * share, share), share)].reshape(
                steps * block, share
            )
            for z in range(chips)
        ]
        values = mm_tn(jnp.concatenate(columns, axis=1), o_mine)
        if turn == 0:
            stage[steps % 2] = values.astype(BF16).reshape(owners, block, width)
            to_core(3).start()
        else:
            h1_all[...] = values.reshape(owners, block, width)

    to_core(3).wait_recv()
    landed(3).start()
    sum_kind(3)
    for kind in range(4):
        to_core(kind).wait_send()
    for copy in pile_copies(2) + pile_copies(3):
        copy.wait()

    for step in range(1, early):
        for copy in gather_relay(step):
            copy.wait_send()

    def sent(step, _):
        for copy in gather_own(step) + gather_relay(step):
            copy.wait_send()
        return 0

    lax.fori_loop(early, steps, sent, 0)

    for copy in put_rows():
        copy.wait()

    def finish(step, _):
        for copy in put_do(step):
            copy.wait()
        keep_do(step).wait()
        return 0

    lax.fori_loop(0, steps, finish, 0)


def ffn(lengths, early, o, tokens, cotangent, wo, wg, wu, wd, gain, bias, steps, packs):
    rows, width = tokens.shape
    feats = o.shape[-1]
    owners = width // feats
    block = rows // (owners * steps)
    hidden = wg.shape[1]
    size = owners * block
    chips = packs // 2
    by_owner = lambda a: a.reshape(owners, steps, block, a.shape[1])
    own = jax.ShapeDtypeStruct((steps, block, width), F32)
    half = (steps, 2, block // 2, width)
    dma = pltpu.SemaphoreType.DMA
    flops = 2 * rows * width * (width + 9 * hidden)
    h1, dh1, sums, do, _, *rest = pl.pallas_call(
        functools.partial(ffn_kernel, packs),
        in_specs=[SMEM] + [ANY] * 14 + [VMEM, VMEM],
        out_specs=[VMEM, VMEM, VMEM] + [ANY] * (7 + len(PILES)),
        out_shape=[
            own,
            own,
            jax.ShapeDtypeStruct((2, width), F32),
            jax.ShapeDtypeStruct((owners, steps, block, feats), BF16),
            jax.ShapeDtypeStruct((4, size, width), BF16),
        ]
        + [
            jax.ShapeDtypeStruct((taken, block, width), BF16)
            for taken in (steps, steps - 1, steps - 1, steps, 2)
        ]
        + [jax.ShapeDtypeStruct((2, 2, width // packs, width), BF16)] * len(PILES),
        scratch_shapes=[
            pltpu.VMEM((width, width), BF16),
            pltpu.VMEM((width, hidden), BF16),
            pltpu.VMEM((width, hidden), BF16),
            pltpu.VMEM((hidden, width), BF16),
            pltpu.VMEM((steps, owners, block, width), BF16),
            pltpu.VMEM((2, owners, block, width), BF16),
            pltpu.VMEM((2, owners, block, width), BF16),
            pltpu.VMEM((owners, block, width), F32),
            pltpu.VMEM((size, hidden), BF16),
            pltpu.VMEM((size, hidden), BF16),
            pltpu.VMEM((size, hidden), BF16),
            pltpu.VMEM((3, owners, 2, block // 2, width), BF16),
            pltpu.VMEM(half, BF16),
            pltpu.VMEM(half, BF16),
            pltpu.VMEM((steps, block // 2, width), BF16),
            pltpu.VMEM((steps, block // 2, width), BF16),
            pltpu.VMEM((width, size), BF16),
            pltpu.VMEM((width, size), BF16),
            pltpu.VMEM((3, width, hidden), F32),
            pltpu.VMEM((2, owners, block, width), BF16),
            pltpu.VMEM((steps, owners, block, feats), BF16),
            pltpu.VMEM((steps, block, width), BF16),
            dma((7,)),
            dma((2,)),
            dma((2,)),
            dma((steps,)),
            dma((early[0].shape[1], 4)),
            dma((4, 2)),
            dma((steps,)),
            dma((2, chips)),
            dma((4,)),
            dma((4,)),
            dma((15, steps)),
            dma((15, steps)),
        ],
        compiler_params=pltpu.CompilerParams(
            collective_id=0, has_side_effects=True, vmem_limit_bytes=VMEM_CAP
        ),
        cost_estimate=pl.CostEstimate(flops=flops, bytes_accessed=rows * width * 14, transcendentals=0),
        name="ffn",
    )(lengths, *early, o, by_owner(tokens), by_owner(cotangent), *wo, wg, wu, wd, gain, bias)
    return h1, dh1, sums, do.reshape(rows, feats), rest[:5], rest[5:]


def last_kernel(
    packs,
    grad_hbm, grad_t_hbm, a1_hbm, tok_hbm, dh1_ref, h1_hbm, wq_ref, wk_ref, wv_ref, gain_ref, sums2_ref, *rest,
):
    chips = packs // 2
    downs, rest = rest[:5], rest[5:]
    piles, rest = rest[: len(PILES)], rest[len(PILES) :]
    (
        out_hbm, tg_hbm, gq_hbm, gk_hbm, gv_hbm, gate_hbm, up_hbm, down_hbm, proj_hbm, norm_ref,
        out_ref, tg_ref, gq_ref, gk_ref, gv_ref, gate_ref, up_ref, down_ref, proj_ref, row_sem, result_sem,
        grad, grad_t, a1, tok, part, from_x, from_y, last_x, last_y, h1, down, pile, pile_out, pile_in, sums1,
        full, core_out, core_in, chip_out, chip_in, proj_out, proj_in, norm_out, norm_in,
        grad_sem, tok_sem, load_sem, core_send, core_recv, chip_send, chip_recv, pile_send, pile_recv,
        small_send, small_recv, send_sem, recv_sem,
    ) = rest
    steps, owners, _, half, width = part.shape
    feats = wq_ref.shape[1]
    size = owners * 2 * half
    share = width // packs
    tall = 3 * feats
    sems = (send_sem, recv_sem)
    me, x, y, d = neighbours()
    core, chip, other_core, next_chips = pack_neighbours(packs)

    def fetch(step):
        return [
            pltpu.make_async_copy(grad_hbm.at[:, step], grad.at[step], grad_sem.at[step]),
            pltpu.make_async_copy(tok_hbm.at[:, step], tok.at[step], tok_sem.at[step]),
        ]

    later = [(grad_t_hbm, grad_t), (a1_hbm, a1)]
    later += [(piles[i], pile.at[i]) for i in range(len(PILES))]
    later += [(h1_hbm, h1)]
    later += [(downs[i], down.at[i, pl.ds(0, downs[i].shape[0])]) for i in range(4)]
    later += [(downs[4], down.at[pl.ds(1, 2), steps - 1])]
    later = [pltpu.make_async_copy(a, b, load_sem.at[i]) for i, (a, b) in enumerate(later)]

    def to_core():
        return remote_pack(core_out, core_in, core_send, core_recv, other_core)

    def to_chips():
        return [
            remote_pack(
                chip_out.at[lax.rem(chip + i + 1, chips)], chip_in.at[i],
                chip_send.at[i], chip_recv.at[i], device,
            )
            for i, device in enumerate(next_chips)
        ]

    def pile_copies():
        index = lax.axis_index("dp")
        return [
            remote_pack(
                pile_out.at[i], pile_in.at[i], pile_send.at[i], pile_recv.at[i],
                index + 2 * (chip_across(chip, bits) - chip),
            )
            for i, bits in enumerate(reversed(PARTNERS))
        ]

    def small(kind, source, target):
        return [
            remote(source(device), target.at[i], (small_send, small_recv), kind, i, device)
            for i, device in enumerate((x, y, d))
        ]

    def proj_copies():
        return small(0, lambda device: proj_out.at[device], proj_in)

    def norm_copies():
        return small(1, lambda device: norm_out, norm_in)

    def begin(step, _):
        for copy in fetch(step):
            copy.start()
        return 0

    lax.fori_loop(0, steps, begin, 0)
    for copy in later:
        copy.start()
    group_barrier((x, y, d), [other_core] + next_chips)
    sums1[...] = jnp.zeros_like(sums1)

    def first(step, _):
        for copy in fetch(step):
            copy.wait()
        rows = grad[step].reshape(size, tall)
        da = mm_nt(rows[:, :feats], wq_ref[...])
        da = da + mm_nt(rows[:, feats : 2 * feats], wk_ref[...])
        da = da + mm_nt(rows[:, 2 * feats :], wv_ref[...])
        part[step] = da.astype(BF16).reshape(owners, 2, half, width)
        for copy in scatter_first(part, step, from_x, from_y, sems, 0, step):
            copy.start()

        @pl.when(step == 0)
        def _():
            for copy in later[2 : 2 + len(PILES)]:
                copy.wait()
            for i in range(2):
                total = pile[2 * i, 1].astype(F32) + pile[2 * i + 1, 1].astype(F32)
                pile_out[i] = total.astype(BF16)
            for copy in pile_copies():
                copy.start()

        hat, _ = norm_rows(tok[step].reshape(size, width).astype(F32))
        sums1[0:1] += jnp.sum(da * hat, axis=0, keepdims=True)
        sums1[1:2] += jnp.sum(da, axis=0, keepdims=True)
        return 0

    lax.fori_loop(0, steps, first, 0)
    later[0].wait()
    later[1].wait()
    for kind in range(3):
        rows = pl.ds(kind * feats, feats)
        full[rows, :] = mm(grad_t[rows, :], a1[...])
    full[pl.ds(tall, 16), :] = jnp.concatenate(
        [sums1[...], sums2_ref[...], jnp.zeros((12, width), F32)], axis=0
    )
    for z in range(chips):
        columns = pl.ds(pl.multiple_of((2 * z + 1 - core) * share, share), share)
        core_out[z] = full[:, columns].astype(BF16)
    to_core().start()

    to_core().wait_recv()
    for z in range(chips):
        columns = pl.ds(pl.multiple_of((2 * z + core) * share, share), share)
        chip_out[z] = (full[:, columns] + core_in[z].astype(F32)).astype(BF16)
    for copy in to_chips():
        copy.start()
    for copy in later[2 + len(PILES) :]:
        copy.wait()

    def sum_piles():
        for copy in pile_copies():
            copy.wait_recv()
        for kind in range(4):
            half, at = kind // 2, kind % 2
            total = pile[2 * half, 0, at].astype(F32) + pile[2 * half + 1, 0, at].astype(F32)
            total = total + pile_in[half, at].astype(F32)
            if kind < 2:
                (gate_ref, up_ref)[kind][...] = total
            elif kind == 2:
                down_ref[...] = total.T
            else:
                for group in range(owners):
                    proj_out[group] = total[:, group * feats : (group + 1) * feats].astype(BF16)
                for copy in proj_copies():
                    copy.start()

    def row_copies(step):
        return [
            pltpu.make_async_copy(source.at[step], out.at[step], row_sem.at[i, step])
            for i, (source, out) in enumerate(((out_ref, out_hbm), (tg_ref, tg_hbm)))
        ]

    results = (
        (gq_ref, gq_hbm), (gk_ref, gk_hbm), (gv_ref, gv_hbm), (gate_ref, gate_hbm),
        (up_ref, up_hbm), (down_ref, down_hbm), (proj_ref, proj_hbm),
    )
    results = [
        pltpu.make_async_copy(source, out, result_sem.at[i])
        for i, (source, out) in enumerate(results)
    ]

    def finish(step):
        da = scatter_last(part, step, from_x, from_y, last_x, last_y, sems, 0, step)
        hat, scale = norm_rows(tok[step, me].astype(F32))
        inner = da * gain_ref[...]
        inner = inner - jnp.mean(inner, axis=-1, keepdims=True) - hat * jnp.mean(
            inner * hat, axis=-1, keepdims=True
        )
        tg_ref[step] = (dh1_ref[step] + scale * inner).astype(BF16)
        row_copies(step)[1].start()

    def second(step, _):
        scatter_middle(part, step, from_x, from_y, last_x, last_y, sems, 0, step)
        total = h1[step]
        for i in range(4):
            total = total + down[i, step].astype(F32)
        out_ref[step] = total.astype(BF16)
        row_copies(step)[0].start()
        return 0

    def third(step, _):
        finish(step)
        return 0

    lax.fori_loop(0, steps, second, 0)
    sum_piles()
    for copy in results[3:6]:
        copy.start()
    lax.fori_loop(0, steps - 2, third, 0)
    total = chip_out[chip].astype(F32)
    for i, copy in enumerate(to_chips()):
        copy.wait_recv()
        total = total + chip_in[i].astype(F32)
    norm_out[...] = total[tall : tall + 8]
    for copy in norm_copies():
        copy.start()
    finish(steps - 2)
    for kind, ref in enumerate((gq_ref, gk_ref, gv_ref)):
        ref[...] = total[kind * feats : (kind + 1) * feats].T
        results[kind].start()
    total = proj_out[me].astype(F32)
    for i, copy in enumerate(proj_copies()):
        copy.wait_recv()
        total = total + proj_in[i].astype(F32)
    proj_ref[...] = total.T
    results[6].start()
    finish(steps - 1)
    total = norm_out[...]
    for i, copy in enumerate(norm_copies()):
        copy.wait_recv()
        total = total + norm_in[i]
    norm_ref[...] = total
    for copy in results:
        copy.wait()
    for step in range(steps):
        for copy in row_copies(step):
            copy.wait()
    for copy in [to_core()] + to_chips() + pile_copies() + proj_copies() + norm_copies():
        copy.wait_send()


def last(grads, grads_t, a1, tokens, dh1, h1, wq, wk, wv, gain, sums2, downs, piles, packs):
    rows, width = tokens.shape
    steps, block, _ = dh1.shape
    owners = rows // (steps * block)
    feats = wq.shape[1]
    hidden = piles[0].shape[-1]
    chips = packs // 2
    share = width // packs
    tall = 3 * feats + 16
    by_owner = lambda a: a.reshape(owners, steps, block, a.shape[1])
    half = (steps, 2, block // 2, width)
    dma = pltpu.SemaphoreType.DMA
    own = jax.ShapeDtypeStruct((steps, block, width), BF16)
    f32 = lambda *shape: jax.ShapeDtypeStruct(shape, F32)
    out_shape = [own, own] + [f32(share, feats)] * 3
    out_shape += [f32(share, hidden)] * 2 + [f32(hidden, share), f32(feats, share), f32(8, share)]
    return pl.pallas_call(
        functools.partial(last_kernel, packs),
        in_specs=[ANY] * 4 + [VMEM, ANY] + [VMEM] * 5 + [ANY] * (5 + len(piles)),
        out_specs=[ANY] * 9 + [VMEM],
        out_shape=out_shape,
        scratch_shapes=[pltpu.VMEM(a.shape, a.dtype) for a in out_shape[:9]]
        + [
            dma((2, steps)),
            dma((7,)),
            pltpu.VMEM((steps, owners, block, 3 * feats), BF16),
            pltpu.VMEM((3 * feats, rows), BF16),
            pltpu.VMEM((rows, width), BF16),
            pltpu.VMEM((steps, owners, block, width), BF16),
            pltpu.VMEM((steps, owners, 2, block // 2, width), BF16),
            pltpu.VMEM(half, BF16),
            pltpu.VMEM(half, BF16),
            pltpu.VMEM((steps, block // 2, width), BF16),
            pltpu.VMEM((steps, block // 2, width), BF16),
            pltpu.VMEM((steps, block, width), F32),
            pltpu.VMEM((4, steps, block, width), BF16),
            pltpu.VMEM((len(PILES), 2, 2, share, hidden), BF16),
            pltpu.VMEM((2, 2, share, hidden), BF16),
            pltpu.VMEM((2, 2, share, hidden), BF16),
            pltpu.VMEM((2, width), F32),
            pltpu.VMEM((tall, width), F32),
            pltpu.VMEM((chips, tall, share), BF16),
            pltpu.VMEM((chips, tall, share), BF16),
            pltpu.VMEM((chips, tall, share), BF16),
            pltpu.VMEM((chips - 1, tall, share), BF16),
            pltpu.VMEM((owners, share, feats), BF16),
            pltpu.VMEM((owners - 1, share, feats), BF16),
            pltpu.VMEM((8, share), F32),
            pltpu.VMEM((owners - 1, 8, share), F32),
            dma((steps,)),
            dma((steps,)),
            dma((8 + len(piles),)),
            dma,
            dma,
            dma((chips - 1,)),
            dma((chips - 1,)),
            dma((2,)),
            dma((2,)),
            dma((2, owners - 1)),
            dma((2, owners - 1)),
            dma((6, steps)),
            dma((6, steps)),
        ],
        compiler_params=pltpu.CompilerParams(
            collective_id=1, has_side_effects=True, vmem_limit_bytes=VMEM_CAP
        ),
        cost_estimate=pl.CostEstimate(
            flops=12 * rows * width * feats, bytes_accessed=rows * width * 20, transcendentals=0
        ),
        name="last",
    )(
        by_owner(grads), grads_t, a1, by_owner(tokens), dh1, h1, wq, wk, wv, gain, sums2, *downs, *piles
    )


def hand_out_kernel(count, *refs):
    sources, norm_ref, refs = refs[:count], refs[count], refs[count + 1 :]
    outs, norms, held = refs[:count], refs[count : count + 4], refs[count + 4 : 2 * count + 4]
    in_sem, out_sem = refs[2 * count + 4 :]
    loads = [pltpu.make_async_copy(sources[i], held[i], in_sem.at[i]) for i in range(count)]
    stores = [pltpu.make_async_copy(held[i], outs[i], out_sem.at[i]) for i in range(count)]
    for copy in loads:
        copy.start()
    for i, norm in enumerate(norms):
        norm[...] = norm_ref[i]
    for load, store in zip(loads, stores):
        load.wait()
        store.start()
    for store in stores:
        store.wait()


def hand_out(arrays, norms):
    count = len(arrays)
    shape = lambda a: jax.ShapeDtypeStruct(a.shape, a.dtype)
    return pl.pallas_call(
        functools.partial(hand_out_kernel, count),
        in_specs=[ANY] * count + [VMEM],
        out_specs=[ANY] * count + [VMEM] * 4,
        out_shape=[shape(a) for a in arrays] + [jax.ShapeDtypeStruct(norms.shape[1:], F32)] * 4,
        scratch_shapes=[pltpu.VMEM(a.shape, a.dtype) for a in arrays]
        + [pltpu.SemaphoreType.DMA((count,))] * 2,
        compiler_params=pltpu.CompilerParams(vmem_limit_bytes=VMEM_CAP),
        name="hand_out",
    )(*arrays, norms)


def local_square(
    tokens, lengths, cotangent, norm1_gain, norm1_bias, w_query, w_key, w_value, w_output,
    norm2_gain, norm2_bias, w_gate, w_up, w_down,
):
    rows, width = tokens.shape
    groups = lax.axis_size("mp")
    packs = lax.axis_size("dp")
    gain1, bias1 = norm1_gain[None, :], norm1_bias[None, :]
    exchange = lambda a, shift: lax.ppermute(a, "mp", [(i, i ^ shift) for i in range(groups)])
    w_outputs = [w_output] + [exchange(w_output, shift) for shift in range(1, groups)]
    a1, k, v, qt, kt, vt, cosine, sine = project(
        lengths, tokens, gain1, bias1, w_query, w_key, w_value
    )
    early, early_first, mixed_t, lse = attend(lengths, qt, k, vt, 0, EARLY, STEPS)
    early = [early, exchange(early, 1), exchange(early, 2), exchange(early_first, 3)]
    qt_late, *w_outputs = lax.optimization_barrier((qt, *w_outputs))
    mixed, mixed_t, lse = attend(lengths, qt_late, k, vt, EARLY, STEPS, STEPS, (mixed_t, lse))
    h1, dh1, sums2, mixed_grad, downs, piles = ffn(
        lengths, early, mixed, tokens, cotangent, w_outputs, w_gate, w_up, w_down,
        norm2_gain[None, :], norm2_bias[None, :], STEPS, packs,
    )
    downs[1:4] = [exchange(downs[shift], shift) for shift in range(1, groups)]
    for i, bits in enumerate(PARTNERS):
        perm = [(j, j ^ (2 * bits)) for j in range(packs)]
        piles[2 * i + 1] = lax.ppermute(piles[2 * i + 1], "dp", perm)
    grads, grads_t = attend_back(
        lengths, qt, k, kt, v, mixed_grad, mixed_t, lse, cosine, sine
    )
    *results, norms = last(
        grads, grads_t, a1, tokens, dh1, h1, w_query, w_key, w_value, gain1, sums2, downs, piles, packs
    )
    output, tokens_grad, grad_q, grad_k, grad_v, gate, up, down, proj, *sums = hand_out(
        results, norms
    )
    own_rows = (rows // groups, width)
    return (
        output.reshape(own_rows),
        tokens_grad.reshape(own_rows),
        grad_q,
        grad_k,
        grad_v,
        proj,
        gate,
        up,
        down,
        *sums,
    )


def layer_stats(row_values, gain_vec, bias_vec):
    normed, row_scale = norm_rows(row_values)
    return (normed * gain_vec + bias_vec, normed, row_scale)


def layer_back(gradient, normed, row_scale, gain_vec):
    inner_grad = gradient * gain_vec
    centred_grad = inner_grad - jnp.mean(inner_grad, axis=-1, keepdims=True)
    return row_scale * (
        centred_grad - normed * jnp.mean(inner_grad * normed, axis=-1, keepdims=True)
    )


def scatter_rows(partial, axis, dim=0):
    return lax.psum_scatter(
        partial.astype(BF16), axis, scatter_dimension=dim, tiled=True
    ).astype(F32)


def local(
    tokens, lengths, cotangent, norm1_gain, norm1_bias, w_query, w_key, w_value, w_output,
    norm2_gain, norm2_bias, w_gate, w_up, w_down,
):
    row_count, width = tokens.shape
    feats = w_query.shape[1]
    gain1, bias1 = norm1_gain[None, :], norm1_bias[None, :]
    a1, k, v, qt, kt, vt, cosine, sine = project(
        lengths, tokens, gain1, bias1, w_query, w_key, w_value
    )
    mixed, mixed_t, lse = attend(lengths, qt, k, vt, 0, 1, 1)
    mixed = mixed.reshape(row_count, feats)

    share_rows = row_count // lax.axis_size("mp")
    own_start = lax.axis_index("mp") * share_rows
    own = lambda a: lax.dynamic_slice_in_dim(a, own_start, share_rows, 0)
    live_end = row_count - lengths[0, lengths.shape[1] - 1]
    live = jnp.arange(row_count, dtype=jnp.int32)[:, None] < live_end
    out_grad = jnp.where(live, cotangent, jnp.zeros_like(cotangent))

    attn_rows = scatter_rows(mm(mixed, w_output), "mp")
    residual = own(tokens).astype(F32) + attn_rows
    normed_second, hat_second, scale_second = layer_stats(residual, norm2_gain, norm2_bias)
    inputs_second = lax.all_gather(normed_second.astype(BF16), "mp", axis=0, tiled=True)
    gate_pre = mm(inputs_second, w_gate)
    up_proj = mm(inputs_second, w_up)
    gate_sig = jax.nn.sigmoid(gate_pre)
    gate_act = gate_pre * gate_sig
    hidden = (gate_act * up_proj).astype(BF16)
    output_own = residual + scatter_rows(mm(hidden, w_down), "mp")
    down_w_grad = mm_tn(hidden, out_grad)
    hidden_grad = mm_nt(out_grad, w_down)
    gate_in_grad = (hidden_grad * up_proj * gate_sig * (1.0 + gate_pre * (1.0 - gate_sig))).astype(BF16)
    up_in_grad = (hidden_grad * gate_act).astype(BF16)
    gate_w_grad = mm_tn(inputs_second, gate_in_grad)
    up_w_grad = mm_tn(inputs_second, up_in_grad)
    ffn_sums = (
        scatter_rows(gate_w_grad, "dp"),
        scatter_rows(up_w_grad, "dp"),
        scatter_rows(down_w_grad, "dp", 1),
    )
    second_grad = scatter_rows(mm_nt(gate_in_grad, w_gate) + mm_nt(up_in_grad, w_up), "mp")
    residual_grad = own(out_grad).astype(F32) + layer_back(
        second_grad, hat_second, scale_second, norm2_gain
    )
    attn_grad = lax.all_gather(residual_grad.astype(BF16), "mp", axis=0, tiled=True)
    gain_second_grad = jnp.sum(second_grad * hat_second, axis=0)
    bias_second_grad = jnp.sum(second_grad, axis=0)
    output_w_grad = mm_tn(mixed, attn_grad)
    mixed_grad = mm_nt(attn_grad, w_output).astype(BF16)

    grads, grads_t = attend_back(
        lengths, qt, k, kt, v, mixed_grad, mixed_t, lse, cosine, sine
    )
    w_qkv = jnp.concatenate([w_query, w_key, w_value], axis=1)
    qkv_w_grad = mm(grads_t, a1)
    first_grad = scatter_rows(mm_nt(grads, w_qkv), "mp")
    hat_own, scale_own = norm_rows(own(tokens).astype(F32))
    tokens_grad = (residual_grad + layer_back(first_grad, hat_own, scale_own, norm1_gain)).astype(BF16)
    gain_parts = jnp.stack(
        [
            jnp.sum(first_grad * hat_own, axis=0),
            jnp.sum(first_grad, axis=0),
            gain_second_grad,
            bias_second_grad,
        ]
    )
    gain_parts = scatter_rows(lax.psum(gain_parts, "mp"), "dp", 1)
    attn_sums = scatter_rows(jnp.concatenate([qkv_w_grad, output_w_grad], axis=0), "dp", 1)
    return (
        output_own.astype(BF16),
        tokens_grad,
        attn_sums[:feats].T,
        attn_sums[feats : 2 * feats].T,
        attn_sums[2 * feats : 3 * feats].T,
        attn_sums[3 * feats :],
        ffn_sums[0],
        ffn_sums[1],
        ffn_sums[2],
        gain_parts[0],
        gain_parts[1],
        gain_parts[2],
        gain_parts[3],
    )


def solution(mesh):
    square = mesh.shape["mp"] == 4 and mesh.shape["dp"] == 2 * CHIPS
    rows, weight_in, weight_out = P("dp", None), P(None, "mp"), P("mp", None)
    row_out = P(("dp", "mp"), None)
    return jax.shard_map(
        local_square if square else local,
        mesh=mesh,
        in_specs=(rows, rows, rows, P(), P(), weight_in, weight_in, weight_in, weight_out)
        + (P(), P(), weight_in, weight_in, weight_out),
        out_specs=(row_out, row_out)
        + (P("dp", "mp"),) * 3
        + (P("mp", "dp"), P("dp", "mp"), P("dp", "mp"), P("mp", "dp"))
        + (P("dp"),) * 4,
        check_vma=False,
    )
```

```python
import functools
import math

import jax
import jax.numpy as jnp
import numpy as np
from jax import lax
from jax.experimental import pallas as pl
from jax.experimental.pallas import tpu as pltpu
from jax.sharding import PartitionSpec as P

HD = 64
HALF = HD // 2
PAIR = 2 * HD
QB = 128
KB = 256
EPS = 1e-05
BASE = 10000.0
NEG = -1e30
MOST = 1024
SCALE = HD**-0.5
VMEM = pl.BlockSpec(memory_space=pltpu.VMEM)
SMEM = pl.BlockSpec(memory_space=pltpu.SMEM)
ANY = pl.BlockSpec(memory_space=pl.ANY)
MESH = pl.DeviceIdType.MESH
STEPS = 5
EARLY = 2
TILE = 256
VMEM_CAP = 62 << 20
F32 = jnp.float32
BF16 = jnp.bfloat16


def mm(a, b):
    return jnp.dot(a, b, preferred_element_type=F32)


def mm_nt(a, b):
    return lax.dot_general(a, b, (((1,), (1,)), ((), ())), preferred_element_type=F32)


def mm_tn(a, b):
    return lax.dot_general(a, b, (((0,), (0,)), ((), ())), preferred_element_type=F32)


def window_bounds(len_ref, position):
    entries = len_ref.shape[1]
    start = jnp.zeros_like(position)
    end = jnp.zeros_like(position)
    edge = jnp.int32(0)
    for entry in range(entries):
        size = len_ref[0, entry]
        inside = position >= edge
        start = jnp.where(inside, edge, start)
        edge = edge + size
        end = jnp.where(inside, edge, end)
    return start, end


def norm_rows(rows):
    mean = jnp.mean(rows, axis=-1, keepdims=True)
    centred = rows - mean
    scale = lax.rsqrt(jnp.mean(centred * centred, axis=-1, keepdims=True) + EPS)
    return centred * scale, scale


def rotate_t(field, cosine, sine, direction):
    parts = []
    for head in range(field.shape[0] // HD):
        first = field[head * HD : head * HD + HALF]
        second = field[head * HD + HALF : (head + 1) * HD]
        parts.append(first * cosine - direction * (second * sine))
        parts.append(second * cosine + direction * (first * sine))
    return jnp.concatenate(parts, axis=0)


def qkv_kernel(
    len_ref, tok_ref, gain_ref, bias_ref, freq_ref, wq_ref, wk_ref, wv_ref,
    a1_ref, k_ref, v_ref, qt_ref, kt_ref, vt_ref, cos_ref, sin_ref,
):
    rows = tok_ref.shape[0]
    position = lax.broadcasted_iota(jnp.int32, (1, rows), 1) + pl.program_id(0) * rows
    start, _ = window_bounds(len_ref, position)
    offset = (position - start).astype(F32)
    theta = freq_ref[...] * offset
    cosine, sine = jnp.cos(theta), jnp.sin(theta)
    cos_ref[...] = cosine
    sin_ref[...] = sine
    hat, _ = norm_rows(tok_ref[...].astype(F32))
    a1 = (hat * gain_ref[...] + bias_ref[...]).astype(BF16)
    a1_ref[...] = a1
    for w_ref, out_ref, out_t_ref, scale in (
        (wq_ref, None, qt_ref, SCALE),
        (wk_ref, k_ref, kt_ref, None),
    ):
        field = rotate_t(mm(a1, w_ref[...]).T, cosine, sine, 1.0).astype(BF16)
        if scale is not None:
            field = field * jnp.asarray(scale, BF16)
        out_t_ref[...] = field
        if out_ref is not None:
            out_ref[...] = field.T
    values = mm(a1, wv_ref[...]).astype(BF16)
    v_ref[...] = values
    vt_ref[...] = values.T


def project(lengths, tokens, gain, bias, wq, wk, wv):
    rows, width = tokens.shape
    feats = wq.shape[1]
    block = min(512, rows)
    freq = np.float32(BASE) ** (np.float32(-2.0 / HD) * np.arange(HALF, dtype=np.float32))
    freq = jnp.asarray(freq[:, None], F32)
    whole = lambda a: pl.BlockSpec(a.shape, lambda i: (0, 0))
    by_row = lambda cols: pl.BlockSpec((block, cols), lambda i: (i, 0))
    by_col = lambda size: pl.BlockSpec((size, block), lambda i: (0, i))
    nat = jax.ShapeDtypeStruct((rows, feats), BF16)
    trans = jax.ShapeDtypeStruct((feats, rows), BF16)
    table = jax.ShapeDtypeStruct((HALF, rows), F32)
    return pl.pallas_call(
        qkv_kernel,
        grid=(rows // block,),
        in_specs=[SMEM, by_row(width)] + [whole(a) for a in (gain, bias, freq, wq, wk, wv)],
        out_specs=[by_row(width)] + [by_row(feats)] * 2 + [by_col(feats)] * 3 + [by_col(HALF)] * 2,
        out_shape=[jax.ShapeDtypeStruct((rows, width), BF16)] + [nat] * 2 + [trans] * 3 + [table] * 2,
        compiler_params=pltpu.CompilerParams(vmem_limit_bytes=VMEM_CAP),
        cost_estimate=pl.CostEstimate(
            flops=6 * rows * width * feats, bytes_accessed=rows * width * 8, transcendentals=0
        ),
        name="qkv",
    )(lengths, tokens, gain, bias, freq, wq, wk, wv)


def block_diagonal_t(pair):
    head = lax.broadcasted_iota(jnp.int32, pair.shape, 0) < HD
    zero = jnp.zeros_like(pair)
    return jnp.concatenate([jnp.where(head, pair, zero), jnp.where(head, zero, pair)], axis=1)


def diagonal_blocks(product):
    return jnp.concatenate([product[:HD, :QB], product[HD:, QB:]], axis=1)


def key_range(len_ref, first):
    low, _ = window_bounds(len_ref, first)
    _, high = window_bounds(len_ref, first + (QB - 1))
    base = low // QB * QB
    return base, (high - base + (KB - 1)) // KB


def key_rows(at, rows):
    return pl.ds(pl.multiple_of(jnp.clip(at, 0, rows - KB), QB), KB)


def inside_window(start, end, at, rows):
    shift = jnp.minimum(at, rows - KB)
    key = lax.broadcasted_iota(jnp.int32, (KB, QB), 0)
    inside = (key >= jnp.maximum(start, at) - shift) & (key < end - shift)
    return jnp.concatenate([inside, inside], axis=1)


def fill_schedule(len_ref, sched, blocks, index_of, rows):
    def nothing(n):
        sched[0, n] = 0
        sched[1, n] = rows

    def one_query(turn, n):
        base, count = key_range(len_ref, index_of(turn) * QB)

        def one_key(kb, _):
            sched[0, n + kb] = turn
            sched[1, n + kb] = base + kb * KB
            return 0

        lax.fori_loop(0, count, one_key, 0)
        return n + count

    nothing(0)
    n = lax.fori_loop(0, blocks, one_query, jnp.int32(1))
    for extra in range(3):
        nothing(n + extra)
    return n - 1


def store_window(len_ref, window, turn, first):
    position = lax.broadcasted_iota(jnp.int32, (1, QB), 1) + first
    window[turn, 0:1], window[turn, 1:2] = window_bounds(len_ref, position)


def run_pipeline(count, scores, soften, mix):
    def two_pairs(turn, _):
        n = 1 + 2 * turn
        mix(n - 1, 1)
        scores(n + 1, 1)
        soften(n, 0)
        mix(n, 0)
        scores(n + 2, 0)
        soften(n + 1, 1)
        return 0

    turns = (count + 1) // 2
    scores(1, 0)
    lax.fori_loop(0, turns, two_pairs, 0)
    mix(2 * turns, 1)


def attend_kernel(begin, steps, len_ref, qt_ref, k_hbm, vt_hbm, *rest):
    if begin > 0:
        ot_before, lse_before, *rest = rest
    o_ref, *rest = rest
    first_ref = None
    if begin == 0 and steps > 1:
        first_ref, *rest = rest
    ot_ref, lse_ref, k_ref, vt_ref, load_sem, *rest = rest
    sched, window, diag, stat, acc, keep_buf, score_buf, prob_buf = rest
    loads = [
        pltpu.make_async_copy(k_hbm, k_ref, load_sem.at[0]),
        pltpu.make_async_copy(vt_hbm, vt_ref, load_sem.at[1]),
    ]
    for copy in loads:
        copy.start()
    if begin > 0:
        ot_ref[...] = ot_before[...]
        lse_ref[...] = lse_before[...]
    owners, taken = o_ref.shape[:2]
    feats, rows = qt_ref.shape
    pairs = range(feats // PAIR)
    feat = [pl.ds(p * PAIR, PAIR) for p in pairs]

    def index_of(turn):
        return turn // taken * steps + begin + lax.rem(turn, taken)

    def prepare(turn, _):
        first = index_of(turn) * QB
        cols = pl.ds(pl.multiple_of(first, QB), QB)
        store_window(len_ref, window, turn, first)
        for p in pairs:
            diag[turn, p] = block_diagonal_t(qt_ref[feat[p], cols])
            stat[turn, p : p + 1] = jnp.full((1, 2 * QB), NEG, F32)
            stat[turn, 4 + p : 5 + p] = jnp.zeros((1, 2 * QB), F32)
            acc[turn, p] = jnp.zeros((HD, 2 * QB), F32)
        return 0

    lax.fori_loop(0, owners * taken, prepare, 0)
    count = fill_schedule(len_ref, sched, owners * taken, index_of, rows)
    for copy in loads:
        copy.wait()

    def scores(n, buf):
        turn, keys = sched[0, n], key_rows(sched[1, n], rows)
        for p in pairs:
            score_buf[buf, p] = mm(k_ref[keys, feat[p]], diag[turn, p])

    def soften(n, buf):
        turn = sched[0, n]
        inside = inside_window(window[turn, 0:1], window[turn, 1:2], sched[1, n], rows)
        for p in pairs:
            top, total = stat[turn, p : p + 1], stat[turn, 4 + p : 5 + p]
            values = jnp.where(inside, score_buf[buf, p], NEG)
            new_top = jnp.maximum(top, jnp.max(values, axis=0, keepdims=True))
            prob = jnp.exp(values - new_top)
            keep = jnp.exp(top - new_top)
            stat[turn, p : p + 1] = new_top
            stat[turn, 4 + p : 5 + p] = keep * total + jnp.sum(prob, axis=0, keepdims=True)
            keep_buf[buf, p : p + 1] = keep
            prob_buf[buf, p] = prob.astype(BF16)

    def mix(n, buf):
        turn, keys = sched[0, n], key_rows(sched[1, n], rows)
        for p in pairs:
            mixed = diagonal_blocks(mm(vt_ref[feat[p], keys], prob_buf[buf, p]))
            acc[turn, p] = acc[turn, p] * keep_buf[buf, p : p + 1] + mixed

    prob_buf[1] = jnp.zeros_like(prob_buf[1])
    keep_buf[1] = jnp.ones_like(keep_buf[1])
    run_pipeline(count, scores, soften, mix)

    def finish(turn, _):
        index = index_of(turn)
        cols = pl.ds(pl.multiple_of(index * QB, QB), QB)
        for p in pairs:
            top, total = stat[turn, p : p + 1], stat[turn, 4 + p : 5 + p]
            mixed = acc[turn, p] / total
            mixed = jnp.concatenate([mixed[:, :QB], mixed[:, QB:]], axis=0).astype(BF16)
            lse_ref[index, p : p + 1] = top + jnp.log(total)
            ot_ref[feat[p], cols] = mixed
            mixed = mixed.T
            o_ref[turn // taken, lax.rem(turn, taken), :, feat[p]] = mixed
            if first_ref is not None:

                @pl.when(lax.rem(turn, taken) == 0)
                def _():
                    first_ref[turn // taken, 0, :, feat[p]] = mixed

        return 0

    lax.fori_loop(0, owners * taken, finish, 0)


def schedule_size(blocks):
    return blocks * ((2 * MOST + 2 * QB) // KB + 1) + 4


def attend(lengths, qt, k, vt, begin, end, steps, before=()):
    feats, rows = qt.shape
    pairs = feats // PAIR
    owners = rows // (steps * QB)
    share = (end - begin) / steps
    blocks = owners * (end - begin)
    first = []
    if begin == 0 and steps > 1:
        first = [jax.ShapeDtypeStruct((owners, 1, QB, feats), BF16)]
    return pl.pallas_call(
        functools.partial(attend_kernel, begin, steps),
        in_specs=[SMEM, VMEM, ANY, ANY] + [VMEM] * len(before),
        out_specs=[VMEM] * (3 + len(first)),
        out_shape=[jax.ShapeDtypeStruct((owners, end - begin, QB, feats), BF16)]
        + first
        + [
            jax.ShapeDtypeStruct((feats, rows), BF16),
            jax.ShapeDtypeStruct((rows // QB, pairs, 2 * QB), F32),
        ],
        scratch_shapes=[
            pltpu.VMEM((rows, feats), BF16),
            pltpu.VMEM((feats, rows), BF16),
            pltpu.SemaphoreType.DMA((2,)),
            pltpu.SMEM((2, schedule_size(blocks)), jnp.int32),
            pltpu.VMEM((blocks, 8, QB), jnp.int32),
            pltpu.VMEM((blocks, pairs, PAIR, 2 * QB), BF16),
            pltpu.VMEM((blocks, 8, 2 * QB), F32),
            pltpu.VMEM((blocks, pairs, HD, 2 * QB), F32),
            pltpu.VMEM((2, 8, 2 * QB), F32),
            pltpu.VMEM((2, pairs, KB, 2 * QB), F32),
            pltpu.VMEM((2, pairs, KB, 2 * QB), BF16),
        ],
        compiler_params=pltpu.CompilerParams(vmem_limit_bytes=VMEM_CAP),
        cost_estimate=pl.CostEstimate(
            flops=int(8 * share * rows * rows * feats),
            bytes_accessed=rows * feats * 10,
            transcendentals=int(share * rows * rows),
        ),
        name="attend",
    )(lengths, qt, k, vt, *before)


def attend_back_kernel(
    len_ref, qt_ref, k_hbm, kt_hbm, v_hbm, do_ref, ot_ref, lse_ref, cos_hbm, sin_hbm,
    grad_hbm, grad_t_hbm, grad_ref, grad_t_ref, k_ref, kt_ref, v_ref, cos_ref, sin_ref, load_sem, out_sem, sched, window, q_diag, do_diag, stat, dq_acc, dk_acc, dv_acc,
    score_buf, prob_grad_buf, prob_buf, score_grad_buf,
):
    feats, rows = qt_ref.shape
    pairs = range(feats // PAIR)
    feat = [pl.ds(p * PAIR, PAIR) for p in pairs]
    loads = (
        (k_hbm, k_ref), (kt_hbm, kt_ref), (v_hbm, v_ref), (cos_hbm, cos_ref), (sin_hbm, sin_ref),
    )
    loads = [pltpu.make_async_copy(a, b, load_sem.at[i]) for i, (a, b) in enumerate(loads)]
    for copy in loads:
        copy.start()

    def store(turn):
        cols = pl.ds(pl.multiple_of(turn * QB, QB), QB)
        return [
            pltpu.make_async_copy(grad_ref.at[cols], grad_hbm.at[cols], out_sem.at[0, turn]),
            pltpu.make_async_copy(
                grad_t_ref.at[:, cols], grad_t_hbm.at[:, cols], out_sem.at[1, turn]
            ),
        ]

    dk_acc[...] = jnp.zeros_like(dk_acc)
    dv_acc[...] = jnp.zeros_like(dv_acc)
    dq_acc[...] = jnp.zeros_like(dq_acc)

    def prepare(turn, _):
        cols = pl.ds(pl.multiple_of(turn * QB, QB), QB)
        store_window(len_ref, window, turn, turn * QB)
        for p in pairs:
            do_t = do_ref[cols, feat[p]].T
            delta = do_t.astype(F32) * ot_ref[feat[p], cols].astype(F32)
            delta = [jnp.sum(part, axis=0, keepdims=True) for part in (delta[:HD], delta[HD:])]
            q_diag[turn, p] = block_diagonal_t(qt_ref[feat[p], cols])
            do_diag[turn, p] = block_diagonal_t(do_t)
            stat[turn, p : p + 1] = lse_ref[turn, p : p + 1]
            stat[turn, 4 + p : 5 + p] = jnp.concatenate(delta, axis=1)
        return 0

    lax.fori_loop(0, rows // QB, prepare, 0)
    count = fill_schedule(len_ref, sched, rows // QB, lambda turn: turn, rows)
    for copy in loads:
        copy.wait()

    def scores(n, buf):
        turn, keys = sched[0, n], key_rows(sched[1, n], rows)
        for p in pairs:
            score_buf[buf, p] = mm(k_ref[keys, feat[p]], q_diag[turn, p])
            prob_grad_buf[buf, p] = mm(v_ref[keys, feat[p]], do_diag[turn, p])

    def soften(n, buf):
        turn = sched[0, n]
        inside = inside_window(window[turn, 0:1], window[turn, 1:2], sched[1, n], rows)
        for p in pairs:
            lse, delta = stat[turn, p : p + 1], stat[turn, 4 + p : 5 + p]
            prob = jnp.where(inside, jnp.exp(score_buf[buf, p] - lse), 0.0)
            prob_buf[buf, p] = prob.astype(BF16)
            score_grad_buf[buf, p] = (prob * (prob_grad_buf[buf, p] - delta)).astype(BF16)

    def mix(n, buf):
        turn, keys = sched[0, n], key_rows(sched[1, n], rows)
        for p in pairs:
            dv_acc[feat[p], keys] += mm_nt(do_diag[turn, p], prob_buf[buf, p])
            dk_acc[feat[p], keys] += mm_nt(q_diag[turn, p], score_grad_buf[buf, p])
            dq_acc[turn, p] += diagonal_blocks(mm(kt_ref[feat[p], keys], score_grad_buf[buf, p]))

    prob_buf[1] = jnp.zeros_like(prob_buf[1])
    score_grad_buf[1] = jnp.zeros_like(score_grad_buf[1])
    run_pipeline(count, scores, soften, mix)

    def finish(turn, _):
        cols = pl.ds(pl.multiple_of(turn * QB, QB), QB)
        cosine, sine = cos_ref[:, cols], sin_ref[:, cols]
        for p in pairs:
            dq = jnp.concatenate([dq_acc[turn, p, :, :QB], dq_acc[turn, p, :, QB:]], axis=0) * SCALE
            fields = (
                rotate_t(dq, cosine, sine, -1.0),
                rotate_t(dk_acc[feat[p], cols], cosine, sine, -1.0),
                dv_acc[feat[p], cols],
            )
            for kind, field in enumerate(fields):
                place = pl.ds(kind * feats + p * PAIR, PAIR)
                field = field.astype(BF16)
                grad_t_ref[place, cols] = field
                grad_ref[cols, place] = field.T
        for copy in store(turn):
            copy.start()
        return 0

    lax.fori_loop(0, rows // QB, finish, 0)

    def stored(turn, _):
        for copy in store(turn):
            copy.wait()
        return 0

    lax.fori_loop(0, rows // QB, stored, 0)


def attend_back(lengths, qt, k, kt, v, do, ot, lse, cosine, sine):
    feats, rows = qt.shape
    blocks = rows // QB
    return pl.pallas_call(
        attend_back_kernel,
        in_specs=[SMEM, VMEM] + [ANY] * 3 + [VMEM] * 3 + [ANY] * 2,
        out_specs=[ANY, ANY],
        out_shape=[
            jax.ShapeDtypeStruct((rows, 3 * feats), BF16),
            jax.ShapeDtypeStruct((3 * feats, rows), BF16),
        ],
        scratch_shapes=[
            pltpu.VMEM((rows, 3 * feats), BF16),
            pltpu.VMEM((3 * feats, rows), BF16),
            pltpu.VMEM((rows, feats), BF16),
            pltpu.VMEM((feats, rows), BF16),
            pltpu.VMEM((rows, feats), BF16),
            pltpu.VMEM(cosine.shape, F32),
            pltpu.VMEM(sine.shape, F32),
            pltpu.SemaphoreType.DMA((5,)),
            pltpu.SemaphoreType.DMA((2, blocks)),
            pltpu.SMEM((2, schedule_size(blocks)), jnp.int32),
            pltpu.VMEM((blocks, 8, QB), jnp.int32),
            pltpu.VMEM((blocks, feats // PAIR, PAIR, 2 * QB), BF16),
            pltpu.VMEM((blocks, feats // PAIR, PAIR, 2 * QB), BF16),
            pltpu.VMEM((blocks, 8, 2 * QB), F32),
            pltpu.VMEM((blocks, feats // PAIR, HD, 2 * QB), F32),
            pltpu.VMEM((feats, rows), F32),
            pltpu.VMEM((feats, rows), F32),
        ]
        + [pltpu.VMEM((2, feats // PAIR, KB, 2 * QB), kind) for kind in (F32, F32, BF16, BF16)],
        compiler_params=pltpu.CompilerParams(vmem_limit_bytes=VMEM_CAP),
        cost_estimate=pl.CostEstimate(
            flops=10 * rows * rows * feats, bytes_accessed=rows * feats * 28, transcendentals=rows * rows
        ),
        name="attend_back",
    )(lengths, qt, k, kt, v, do, ot, lse, cosine, sine)


def neighbours():
    me = lax.axis_index("mp")
    one = lax.rem(me, 2)
    across = me + 1 - 2 * one
    along = lax.rem(me + 2, 4)
    return me, across, along, lax.rem(across + 2, 4)


def remote(src, dst, sems, kind, step, device):
    send, recv = sems
    return pltpu.make_async_remote_copy(
        src_ref=src,
        dst_ref=dst,
        send_sem=send.at[kind, step],
        recv_sem=recv.at[kind, step],
        device_id={"mp": device},
        device_id_type=MESH,
    )


def pack_neighbours(packs):
    index = lax.axis_index("dp")
    core, chip = lax.rem(index, 2), index // 2
    chips = packs // 2
    return core, chip, index + 1 - 2 * core, [
        lax.rem(index + 2 * shift, packs) for shift in range(1, chips)
    ]


def chip_across(chip, bits):
    low, high = lax.rem(chip, 2), chip // 2
    low = 1 - low if bits % 2 else low
    high = 1 - high if bits // 2 else high
    return low + 2 * high


def remote_pack(src, dst, send, recv, device):
    return pltpu.make_async_remote_copy(
        src_ref=src, dst_ref=dst, send_sem=send, recv_sem=recv,
        device_id={"dp": device}, device_id_type=MESH,
    )


CHIPS = 4
PILES = (((0, 2), 0), ((1, 3), 0), ((0, 1), 2), ((2, 3), 2))
PARTNERS = (1, 2)


def group_barrier(devices, packs=()):
    barrier = pltpu.get_barrier_semaphore()
    for device in devices:
        pl.semaphore_signal(barrier, inc=1, device_id={"mp": device}, device_id_type=MESH)
    for device in packs:
        pl.semaphore_signal(barrier, inc=1, device_id={"dp": device}, device_id_type=MESH)
    pl.semaphore_wait(barrier, len(devices) + len(packs))


def scatter_first(part, slot, from_x, from_y, sems, kind, step):
    me, x, y, d = neighbours()
    return [
        remote(part.at[slot, x, 0], from_x.at[step, 0], sems, kind, step, x),
        remote(part.at[slot, y, 1], from_y.at[step, 0], sems, kind + 1, step, y),
        remote(part.at[slot, d, 0], from_x.at[step, 1], sems, kind + 2, step, x),
        remote(part.at[slot, d, 1], from_y.at[step, 1], sems, kind + 3, step, y),
    ]


def scatter_second(from_x, from_y, last_x, last_y, sems, kind, step):
    me, x, y, d = neighbours()
    return [
        remote(from_x.at[step, 1], last_y.at[step], sems, kind + 4, step, y),
        remote(from_y.at[step, 1], last_x.at[step], sems, kind + 5, step, x),
    ]


def scatter_middle(part, slot, from_x, from_y, last_x, last_y, sems, kind, step):
    me, x, y, d = neighbours()
    first = scatter_first(part, slot, from_x, from_y, sems, kind, step)
    second = scatter_second(from_x, from_y, last_x, last_y, sems, kind, step)
    first[2].wait_recv()
    total = from_x[step, 1].astype(F32) + part[slot, y, 0].astype(F32)
    from_x[step, 1] = total.astype(BF16)
    second[0].start()
    first[3].wait_recv()
    total = from_y[step, 1].astype(F32) + part[slot, x, 1].astype(F32)
    from_y[step, 1] = total.astype(BF16)
    second[1].start()


def scatter_last(part, slot, from_x, from_y, last_x, last_y, sems, kind, step):
    me, x, y, d = neighbours()
    first = scatter_first(part, slot, from_x, from_y, sems, kind, step)
    second = scatter_second(from_x, from_y, last_x, last_y, sems, kind, step)
    first[0].wait_recv()
    first[1].wait_recv()
    second[0].wait_recv()
    second[1].wait_recv()
    upper = part[slot, me, 0].astype(F32) + from_x[step, 0].astype(F32) + last_y[step].astype(F32)
    lower = part[slot, me, 1].astype(F32) + from_y[step, 0].astype(F32) + last_x[step].astype(F32)
    for copy in first + second:
        copy.wait_send()
    return jnp.concatenate([upper, lower], axis=0)


def ffn_kernel(
    packs,
    len_ref, early0, early1, early2, early3, o_hbm, tok_hbm, cot_hbm, wo0, wo1, wo2, wo3, wg_hbm, wu_hbm, wd_hbm, gain_ref, bias_ref,
    h1_hbm, dh1_hbm, sums_ref, do_hbm, land_hbm, down0_hbm, down1_hbm, down2_hbm, down3_hbm, rows_hbm, *rest,
):
    chips = packs // 2
    piles = rest[: len(PILES)]
    (
        wo, wg, wu, wd, o_all, tok, cot, h1_all, hid, dgate, dup, part, from_x, from_y, last_x, last_y,
        a2_t, eb_t, acc, stage, do_own, db_own, h1_ref, dh1_ref, kept_sem, load_sem, tok_sem, cot_sem, own_sem, early_sem, stage_sem, put_sem, pile_sem,
        core_send, core_recv, send_sem, recv_sem,
    ) = rest[len(PILES) :]
    core, chip, other_core, _ = pack_neighbours(packs)
    steps, owners, block, width = o_all.shape
    share = width // packs
    feats = o_hbm.shape[-1]
    size = owners * block
    tiles = [pl.ds(at, TILE) for at in range(0, width, TILE)]
    early = early0.shape[1]
    some = owners
    sems = (send_sem, recv_sem)
    me, x, y, d = neighbours()
    row_total = owners * steps * block
    live_end = row_total - len_ref[0, len_ref.shape[1] - 1]

    loads = [(wg_hbm, wg), (wu_hbm, wu), (wd_hbm, wd)]
    for source, group in ((wo0, me), (wo1, x), (wo2, y), (wo3, d)):
        loads.append((source, wo.at[pl.ds(pl.multiple_of(group * feats, feats), feats)]))
    loads = [pltpu.make_async_copy(a, b, load_sem.at[i]) for i, (a, b) in enumerate(loads)]

    def fetch(step):
        slot = lax.rem(step, 2)
        return (
            pltpu.make_async_copy(tok_hbm.at[:, step], tok.at[slot], tok_sem.at[slot]),
            pltpu.make_async_copy(cot_hbm.at[:, step], cot.at[slot], cot_sem.at[slot]),
        )

    def lanes(group):
        return pl.ds(pl.multiple_of(group * feats, feats), feats)

    def early_copies(step):
        return [
            pltpu.make_async_copy(
                source.at[:, step], o_all.at[step, :, :, lanes(group)], early_sem.at[step, i]
            )
            for i, (source, group) in enumerate(
                ((early0, me), (early1, x), (early2, y), (early3, d))
            )
            if step < source.shape[1]
        ]

    def own_copy(step):
        return pltpu.make_async_copy(
            o_hbm.at[:, step - early], o_all.at[step, :, :, lanes(me)], own_sem.at[step]
        )

    def gather_own(step):
        source, target = o_hbm.at[:, step - early], o_all.at[step, :, :, lanes(me)]
        return [
            remote(source, target, sems, 0, step, x),
            remote(source, target, sems, 1, step, y),
        ]

    halfway = owners // 2

    def gather_relay(step):
        upper = o_all.at[step, pl.ds(0, halfway), :, lanes(x)]
        lower = o_all.at[step, pl.ds(halfway, halfway), :, lanes(y)]
        return [
            remote(upper, upper, sems, 2, step, y),
            remote(lower, lower, sems, 3, step, x),
        ]

    def relay(step):
        for copy, passed in zip(gather_own(step), gather_relay(step)):
            copy.wait_recv()
            passed.start()

    outgoing = (hid, dgate, dup)

    def to_core(kind):
        source = outgoing[kind] if kind < 3 else stage.at[steps % 2].reshape(size, width)
        return remote_pack(
            source, land_hbm.at[kind], core_send.at[kind], core_recv.at[kind], other_core
        )

    def landed(kind):
        return pltpu.make_async_copy(
            land_hbm.at[kind], tok.at[kind % 2].reshape(size, width), tok_sem.at[kind % 2]
        )

    def pile_copies(kind):
        summed = cot.at[kind % 2].reshape(size, width)
        return [
            pltpu.make_async_copy(
                summed.at[pl.ds(pl.multiple_of(chip_across(chip, bits) * share, share), share)],
                pile.at[i, kind - first],
                pile_sem.at[kind % 2, bits],
            )
            for pile, (places, first) in zip(piles, PILES)
            for i, bits in enumerate(places)
            if first <= kind < first + 2
        ]

    def sum_kind(kind):
        landed(kind).wait()
        if kind >= 2:
            for copy in pile_copies(kind - 2):
                copy.wait()
        theirs = tok[kind % 2].reshape(size, width)
        if kind < 3:
            mine = [
                acc[kind, pl.ds(pl.multiple_of((2 * z + core) * share, share), share), :]
                for z in range(chips)
            ]
            mine = jnp.concatenate(mine, axis=0)
        else:
            mine = h1_all[...].reshape(size, width)
        total = (mine + theirs.astype(F32)).astype(BF16)
        cot[kind % 2] = total.reshape(owners, block, width)
        for copy in pile_copies(kind):
            copy.start()

    def put_rows():
        slot = (steps - 1) % 2
        return [
            remote(stage.at[slot, target], rows_hbm.at[i], sems, 13 + i, 0, target)
            for i, target in enumerate((x, y))
        ]

    def put_do(step):
        return [
            remote(do_own.at[step, target], do_hbm.at[me, step], sems, 10 + i, step, target)
            for i, target in enumerate((x, y, d))
        ]

    def keep_rows(step):
        return [
            pltpu.make_async_copy(source.at[step], out.at[step], kept_sem.at[i, step])
            for i, (source, out) in enumerate(((h1_ref, h1_hbm), (dh1_ref, dh1_hbm)))
        ]

    def keep_do(step):
        return pltpu.make_async_copy(do_own.at[step, me], do_hbm.at[me, step], put_sem.at[step])

    for copy in fetch(0):
        copy.start()
    for copy in loads:
        copy.start()
    for step in range(early):
        for copy in early_copies(step):
            copy.start()
    group_barrier((x, y, d), (other_core,))

    def begin(step, _):
        for copy in gather_own(step):
            copy.start()
        own_copy(step).start()
        return 0

    lax.fori_loop(early, steps, begin, 0)
    acc[...] = jnp.zeros_like(acc)
    sums_ref[...] = jnp.zeros_like(sums_ref)
    for copy in loads:
        copy.wait()

    def step_body(step, _):
        slot = lax.rem(step, 2)
        now, before, older = [lax.rem(step + lag, 3) for lag in (0, 2, 1)]

        @pl.when(step + 1 < steps)
        def _():
            for copy in fetch(step + 1):
                copy.start()

        @pl.when((step + 1 < steps) & (step + 1 >= early))
        def _():
            relay(step + 1)

        for which in range(early):

            @pl.when(step == which)
            def _():
                if which == 0:
                    for copy in early_copies(0):
                        copy.wait()
                    for after in range(1, early):
                        for copy in early_copies(after):
                            copy.wait()
                        for copy in gather_relay(after):
                            copy.start()
                else:
                    for copy in gather_relay(which):
                        copy.wait_recv()

        @pl.when((step < steps) & (step >= early))
        def _():
            for copy in gather_relay(step):
                copy.wait_recv()
            own_copy(step).wait()

        @pl.when(step < steps)
        def _():
            for copy in fetch(step):
                copy.wait()
            def some_rows(turn, _):
                count = some * block
                who = pl.ds(turn * some, some)
                rows = pl.ds(pl.multiple_of(turn * count, count), count)
                position = lax.broadcasted_iota(jnp.int32, (some, block, 1), 1) + step * block
                position = position + (steps * block) * (
                    lax.broadcasted_iota(jnp.int32, (some, block, 1), 0) + turn * some
                )
                eb = jnp.where(position < live_end, cot[slot, who].astype(F32), 0.0).astype(BF16)
                cot[slot, who] = eb
                eb = eb.reshape(count, width)
                mixed = o_all[step, who].reshape(count, width)
                for cols in tiles:
                    h1 = tok[slot, who, :, cols].reshape(count, TILE).astype(F32)
                    h1 = h1 + mm(mixed, wo[:, cols])
                    h1_all[who, :, cols] = h1.reshape(some, block, TILE)
                hat, _ = norm_rows(h1_all[who].reshape(count, width))
                a2 = (hat * gain_ref[...] + bias_ref[...]).astype(BF16)

                def products(cols):
                    return mm(a2, wg[:, cols]), mm(a2, wu[:, cols]), mm_nt(eb, wd[cols, :])

                def hidden(cols, gate, up, back):
                    sig = 0.5 * jnp.tanh(0.5 * gate) + 0.5
                    act = gate * sig
                    hid[rows, cols] = (act * up).astype(BF16)
                    dgate[rows, cols] = (back * up * (sig + act * (1.0 - sig))).astype(BF16)
                    dup[rows, cols] = (back * act).astype(BF16)

                ready = products(tiles[0])
                a2_t[:, rows] = a2.T
                eb_t[:, rows] = eb.T
                for cols, ahead in zip(tiles, tiles[1:] + [None]):
                    coming = products(ahead) if ahead is not None else None
                    hidden(cols, *ready)
                    ready = coming
                for cols in tiles:
                    dc = mm_nt(dgate[rows, :], wg[cols, :]) + mm_nt(dup[rows, :], wu[cols, :])
                    part[now, who, :, :, cols] = dc.astype(BF16).reshape(some, 2, block // 2, TILE)
                return 0

            lax.fori_loop(0, owners // some, some_rows, 0)
            h1_ref[step] = h1_all[me]
            dh1_ref[step] = cot[slot, me].astype(F32)
            for copy in scatter_first(part, now, from_x, from_y, sems, 4, step):
                copy.start()

        @pl.when(step == steps)
        def _():
            for kind in range(3):
                for z in range(chips):
                    rows = pl.ds(pl.multiple_of((2 * z + 1 - core) * share, share), share)
                    outgoing[kind][z * share : (z + 1) * share, :] = acc[kind, rows, :].astype(BF16)
                to_core(kind).start()

        @pl.when((step >= 1) & (step <= steps))
        def _():
            scatter_middle(
                part, before, from_x, from_y, last_x, last_y, sems, 4, step - 1
            )

        @pl.when(step == steps)
        def _():
            for kind in range(2):
                to_core(kind).wait_recv()
                landed(kind).start()
            sum_kind(0)
            to_core(2).wait_recv()
            landed(2).start()
            sum_kind(1)
            sum_kind(2)

        def stage_copies(at, final):
            slot = lax.rem(at, 2)
            places = [(me, down0_hbm), (d, down3_hbm)]
            if not final:
                places += [(x, down1_hbm), (y, down2_hbm)]
            return [
                pltpu.make_async_copy(stage.at[slot, who], out.at[at], stage_sem.at[i, slot])
                for i, (who, out) in enumerate(places)
            ]

        @pl.when(step < steps)
        def _():
            @pl.when(step >= 2)
            def _():
                for copy in stage_copies(step - 2, False):
                    copy.wait()

            def some_output(turn, _):
                count = some * block
                who = pl.ds(turn * some, some)
                rows = pl.ds(pl.multiple_of(turn * count, count), count)
                for cols in tiles:
                    partial = mm(hid[rows, :], wd[:, cols]).astype(BF16)
                    stage[slot, who, :, cols] = partial.reshape(some, block, TILE)
                return 0

            lax.fori_loop(0, owners // some, some_output, 0)

            @pl.when(step < steps - 1)
            def _():
                for copy in stage_copies(step, False):
                    copy.start()

            @pl.when(step == steps - 1)
            def _():
                for copy in stage_copies(step, True):
                    copy.start()

            def some_grads(turn, _):
                rows = pl.ds(pl.multiple_of(turn * size, size), size)
                for cols in tiles:
                    acc[0, rows, cols] += mm(a2_t[rows, :], dgate[:, cols])
                    acc[1, rows, cols] += mm(a2_t[rows, :], dup[:, cols])
                    acc[2, rows, cols] += mm(eb_t[rows, :], hid[:, cols])
                return 0

            lax.fori_loop(0, width // size, some_grads, 0)

        @pl.when(step == steps)
        def _():
            for copy in stage_copies(steps - 2, False) + stage_copies(steps - 1, True):
                copy.wait()

        @pl.when(step >= 2)
        def _():
            prev = step - 2
            dc = scatter_last(part, older, from_x, from_y, last_x, last_y, sems, 4, prev)
            hat, scale = norm_rows(h1_ref[prev])
            sums_ref[0:1] += jnp.sum(dc * hat, axis=0, keepdims=True)
            sums_ref[1:2] += jnp.sum(dc, axis=0, keepdims=True)
            inner = dc * gain_ref[...]
            inner = inner - jnp.mean(inner, axis=-1, keepdims=True) - hat * jnp.mean(
                inner * hat, axis=-1, keepdims=True
            )
            dh1 = dh1_ref[prev] + scale * inner
            dh1_ref[prev] = dh1
            for copy in keep_rows(prev):
                copy.start()
            db = dh1.astype(BF16)
            db_own[prev] = db
            back = mm_nt(db, wo[...]).astype(BF16)
            for group in range(owners):
                do_own[prev, group] = back[:, group * feats : (group + 1) * feats]
            for copy in put_do(prev):
                copy.start()
            keep_do(prev).start()

        @pl.when(step == steps)
        def _():
            for copy in put_rows():
                copy.start()

        return 0

    lax.fori_loop(0, steps + 2, step_body, 0)

    o_mine = jnp.concatenate([o_all[step, me] for step in range(steps)], axis=0)
    for turn, which in enumerate((1 - core, core)):
        columns = [
            db_own[:, :, pl.ds(pl.multiple_of((2 * z + which) * share, share), share)].reshape(
                steps * block, share
            )
            for z in range(chips)
        ]
        values = mm_tn(jnp.concatenate(columns, axis=1), o_mine)
        if turn == 0:
            stage[steps % 2] = values.astype(BF16).reshape(owners, block, width)
            to_core(3).start()
        else:
            h1_all[...] = values.reshape(owners, block, width)

    to_core(3).wait_recv()
    landed(3).start()
    sum_kind(3)
    for kind in range(4):
        to_core(kind).wait_send()
    for copy in pile_copies(2) + pile_copies(3):
        copy.wait()

    for step in range(1, early):
        for copy in gather_relay(step):
            copy.wait_send()

    def sent(step, _):
        for copy in gather_own(step) + gather_relay(step):
            copy.wait_send()
        return 0

    lax.fori_loop(early, steps, sent, 0)

    for copy in put_rows():
        copy.wait()

    def finish(step, _):
        for copy in put_do(step) + keep_rows(step):
            copy.wait()
        keep_do(step).wait()
        return 0

    lax.fori_loop(0, steps, finish, 0)


def ffn(lengths, early, o, tokens, cotangent, wo, wg, wu, wd, gain, bias, steps, packs):
    rows, width = tokens.shape
    feats = o.shape[-1]
    owners = width // feats
    block = rows // (owners * steps)
    hidden = wg.shape[1]
    size = owners * block
    chips = packs // 2
    by_owner = lambda a: a.reshape(owners, steps, block, a.shape[1])
    own = jax.ShapeDtypeStruct((steps, block, width), F32)
    half = (steps, 2, block // 2, width)
    dma = pltpu.SemaphoreType.DMA
    flops = 2 * rows * width * (width + 9 * hidden)
    h1, dh1, sums, do, _, *rest = pl.pallas_call(
        functools.partial(ffn_kernel, packs),
        in_specs=[SMEM] + [ANY] * 14 + [VMEM, VMEM],
        out_specs=[ANY, ANY, VMEM] + [ANY] * (7 + len(PILES)),
        out_shape=[
            own,
            own,
            jax.ShapeDtypeStruct((2, width), F32),
            jax.ShapeDtypeStruct((owners, steps, block, feats), BF16),
            jax.ShapeDtypeStruct((4, size, width), BF16),
        ]
        + [
            jax.ShapeDtypeStruct((taken, block, width), BF16)
            for taken in (steps, steps - 1, steps - 1, steps, 2)
        ]
        + [jax.ShapeDtypeStruct((2, 2, width // packs, width), BF16)] * len(PILES),
        scratch_shapes=[
            pltpu.VMEM((width, width), BF16),
            pltpu.VMEM((width, hidden), BF16),
            pltpu.VMEM((width, hidden), BF16),
            pltpu.VMEM((hidden, width), BF16),
            pltpu.VMEM((steps, owners, block, width), BF16),
            pltpu.VMEM((2, owners, block, width), BF16),
            pltpu.VMEM((2, owners, block, width), BF16),
            pltpu.VMEM((owners, block, width), F32),
            pltpu.VMEM((size, hidden), BF16),
            pltpu.VMEM((size, hidden), BF16),
            pltpu.VMEM((size, hidden), BF16),
            pltpu.VMEM((3, owners, 2, block // 2, width), BF16),
            pltpu.VMEM(half, BF16),
            pltpu.VMEM(half, BF16),
            pltpu.VMEM((steps, block // 2, width), BF16),
            pltpu.VMEM((steps, block // 2, width), BF16),
            pltpu.VMEM((width, size), BF16),
            pltpu.VMEM((width, size), BF16),
            pltpu.VMEM((3, width, hidden), F32),
            pltpu.VMEM((2, owners, block, width), BF16),
            pltpu.VMEM((steps, owners, block, feats), BF16),
            pltpu.VMEM((steps, block, width), BF16),
            pltpu.VMEM(own.shape, F32),
            pltpu.VMEM(own.shape, F32),
            dma((2, steps)),
            dma((7,)),
            dma((2,)),
            dma((2,)),
            dma((steps,)),
            dma((early[0].shape[1], 4)),
            dma((4, 2)),
            dma((steps,)),
            dma((2, chips)),
            dma((4,)),
            dma((4,)),
            dma((15, steps)),
            dma((15, steps)),
        ],
        compiler_params=pltpu.CompilerParams(
            collective_id=0, has_side_effects=True, vmem_limit_bytes=VMEM_CAP
        ),
        cost_estimate=pl.CostEstimate(flops=flops, bytes_accessed=rows * width * 14, transcendentals=0),
        name="ffn",
    )(lengths, *early, o, by_owner(tokens), by_owner(cotangent), *wo, wg, wu, wd, gain, bias)
    return h1, dh1, sums, do.reshape(rows, feats), rest[:5], rest[5:]


def last_kernel(
    packs,
    grad_hbm, grad_t_hbm, a1_hbm, tok_hbm, dh1_hbm, h1_hbm, wq_hbm, wk_hbm, wv_hbm, gain_ref, sums2_ref, *rest,
):
    chips = packs // 2
    downs, rest = rest[:5], rest[5:]
    piles, rest = rest[: len(PILES)], rest[len(PILES) :]
    (
        out_hbm, tg_hbm, gq_hbm, gk_hbm, gv_hbm, gate_hbm, up_hbm, down_hbm, proj_hbm, norm_ref,
        out_ref, tg_ref, gq_ref, gk_ref, gv_ref, gate_ref, up_ref, down_ref, proj_ref, row_sem, result_sem,
        dh1_ref, wq_ref, wk_ref, wv_ref, weight_sem,
        grad, grad_t, a1, tok, part, from_x, from_y, last_x, last_y, h1, down, pile, pile_out, pile_in, sums1,
        full, core_out, core_in, chip_out, chip_in, proj_out, proj_in, norm_out, norm_in,
        grad_sem, tok_sem, load_sem, core_send, core_recv, chip_send, chip_recv, pile_send, pile_recv,
        small_send, small_recv, send_sem, recv_sem,
    ) = rest
    steps, owners, _, half, width = part.shape
    feats = wq_hbm.shape[1]
    size = owners * 2 * half
    share = width // packs
    tall = 3 * feats
    sems = (send_sem, recv_sem)
    me, x, y, d = neighbours()
    core, chip, other_core, next_chips = pack_neighbours(packs)

    def fetch(step):
        return [
            pltpu.make_async_copy(grad_hbm.at[:, step], grad.at[step], grad_sem.at[step]),
            pltpu.make_async_copy(tok_hbm.at[:, step], tok.at[step], tok_sem.at[step]),
        ]

    later = [(grad_t_hbm, grad_t), (a1_hbm, a1)]
    later += [(piles[i], pile.at[i]) for i in range(len(PILES))]
    later += [(h1_hbm, h1)]
    later += [(downs[i], down.at[i, pl.ds(0, downs[i].shape[0])]) for i in range(4)]
    later += [(downs[4], down.at[pl.ds(1, 2), steps - 1])]
    later = [pltpu.make_async_copy(a, b, load_sem.at[i]) for i, (a, b) in enumerate(later)]

    def to_core():
        return remote_pack(core_out, core_in, core_send, core_recv, other_core)

    def to_chips():
        return [
            remote_pack(
                chip_out.at[lax.rem(chip + i + 1, chips)], chip_in.at[i],
                chip_send.at[i], chip_recv.at[i], device,
            )
            for i, device in enumerate(next_chips)
        ]

    def pile_copies():
        index = lax.axis_index("dp")
        return [
            remote_pack(
                pile_out.at[i], pile_in.at[i], pile_send.at[i], pile_recv.at[i],
                index + 2 * (chip_across(chip, bits) - chip),
            )
            for i, bits in enumerate(reversed(PARTNERS))
        ]

    def small(kind, source, target):
        return [
            remote(source(device), target.at[i], (small_send, small_recv), kind, i, device)
            for i, device in enumerate((x, y, d))
        ]

    def proj_copies():
        return small(0, lambda device: proj_out.at[device], proj_in)

    def norm_copies():
        return small(1, lambda device: norm_out, norm_in)

    def begin(step, _):
        for copy in fetch(step):
            copy.start()
        return 0

    weights = ((wq_hbm, wq_ref), (wk_hbm, wk_ref), (wv_hbm, wv_ref), (dh1_hbm, dh1_ref))
    weights = [pltpu.make_async_copy(a, b, weight_sem.at[i]) for i, (a, b) in enumerate(weights)]
    for copy in weights[:3]:
        copy.start()
    lax.fori_loop(0, steps, begin, 0)
    for copy in later + weights[3:]:
        copy.start()
    group_barrier((x, y, d), [other_core] + next_chips)
    sums1[...] = jnp.zeros_like(sums1)

    for copy in weights[:3]:
        copy.wait()

    def first(step, _):
        for copy in fetch(step):
            copy.wait()
        rows = grad[step].reshape(size, tall)
        da = mm_nt(rows[:, :feats], wq_ref[...])
        da = da + mm_nt(rows[:, feats : 2 * feats], wk_ref[...])
        da = da + mm_nt(rows[:, 2 * feats :], wv_ref[...])
        part[step] = da.astype(BF16).reshape(owners, 2, half, width)
        for copy in scatter_first(part, step, from_x, from_y, sems, 0, step):
            copy.start()

        @pl.when(step == 0)
        def _():
            for copy in later[2 : 2 + len(PILES)]:
                copy.wait()
            for i in range(2):
                total = pile[2 * i, 1].astype(F32) + pile[2 * i + 1, 1].astype(F32)
                pile_out[i] = total.astype(BF16)
            for copy in pile_copies():
                copy.start()

        hat, _ = norm_rows(tok[step].reshape(size, width).astype(F32))
        sums1[0:1] += jnp.sum(da * hat, axis=0, keepdims=True)
        sums1[1:2] += jnp.sum(da, axis=0, keepdims=True)
        return 0

    lax.fori_loop(0, steps, first, 0)
    later[0].wait()
    later[1].wait()
    for kind in range(3):
        rows = pl.ds(kind * feats, feats)
        full[rows, :] = mm(grad_t[rows, :], a1[...])
    full[pl.ds(tall, 16), :] = jnp.concatenate(
        [sums1[...], sums2_ref[...], jnp.zeros((12, width), F32)], axis=0
    )
    for z in range(chips):
        columns = pl.ds(pl.multiple_of((2 * z + 1 - core) * share, share), share)
        core_out[z] = full[:, columns].astype(BF16)
    to_core().start()

    to_core().wait_recv()
    for z in range(chips):
        columns = pl.ds(pl.multiple_of((2 * z + core) * share, share), share)
        chip_out[z] = (full[:, columns] + core_in[z].astype(F32)).astype(BF16)
    for copy in to_chips():
        copy.start()
    for copy in later[2 + len(PILES) :]:
        copy.wait()

    def sum_piles():
        for copy in pile_copies():
            copy.wait_recv()
        for kind in range(4):
            half, at = kind // 2, kind % 2
            total = pile[2 * half, 0, at].astype(F32) + pile[2 * half + 1, 0, at].astype(F32)
            total = total + pile_in[half, at].astype(F32)
            if kind < 2:
                (gate_ref, up_ref)[kind][...] = total
            elif kind == 2:
                down_ref[...] = total.T
            else:
                for group in range(owners):
                    proj_out[group] = total[:, group * feats : (group + 1) * feats].astype(BF16)
                for copy in proj_copies():
                    copy.start()

    def row_copies(step):
        return [
            pltpu.make_async_copy(source.at[step], out.at[step], row_sem.at[i, step])
            for i, (source, out) in enumerate(((out_ref, out_hbm), (tg_ref, tg_hbm)))
        ]

    results = (
        (gq_ref, gq_hbm), (gk_ref, gk_hbm), (gv_ref, gv_hbm), (gate_ref, gate_hbm),
        (up_ref, up_hbm), (down_ref, down_hbm), (proj_ref, proj_hbm),
    )
    results = [
        pltpu.make_async_copy(source, out, result_sem.at[i])
        for i, (source, out) in enumerate(results)
    ]

    def finish(step):
        da = scatter_last(part, step, from_x, from_y, last_x, last_y, sems, 0, step)
        hat, scale = norm_rows(tok[step, me].astype(F32))
        inner = da * gain_ref[...]
        inner = inner - jnp.mean(inner, axis=-1, keepdims=True) - hat * jnp.mean(
            inner * hat, axis=-1, keepdims=True
        )
        tg_ref[step] = (dh1_ref[step] + scale * inner).astype(BF16)
        row_copies(step)[1].start()

    def second(step, _):
        scatter_middle(part, step, from_x, from_y, last_x, last_y, sems, 0, step)
        total = h1[step]
        for i in range(4):
            total = total + down[i, step].astype(F32)
        out_ref[step] = total.astype(BF16)
        row_copies(step)[0].start()
        return 0

    def third(step, _):
        finish(step)
        return 0

    weights[3].wait()
    lax.fori_loop(0, steps, second, 0)
    sum_piles()
    for copy in results[3:6]:
        copy.start()
    lax.fori_loop(0, steps - 2, third, 0)
    total = chip_out[chip].astype(F32)
    for i, copy in enumerate(to_chips()):
        copy.wait_recv()
        total = total + chip_in[i].astype(F32)
    norm_out[...] = total[tall : tall + 8]
    for copy in norm_copies():
        copy.start()
    finish(steps - 2)
    for kind, ref in enumerate((gq_ref, gk_ref, gv_ref)):
        ref[...] = total[kind * feats : (kind + 1) * feats].T
        results[kind].start()
    total = proj_out[me].astype(F32)
    for i, copy in enumerate(proj_copies()):
        copy.wait_recv()
        total = total + proj_in[i].astype(F32)
    proj_ref[...] = total.T
    results[6].start()
    finish(steps - 1)
    total = norm_out[...]
    for i, copy in enumerate(norm_copies()):
        copy.wait_recv()
        total = total + norm_in[i]
    norm_ref[...] = total
    for copy in results:
        copy.wait()
    for step in range(steps):
        for copy in row_copies(step):
            copy.wait()
    for copy in [to_core()] + to_chips() + pile_copies() + proj_copies() + norm_copies():
        copy.wait_send()


def last(grads, grads_t, a1, tokens, dh1, h1, wq, wk, wv, gain, sums2, downs, piles, packs):
    rows, width = tokens.shape
    steps, block, _ = dh1.shape
    owners = rows // (steps * block)
    feats = wq.shape[1]
    hidden = piles[0].shape[-1]
    chips = packs // 2
    share = width // packs
    tall = 3 * feats + 16
    by_owner = lambda a: a.reshape(owners, steps, block, a.shape[1])
    half = (steps, 2, block // 2, width)
    dma = pltpu.SemaphoreType.DMA
    own = jax.ShapeDtypeStruct((steps, block, width), BF16)
    f32 = lambda *shape: jax.ShapeDtypeStruct(shape, F32)
    out_shape = [own, own] + [f32(share, feats)] * 3
    out_shape += [f32(share, hidden)] * 2 + [f32(hidden, share), f32(feats, share), f32(8, share)]
    return pl.pallas_call(
        functools.partial(last_kernel, packs),
        in_specs=[ANY] * 9 + [VMEM] * 2 + [ANY] * (5 + len(piles)),
        out_specs=[ANY] * 9 + [VMEM],
        out_shape=out_shape,
        scratch_shapes=[pltpu.VMEM(a.shape, a.dtype) for a in out_shape[:9]]
        + [
            dma((2, steps)),
            dma((7,)),
            pltpu.VMEM((steps, block, width), F32),
            pltpu.VMEM((width, feats), BF16),
            pltpu.VMEM((width, feats), BF16),
            pltpu.VMEM((width, feats), BF16),
            dma((4,)),
            pltpu.VMEM((steps, owners, block, 3 * feats), BF16),
            pltpu.VMEM((3 * feats, rows), BF16),
            pltpu.VMEM((rows, width), BF16),
            pltpu.VMEM((steps, owners, block, width), BF16),
            pltpu.VMEM((steps, owners, 2, block // 2, width), BF16),
            pltpu.VMEM(half, BF16),
            pltpu.VMEM(half, BF16),
            pltpu.VMEM((steps, block // 2, width), BF16),
            pltpu.VMEM((steps, block // 2, width), BF16),
            pltpu.VMEM((steps, block, width), F32),
            pltpu.VMEM((4, steps, block, width), BF16),
            pltpu.VMEM((len(PILES), 2, 2, share, hidden), BF16),
            pltpu.VMEM((2, 2, share, hidden), BF16),
            pltpu.VMEM((2, 2, share, hidden), BF16),
            pltpu.VMEM((2, width), F32),
            pltpu.VMEM((tall, width), F32),
            pltpu.VMEM((chips, tall, share), BF16),
            pltpu.VMEM((chips, tall, share), BF16),
            pltpu.VMEM((chips, tall, share), BF16),
            pltpu.VMEM((chips - 1, tall, share), BF16),
            pltpu.VMEM((owners, share, feats), BF16),
            pltpu.VMEM((owners - 1, share, feats), BF16),
            pltpu.VMEM((8, share), F32),
            pltpu.VMEM((owners - 1, 8, share), F32),
            dma((steps,)),
            dma((steps,)),
            dma((8 + len(piles),)),
            dma,
            dma,
            dma((chips - 1,)),
            dma((chips - 1,)),
            dma((2,)),
            dma((2,)),
            dma((2, owners - 1)),
            dma((2, owners - 1)),
            dma((6, steps)),
            dma((6, steps)),
        ],
        compiler_params=pltpu.CompilerParams(
            collective_id=1, has_side_effects=True, vmem_limit_bytes=VMEM_CAP
        ),
        cost_estimate=pl.CostEstimate(
            flops=12 * rows * width * feats, bytes_accessed=rows * width * 20, transcendentals=0
        ),
        name="last",
    )(
        by_owner(grads), grads_t, a1, by_owner(tokens), dh1, h1, wq, wk, wv, gain, sums2, *downs, *piles
    )


def hand_out_kernel(count, *refs):
    sources, outs, held = refs[: count + 1], refs[count + 1 : 2 * count + 5], refs[2 * count + 5 : -2]
    in_sem, out_sem = refs[-2:]
    norm, vectors = held[count], held[count + 1 :]
    loads = [pltpu.make_async_copy(sources[i], held[i], in_sem.at[i]) for i in range(count + 1)]
    ready = list(held[:count]) + list(vectors)
    stores = [
        pltpu.make_async_copy(ready[i], outs[i], out_sem.at[i]) for i in range(count + 4)
    ]
    for copy in reversed(loads):
        copy.start()
    loads[count].wait()
    for i, vector in enumerate(vectors):
        vector[...] = norm[i]
        stores[count + i].start()
    for load, store in zip(loads[:count], stores):
        load.wait()
        store.start()
    for store in stores:
        store.wait()


def hand_out(arrays, norms):
    count = len(arrays)
    shape = lambda a: jax.ShapeDtypeStruct(a.shape, a.dtype)
    vectors = [jax.ShapeDtypeStruct(norms.shape[1:], F32)] * 4
    out_shape = [shape(a) for a in arrays] + vectors
    return pl.pallas_call(
        functools.partial(hand_out_kernel, count),
        in_specs=[ANY] * (count + 1),
        out_specs=[ANY] * (count + 4),
        out_shape=out_shape,
        scratch_shapes=[pltpu.VMEM(a.shape, a.dtype) for a in list(arrays) + [norms] + vectors]
        + [pltpu.SemaphoreType.DMA((count + 4,))] * 2,
        compiler_params=pltpu.CompilerParams(vmem_limit_bytes=VMEM_CAP),
        name="hand_out",
    )(*arrays, norms)


def local_square(
    tokens, lengths, cotangent, norm1_gain, norm1_bias, w_query, w_key, w_value, w_output,
    norm2_gain, norm2_bias, w_gate, w_up, w_down,
):
    rows, width = tokens.shape
    groups = lax.axis_size("mp")
    packs = lax.axis_size("dp")
    gain1, bias1 = norm1_gain[None, :], norm1_bias[None, :]
    exchange = lambda a, shift: lax.ppermute(a, "mp", [(i, i ^ shift) for i in range(groups)])
    w_outputs = [w_output] + [exchange(w_output, shift) for shift in range(1, groups)]
    a1, k, v, qt, kt, vt, cosine, sine = project(
        lengths, tokens, gain1, bias1, w_query, w_key, w_value
    )
    early, early_first, mixed_t, lse = attend(lengths, qt, k, vt, 0, EARLY, STEPS)
    early = [early, exchange(early, 1), exchange(early, 2), exchange(early_first, 3)]
    qt_late, *w_outputs = lax.optimization_barrier((qt, *w_outputs))
    mixed, mixed_t, lse = attend(lengths, qt_late, k, vt, EARLY, STEPS, STEPS, (mixed_t, lse))
    h1, dh1, sums2, mixed_grad, downs, piles = ffn(
        lengths, early, mixed, tokens, cotangent, w_outputs, w_gate, w_up, w_down,
        norm2_gain[None, :], norm2_bias[None, :], STEPS, packs,
    )
    downs[1:4] = [exchange(downs[shift], shift) for shift in range(1, groups)]
    for i, bits in enumerate(PARTNERS):
        perm = [(j, j ^ (2 * bits)) for j in range(packs)]
        piles[2 * i + 1] = lax.ppermute(piles[2 * i + 1], "dp", perm)
    grads, grads_t = attend_back(
        lengths, qt, k, kt, v, mixed_grad, mixed_t, lse, cosine, sine
    )
    *results, norms = last(
        grads, grads_t, a1, tokens, dh1, h1, w_query, w_key, w_value, gain1, sums2, downs, piles, packs
    )
    output, tokens_grad, grad_q, grad_k, grad_v, gate, up, down, proj, *sums = hand_out(
        results, norms
    )
    own_rows = (rows // groups, width)
    return (
        output.reshape(own_rows),
        tokens_grad.reshape(own_rows),
        grad_q,
        grad_k,
        grad_v,
        proj,
        gate,
        up,
        down,
        *sums,
    )


def layer_stats(row_values, gain_vec, bias_vec):
    normed, row_scale = norm_rows(row_values)
    return (normed * gain_vec + bias_vec, normed, row_scale)


def layer_back(gradient, normed, row_scale, gain_vec):
    inner_grad = gradient * gain_vec
    centred_grad = inner_grad - jnp.mean(inner_grad, axis=-1, keepdims=True)
    return row_scale * (
        centred_grad - normed * jnp.mean(inner_grad * normed, axis=-1, keepdims=True)
    )


def scatter_rows(partial, axis, dim=0):
    return lax.psum_scatter(
        partial.astype(BF16), axis, scatter_dimension=dim, tiled=True
    ).astype(F32)


def local(
    tokens, lengths, cotangent, norm1_gain, norm1_bias, w_query, w_key, w_value, w_output,
    norm2_gain, norm2_bias, w_gate, w_up, w_down,
):
    row_count, width = tokens.shape
    feats = w_query.shape[1]
    gain1, bias1 = norm1_gain[None, :], norm1_bias[None, :]
    a1, k, v, qt, kt, vt, cosine, sine = project(
        lengths, tokens, gain1, bias1, w_query, w_key, w_value
    )
    mixed, mixed_t, lse = attend(lengths, qt, k, vt, 0, 1, 1)
    mixed = mixed.reshape(row_count, feats)

    share_rows = row_count // lax.axis_size("mp")
    own_start = lax.axis_index("mp") * share_rows
    own = lambda a: lax.dynamic_slice_in_dim(a, own_start, share_rows, 0)
    live_end = row_count - lengths[0, lengths.shape[1] - 1]
    live = jnp.arange(row_count, dtype=jnp.int32)[:, None] < live_end
    out_grad = jnp.where(live, cotangent, jnp.zeros_like(cotangent))

    attn_rows = scatter_rows(mm(mixed, w_output), "mp")
    residual = own(tokens).astype(F32) + attn_rows
    normed_second, hat_second, scale_second = layer_stats(residual, norm2_gain, norm2_bias)
    inputs_second = lax.all_gather(normed_second.astype(BF16), "mp", axis=0, tiled=True)
    gate_pre = mm(inputs_second, w_gate)
    up_proj = mm(inputs_second, w_up)
    gate_sig = jax.nn.sigmoid(gate_pre)
    gate_act = gate_pre * gate_sig
    hidden = (gate_act * up_proj).astype(BF16)
    output_own = residual + scatter_rows(mm(hidden, w_down), "mp")
    down_w_grad = mm_tn(hidden, out_grad)
    hidden_grad = mm_nt(out_grad, w_down)
    gate_in_grad = (hidden_grad * up_proj * gate_sig * (1.0 + gate_pre * (1.0 - gate_sig))).astype(BF16)
    up_in_grad = (hidden_grad * gate_act).astype(BF16)
    gate_w_grad = mm_tn(inputs_second, gate_in_grad)
    up_w_grad = mm_tn(inputs_second, up_in_grad)
    ffn_sums = (
        scatter_rows(gate_w_grad, "dp"),
        scatter_rows(up_w_grad, "dp"),
        scatter_rows(down_w_grad, "dp", 1),
    )
    second_grad = scatter_rows(mm_nt(gate_in_grad, w_gate) + mm_nt(up_in_grad, w_up), "mp")
    residual_grad = own(out_grad).astype(F32) + layer_back(
        second_grad, hat_second, scale_second, norm2_gain
    )
    attn_grad = lax.all_gather(residual_grad.astype(BF16), "mp", axis=0, tiled=True)
    gain_second_grad = jnp.sum(second_grad * hat_second, axis=0)
    bias_second_grad = jnp.sum(second_grad, axis=0)
    output_w_grad = mm_tn(mixed, attn_grad)
    mixed_grad = mm_nt(attn_grad, w_output).astype(BF16)

    grads, grads_t = attend_back(
        lengths, qt, k, kt, v, mixed_grad, mixed_t, lse, cosine, sine
    )
    w_qkv = jnp.concatenate([w_query, w_key, w_value], axis=1)
    qkv_w_grad = mm(grads_t, a1)
    first_grad = scatter_rows(mm_nt(grads, w_qkv), "mp")
    hat_own, scale_own = norm_rows(own(tokens).astype(F32))
    tokens_grad = (residual_grad + layer_back(first_grad, hat_own, scale_own, norm1_gain)).astype(BF16)
    gain_parts = jnp.stack(
        [
            jnp.sum(first_grad * hat_own, axis=0),
            jnp.sum(first_grad, axis=0),
            gain_second_grad,
            bias_second_grad,
        ]
    )
    gain_parts = scatter_rows(lax.psum(gain_parts, "mp"), "dp", 1)
    attn_sums = scatter_rows(jnp.concatenate([qkv_w_grad, output_w_grad], axis=0), "dp", 1)
    return (
        output_own.astype(BF16),
        tokens_grad,
        attn_sums[:feats].T,
        attn_sums[feats : 2 * feats].T,
        attn_sums[2 * feats : 3 * feats].T,
        attn_sums[3 * feats :],
        ffn_sums[0],
        ffn_sums[1],
        ffn_sums[2],
        gain_parts[0],
        gain_parts[1],
        gain_parts[2],
        gain_parts[3],
    )


def solution(mesh):
    square = mesh.shape["mp"] == 4 and mesh.shape["dp"] == 2 * CHIPS
    rows, weight_in, weight_out = P("dp", None), P(None, "mp"), P("mp", None)
    row_out = P(("dp", "mp"), None)
    return jax.shard_map(
        local_square if square else local,
        mesh=mesh,
        in_specs=(rows, rows, rows, P(), P(), weight_in, weight_in, weight_in, weight_out)
        + (P(), P(), weight_in, weight_in, weight_out),
        out_specs=(row_out, row_out)
        + (P("dp", "mp"),) * 3
        + (P("mp", "dp"), P("dp", "mp"), P("dp", "mp"), P("mp", "dp"))
        + (P("dp"),) * 4,
        check_vma=False,
    )
```

```python
import functools
import math

import jax
import jax.numpy as jnp
import numpy as np
from jax import lax
from jax.experimental import pallas as pl
from jax.experimental.pallas import tpu as pltpu
from jax.sharding import PartitionSpec as P

HD = 64
HALF = HD // 2
PAIR = 2 * HD
QB = 128
KB = 256
EPS = 1e-05
BASE = 10000.0
NEG = -1e30
MOST = 1024
SCALE = HD**-0.5
VMEM = pl.BlockSpec(memory_space=pltpu.VMEM)
SMEM = pl.BlockSpec(memory_space=pltpu.SMEM)
ANY = pl.BlockSpec(memory_space=pl.ANY)
MESH = pl.DeviceIdType.MESH
STEPS = 5
EARLY = 2
TILE = 256
VMEM_CAP = 62 << 20
F32 = jnp.float32
BF16 = jnp.bfloat16


def mm(a, b):
    return jnp.dot(a, b, preferred_element_type=F32)


def mm_nt(a, b):
    return lax.dot_general(a, b, (((1,), (1,)), ((), ())), preferred_element_type=F32)


def mm_tn(a, b):
    return lax.dot_general(a, b, (((0,), (0,)), ((), ())), preferred_element_type=F32)


def window_bounds(len_ref, position):
    entries = len_ref.shape[1]
    start = jnp.zeros_like(position)
    end = jnp.zeros_like(position)
    edge = jnp.int32(0)
    for entry in range(entries):
        size = len_ref[0, entry]
        inside = position >= edge
        start = jnp.where(inside, edge, start)
        edge = edge + size
        end = jnp.where(inside, edge, end)
    return start, end


def norm_rows(rows):
    mean = jnp.mean(rows, axis=-1, keepdims=True)
    centred = rows - mean
    scale = lax.rsqrt(jnp.mean(centred * centred, axis=-1, keepdims=True) + EPS)
    return centred * scale, scale


def rotate_t(field, cosine, sine, direction):
    parts = []
    for head in range(field.shape[0] // HD):
        first = field[head * HD : head * HD + HALF]
        second = field[head * HD + HALF : (head + 1) * HD]
        parts.append(first * cosine - direction * (second * sine))
        parts.append(second * cosine + direction * (first * sine))
    return jnp.concatenate(parts, axis=0)


def qkv_kernel(
    len_ref, tok_ref, gain_ref, bias_ref, freq_ref, wq_ref, wk_ref, wv_ref,
    a1_ref, k_ref, v_ref, qt_ref, kt_ref, vt_ref, cos_ref, sin_ref,
):
    rows = tok_ref.shape[0]
    position = lax.broadcasted_iota(jnp.int32, (1, rows), 1) + pl.program_id(0) * rows
    start, _ = window_bounds(len_ref, position)
    offset = (position - start).astype(F32)
    theta = freq_ref[...] * offset
    cosine, sine = jnp.cos(theta), jnp.sin(theta)
    cos_ref[...] = cosine
    sin_ref[...] = sine
    parts = 2
    part = rows // parts
    spans = [pl.ds(i * part, part) for i in range(parts)]
    inputs = []
    for span in spans:
        hat, _ = norm_rows(tok_ref[span, :].astype(F32))
        a1 = (hat * gain_ref[...] + bias_ref[...]).astype(BF16)
        a1_ref[span, :] = a1
        inputs.append(a1)
    for i, (span, a1) in enumerate(zip(spans, inputs)):
        turn = slice(i * part, (i + 1) * part)
        for w_ref, out_ref, out_t_ref, scale in (
            (wq_ref, None, qt_ref, SCALE),
            (wk_ref, k_ref, kt_ref, None),
        ):
            field = mm(a1, w_ref[...]).T
            field = rotate_t(field, cosine[:, turn], sine[:, turn], 1.0).astype(BF16)
            if scale is not None:
                field = field * jnp.asarray(scale, BF16)
            out_t_ref[:, span] = field
            if out_ref is not None:
                out_ref[span, :] = field.T
        values = mm(a1, wv_ref[...]).astype(BF16)
        v_ref[span, :] = values
        vt_ref[:, span] = values.T


def project(lengths, tokens, gain, bias, wq, wk, wv):
    rows, width = tokens.shape
    feats = wq.shape[1]
    block = min(512, rows)
    freq = np.float32(BASE) ** (np.float32(-2.0 / HD) * np.arange(HALF, dtype=np.float32))
    freq = jnp.asarray(freq[:, None], F32)
    whole = lambda a: pl.BlockSpec(a.shape, lambda i: (0, 0))
    by_row = lambda cols: pl.BlockSpec((block, cols), lambda i: (i, 0))
    by_col = lambda size: pl.BlockSpec((size, block), lambda i: (0, i))
    nat = jax.ShapeDtypeStruct((rows, feats), BF16)
    trans = jax.ShapeDtypeStruct((feats, rows), BF16)
    table = jax.ShapeDtypeStruct((HALF, rows), F32)
    return pl.pallas_call(
        qkv_kernel,
        grid=(rows // block,),
        in_specs=[SMEM, by_row(width)] + [whole(a) for a in (gain, bias, freq, wq, wk, wv)],
        out_specs=[by_row(width)] + [by_row(feats)] * 2 + [by_col(feats)] * 3 + [by_col(HALF)] * 2,
        out_shape=[jax.ShapeDtypeStruct((rows, width), BF16)] + [nat] * 2 + [trans] * 3 + [table] * 2,
        compiler_params=pltpu.CompilerParams(vmem_limit_bytes=VMEM_CAP),
        cost_estimate=pl.CostEstimate(
            flops=6 * rows * width * feats, bytes_accessed=rows * width * 8, transcendentals=0
        ),
        name="qkv",
    )(lengths, tokens, gain, bias, freq, wq, wk, wv)


def block_diagonal_t(pair):
    head = lax.broadcasted_iota(jnp.int32, pair.shape, 0) < HD
    zero = jnp.zeros_like(pair)
    return jnp.concatenate([jnp.where(head, pair, zero), jnp.where(head, zero, pair)], axis=1)


def diagonal_blocks(product):
    return jnp.concatenate([product[:HD, :QB], product[HD:, QB:]], axis=1)


def key_range(len_ref, first):
    low, _ = window_bounds(len_ref, first)
    _, high = window_bounds(len_ref, first + (QB - 1))
    base = low // QB * QB
    return base, (high - base + (KB - 1)) // KB


def key_rows(at, rows):
    return pl.ds(pl.multiple_of(jnp.clip(at, 0, rows - KB), QB), KB)


def inside_window(start, end, at, rows):
    shift = jnp.minimum(at, rows - KB)
    key = lax.broadcasted_iota(jnp.int32, (KB, QB), 0)
    inside = (key >= jnp.maximum(start, at) - shift) & (key < end - shift)
    return jnp.concatenate([inside, inside], axis=1)


def fill_schedule(len_ref, sched, blocks, index_of, rows):
    def nothing(n):
        sched[0, n] = 0
        sched[1, n] = rows

    def one_query(turn, n):
        base, count = key_range(len_ref, index_of(turn) * QB)

        def one_key(kb, _):
            sched[0, n + kb] = turn
            sched[1, n + kb] = base + kb * KB
            return 0

        lax.fori_loop(0, count, one_key, 0)
        return n + count

    nothing(0)
    n = lax.fori_loop(0, blocks, one_query, jnp.int32(1))
    for extra in range(3):
        nothing(n + extra)
    return n - 1


def store_window(len_ref, window, turn, first):
    position = lax.broadcasted_iota(jnp.int32, (1, QB), 1) + first
    window[turn, 0:1], window[turn, 1:2] = window_bounds(len_ref, position)


def run_pipeline(count, pairs, inside, scores, soften, mix):
    def one_turn(n, buf):
        mask = inside(n)
        for p in pairs:
            mix(n - 1, 1 - buf, p)
            scores(n + 1, 1 - buf, p)
            soften(n, buf, p, mask)

    def two_turns(turn, _):
        one_turn(1 + 2 * turn, 0)
        one_turn(2 + 2 * turn, 1)
        return 0

    turns = (count + 1) // 2
    for p in pairs:
        scores(1, 0, p)
    lax.fori_loop(0, turns, two_turns, 0)
    for p in pairs:
        mix(2 * turns, 1, p)


def attend_kernel(begin, steps, len_ref, qt_ref, k_hbm, vt_hbm, *rest):
    if begin > 0:
        ot_before, lse_before, *rest = rest
    o_ref, *rest = rest
    first_ref = None
    if begin == 0 and steps > 1:
        first_ref, *rest = rest
    ot_ref, lse_ref, k_ref, vt_ref, load_sem, *rest = rest
    sched, window, diag, stat, acc, keep_buf, score_buf, prob_buf = rest
    loads = [
        pltpu.make_async_copy(k_hbm, k_ref, load_sem.at[0]),
        pltpu.make_async_copy(vt_hbm, vt_ref, load_sem.at[1]),
    ]
    for copy in loads:
        copy.start()
    if begin > 0:
        ot_ref[...] = ot_before[...]
        lse_ref[...] = lse_before[...]
    owners, taken = o_ref.shape[:2]
    feats, rows = qt_ref.shape
    pairs = range(feats // PAIR)
    feat = [pl.ds(p * PAIR, PAIR) for p in pairs]

    def index_of(turn):
        return turn // taken * steps + begin + lax.rem(turn, taken)

    def prepare(turn, _):
        first = index_of(turn) * QB
        cols = pl.ds(pl.multiple_of(first, QB), QB)
        store_window(len_ref, window, turn, first)
        for p in pairs:
            diag[turn, p] = block_diagonal_t(qt_ref[feat[p], cols])
            stat[turn, p : p + 1] = jnp.full((1, 2 * QB), NEG, F32)
            stat[turn, 4 + p : 5 + p] = jnp.zeros((1, 2 * QB), F32)
            acc[turn, p] = jnp.zeros((HD, 2 * QB), F32)
        return 0

    lax.fori_loop(0, owners * taken, prepare, 0)
    count = fill_schedule(len_ref, sched, owners * taken, index_of, rows)
    for copy in loads:
        copy.wait()

    def inside(n):
        turn = sched[0, n]
        return inside_window(window[turn, 0:1], window[turn, 1:2], sched[1, n], rows)

    def scores(n, buf, p):
        turn, keys = sched[0, n], key_rows(sched[1, n], rows)
        score_buf[buf, p] = mm(k_ref[keys, feat[p]], diag[turn, p])

    def soften(n, buf, p, mask):
        turn = sched[0, n]
        top, total = stat[turn, p : p + 1], stat[turn, 4 + p : 5 + p]
        values = jnp.where(mask, score_buf[buf, p], NEG)
        new_top = jnp.maximum(top, jnp.max(values, axis=0, keepdims=True))
        prob = jnp.exp(values - new_top)
        keep = jnp.exp(top - new_top)
        stat[turn, p : p + 1] = new_top
        stat[turn, 4 + p : 5 + p] = keep * total + jnp.sum(prob, axis=0, keepdims=True)
        keep_buf[buf, p : p + 1] = keep
        prob_buf[buf, p] = prob.astype(BF16)

    def mix(n, buf, p):
        turn, keys = sched[0, n], key_rows(sched[1, n], rows)
        mixed = diagonal_blocks(mm(vt_ref[feat[p], keys], prob_buf[buf, p]))
        acc[turn, p] = acc[turn, p] * keep_buf[buf, p : p + 1] + mixed

    prob_buf[1] = jnp.zeros_like(prob_buf[1])
    keep_buf[1] = jnp.ones_like(keep_buf[1])
    run_pipeline(count, pairs, inside, scores, soften, mix)

    def finish(turn, _):
        index = index_of(turn)
        cols = pl.ds(pl.multiple_of(index * QB, QB), QB)
        for p in pairs:
            top, total = stat[turn, p : p + 1], stat[turn, 4 + p : 5 + p]
            mixed = acc[turn, p] / total
            mixed = jnp.concatenate([mixed[:, :QB], mixed[:, QB:]], axis=0).astype(BF16)
            lse_ref[index, p : p + 1] = top + jnp.log(total)
            ot_ref[feat[p], cols] = mixed
            mixed = mixed.T
            o_ref[turn // taken, lax.rem(turn, taken), :, feat[p]] = mixed
            if first_ref is not None:

                @pl.when(lax.rem(turn, taken) == 0)
                def _():
                    first_ref[turn // taken, 0, :, feat[p]] = mixed

        return 0

    lax.fori_loop(0, owners * taken, finish, 0)


def schedule_size(blocks):
    return blocks * ((2 * MOST + 2 * QB) // KB + 1) + 4


def attend(lengths, qt, k, vt, begin, end, steps, before=()):
    feats, rows = qt.shape
    pairs = feats // PAIR
    owners = rows // (steps * QB)
    share = (end - begin) / steps
    blocks = owners * (end - begin)
    first = []
    if begin == 0 and steps > 1:
        first = [jax.ShapeDtypeStruct((owners, 1, QB, feats), BF16)]
    return pl.pallas_call(
        functools.partial(attend_kernel, begin, steps),
        in_specs=[SMEM, VMEM, ANY, ANY] + [VMEM] * len(before),
        out_specs=[VMEM] * (3 + len(first)),
        out_shape=[jax.ShapeDtypeStruct((owners, end - begin, QB, feats), BF16)]
        + first
        + [
            jax.ShapeDtypeStruct((feats, rows), BF16),
            jax.ShapeDtypeStruct((rows // QB, pairs, 2 * QB), F32),
        ],
        scratch_shapes=[
            pltpu.VMEM((rows, feats), BF16),
            pltpu.VMEM((feats, rows), BF16),
            pltpu.SemaphoreType.DMA((2,)),
            pltpu.SMEM((2, schedule_size(blocks)), jnp.int32),
            pltpu.VMEM((blocks, 8, QB), jnp.int32),
            pltpu.VMEM((blocks, pairs, PAIR, 2 * QB), BF16),
            pltpu.VMEM((blocks, 8, 2 * QB), F32),
            pltpu.VMEM((blocks, pairs, HD, 2 * QB), F32),
            pltpu.VMEM((2, 8, 2 * QB), F32),
            pltpu.VMEM((2, pairs, KB, 2 * QB), F32),
            pltpu.VMEM((2, pairs, KB, 2 * QB), BF16),
        ],
        compiler_params=pltpu.CompilerParams(vmem_limit_bytes=VMEM_CAP),
        cost_estimate=pl.CostEstimate(
            flops=int(8 * share * rows * rows * feats),
            bytes_accessed=rows * feats * 10,
            transcendentals=int(share * rows * rows),
        ),
        name="attend",
    )(lengths, qt, k, vt, *before)


def attend_back_kernel(
    len_ref, qt_ref, k_hbm, kt_hbm, v_hbm, do_ref, ot_ref, lse_ref, cos_hbm, sin_hbm,
    grad_hbm, grad_t_hbm, grad_ref, grad_t_ref, k_ref, kt_ref, v_ref, cos_ref, sin_ref, load_sem, out_sem, sched, window, q_diag, do_diag, stat, dq_acc, dk_acc, dv_acc,
    score_buf, prob_grad_buf, prob_buf, score_grad_buf,
):
    feats, rows = qt_ref.shape
    pairs = range(feats // PAIR)
    feat = [pl.ds(p * PAIR, PAIR) for p in pairs]
    loads = (
        (k_hbm, k_ref), (kt_hbm, kt_ref), (v_hbm, v_ref), (cos_hbm, cos_ref), (sin_hbm, sin_ref),
    )
    loads = [pltpu.make_async_copy(a, b, load_sem.at[i]) for i, (a, b) in enumerate(loads)]
    for copy in loads:
        copy.start()

    def store(turn):
        cols = pl.ds(pl.multiple_of(turn * QB, QB), QB)
        return [
            pltpu.make_async_copy(grad_ref.at[cols], grad_hbm.at[cols], out_sem.at[0, turn]),
            pltpu.make_async_copy(
                grad_t_ref.at[:, cols], grad_t_hbm.at[:, cols], out_sem.at[1, turn]
            ),
        ]

    dk_acc[...] = jnp.zeros_like(dk_acc)
    dv_acc[...] = jnp.zeros_like(dv_acc)
    dq_acc[...] = jnp.zeros_like(dq_acc)

    def prepare(turn, _):
        cols = pl.ds(pl.multiple_of(turn * QB, QB), QB)
        store_window(len_ref, window, turn, turn * QB)
        for p in pairs:
            do_t = do_ref[cols, feat[p]].T
            delta = do_t.astype(F32) * ot_ref[feat[p], cols].astype(F32)
            delta = [jnp.sum(part, axis=0, keepdims=True) for part in (delta[:HD], delta[HD:])]
            q_diag[turn, p] = block_diagonal_t(qt_ref[feat[p], cols])
            do_diag[turn, p] = block_diagonal_t(do_t)
            stat[turn, p : p + 1] = lse_ref[turn, p : p + 1]
            stat[turn, 4 + p : 5 + p] = jnp.concatenate(delta, axis=1)
        return 0

    lax.fori_loop(0, rows // QB, prepare, 0)
    count = fill_schedule(len_ref, sched, rows // QB, lambda turn: turn, rows)
    for copy in loads:
        copy.wait()

    def inside(n):
        turn = sched[0, n]
        return inside_window(window[turn, 0:1], window[turn, 1:2], sched[1, n], rows)

    def scores(n, buf, p):
        turn, keys = sched[0, n], key_rows(sched[1, n], rows)
        score_buf[buf, p] = mm(k_ref[keys, feat[p]], q_diag[turn, p])
        prob_grad_buf[buf, p] = mm(v_ref[keys, feat[p]], do_diag[turn, p])

    def soften(n, buf, p, mask):
        turn = sched[0, n]
        lse, delta = stat[turn, p : p + 1], stat[turn, 4 + p : 5 + p]
        prob = jnp.where(mask, jnp.exp(score_buf[buf, p] - lse), 0.0)
        prob_buf[buf, p] = prob.astype(BF16)
        score_grad_buf[buf, p] = (prob * (prob_grad_buf[buf, p] - delta)).astype(BF16)

    def mix(n, buf, p):
        turn, keys = sched[0, n], key_rows(sched[1, n], rows)
        dv_acc[feat[p], keys] += mm_nt(do_diag[turn, p], prob_buf[buf, p])
        dk_acc[feat[p], keys] += mm_nt(q_diag[turn, p], score_grad_buf[buf, p])
        dq_acc[turn, p] += diagonal_blocks(mm(kt_ref[feat[p], keys], score_grad_buf[buf, p]))

    prob_buf[1] = jnp.zeros_like(prob_buf[1])
    score_grad_buf[1] = jnp.zeros_like(score_grad_buf[1])
    run_pipeline(count, pairs, inside, scores, soften, mix)

    def finish(turn, _):
        cols = pl.ds(pl.multiple_of(turn * QB, QB), QB)
        cosine, sine = cos_ref[:, cols], sin_ref[:, cols]
        for p in pairs:
            dq = jnp.concatenate([dq_acc[turn, p, :, :QB], dq_acc[turn, p, :, QB:]], axis=0) * SCALE
            fields = (
                rotate_t(dq, cosine, sine, -1.0),
                rotate_t(dk_acc[feat[p], cols], cosine, sine, -1.0),
                dv_acc[feat[p], cols],
            )
            for kind, field in enumerate(fields):
                place = pl.ds(kind * feats + p * PAIR, PAIR)
                field = field.astype(BF16)
                grad_t_ref[place, cols] = field
                grad_ref[cols, place] = field.T
        for copy in store(turn):
            copy.start()
        return 0

    lax.fori_loop(0, rows // QB, finish, 0)

    def stored(turn, _):
        for copy in store(turn):
            copy.wait()
        return 0

    lax.fori_loop(0, rows // QB, stored, 0)


def attend_back(lengths, qt, k, kt, v, do, ot, lse, cosine, sine):
    feats, rows = qt.shape
    blocks = rows // QB
    return pl.pallas_call(
        attend_back_kernel,
        in_specs=[SMEM, VMEM] + [ANY] * 3 + [VMEM] * 3 + [ANY] * 2,
        out_specs=[ANY, ANY],
        out_shape=[
            jax.ShapeDtypeStruct((rows, 3 * feats), BF16),
            jax.ShapeDtypeStruct((3 * feats, rows), BF16),
        ],
        scratch_shapes=[
            pltpu.VMEM((rows, 3 * feats), BF16),
            pltpu.VMEM((3 * feats, rows), BF16),
            pltpu.VMEM((rows, feats), BF16),
            pltpu.VMEM((feats, rows), BF16),
            pltpu.VMEM((rows, feats), BF16),
            pltpu.VMEM(cosine.shape, F32),
            pltpu.VMEM(sine.shape, F32),
            pltpu.SemaphoreType.DMA((5,)),
            pltpu.SemaphoreType.DMA((2, blocks)),
            pltpu.SMEM((2, schedule_size(blocks)), jnp.int32),
            pltpu.VMEM((blocks, 8, QB), jnp.int32),
            pltpu.VMEM((blocks, feats // PAIR, PAIR, 2 * QB), BF16),
            pltpu.VMEM((blocks, feats // PAIR, PAIR, 2 * QB), BF16),
            pltpu.VMEM((blocks, 8, 2 * QB), F32),
            pltpu.VMEM((blocks, feats // PAIR, HD, 2 * QB), F32),
            pltpu.VMEM((feats, rows), F32),
            pltpu.VMEM((feats, rows), F32),
        ]
        + [pltpu.VMEM((2, feats // PAIR, KB, 2 * QB), kind) for kind in (F32, F32, BF16, BF16)],
        compiler_params=pltpu.CompilerParams(vmem_limit_bytes=VMEM_CAP),
        cost_estimate=pl.CostEstimate(
            flops=10 * rows * rows * feats, bytes_accessed=rows * feats * 28, transcendentals=rows * rows
        ),
        name="attend_back",
    )(lengths, qt, k, kt, v, do, ot, lse, cosine, sine)


def neighbours():
    me = lax.axis_index("mp")
    one = lax.rem(me, 2)
    across = me + 1 - 2 * one
    along = lax.rem(me + 2, 4)
    return me, across, along, lax.rem(across + 2, 4)


def remote(src, dst, sems, kind, step, device):
    send, recv = sems
    return pltpu.make_async_remote_copy(
        src_ref=src,
        dst_ref=dst,
        send_sem=send.at[kind, step],
        recv_sem=recv.at[kind, step],
        device_id={"mp": device},
        device_id_type=MESH,
    )


def pack_neighbours(packs):
    index = lax.axis_index("dp")
    core, chip = lax.rem(index, 2), index // 2
    chips = packs // 2
    return core, chip, index + 1 - 2 * core, [
        lax.rem(index + 2 * shift, packs) for shift in range(1, chips)
    ]


def chip_across(chip, bits):
    low, high = lax.rem(chip, 2), chip // 2
    low = 1 - low if bits % 2 else low
    high = 1 - high if bits // 2 else high
    return low + 2 * high


def remote_pack(src, dst, send, recv, device):
    return pltpu.make_async_remote_copy(
        src_ref=src, dst_ref=dst, send_sem=send, recv_sem=recv,
        device_id={"dp": device}, device_id_type=MESH,
    )


CHIPS = 4
PILES = (((0, 2), 0), ((1, 3), 0), ((0, 1), 2), ((2, 3), 2))
PARTNERS = (1, 2)


def group_barrier(devices, packs=()):
    barrier = pltpu.get_barrier_semaphore()
    for device in devices:
        pl.semaphore_signal(barrier, inc=1, device_id={"mp": device}, device_id_type=MESH)
    for device in packs:
        pl.semaphore_signal(barrier, inc=1, device_id={"dp": device}, device_id_type=MESH)
    pl.semaphore_wait(barrier, len(devices) + len(packs))


def scatter_first(part, slot, from_x, from_y, sems, kind, step):
    me, x, y, d = neighbours()
    return [
        remote(part.at[slot, x, 0], from_x.at[step, 0], sems, kind, step, x),
        remote(part.at[slot, y, 1], from_y.at[step, 0], sems, kind + 1, step, y),
        remote(part.at[slot, d, 0], from_x.at[step, 1], sems, kind + 2, step, x),
        remote(part.at[slot, d, 1], from_y.at[step, 1], sems, kind + 3, step, y),
    ]


def scatter_second(from_x, from_y, last_x, last_y, sems, kind, step):
    me, x, y, d = neighbours()
    return [
        remote(from_x.at[step, 1], last_y.at[step], sems, kind + 4, step, y),
        remote(from_y.at[step, 1], last_x.at[step], sems, kind + 5, step, x),
    ]


def scatter_middle(part, slot, from_x, from_y, last_x, last_y, sems, kind, step):
    me, x, y, d = neighbours()
    first = scatter_first(part, slot, from_x, from_y, sems, kind, step)
    second = scatter_second(from_x, from_y, last_x, last_y, sems, kind, step)
    first[2].wait_recv()
    total = from_x[step, 1].astype(F32) + part[slot, y, 0].astype(F32)
    from_x[step, 1] = total.astype(BF16)
    second[0].start()
    first[3].wait_recv()
    total = from_y[step, 1].astype(F32) + part[slot, x, 1].astype(F32)
    from_y[step, 1] = total.astype(BF16)
    second[1].start()


def scatter_last(part, slot, from_x, from_y, last_x, last_y, sems, kind, step):
    me, x, y, d = neighbours()
    first = scatter_first(part, slot, from_x, from_y, sems, kind, step)
    second = scatter_second(from_x, from_y, last_x, last_y, sems, kind, step)
    first[0].wait_recv()
    first[1].wait_recv()
    second[0].wait_recv()
    second[1].wait_recv()
    upper = part[slot, me, 0].astype(F32) + from_x[step, 0].astype(F32) + last_y[step].astype(F32)
    lower = part[slot, me, 1].astype(F32) + from_y[step, 0].astype(F32) + last_x[step].astype(F32)
    for copy in first + second:
        copy.wait_send()
    return jnp.concatenate([upper, lower], axis=0)


def ffn_kernel(
    packs,
    len_ref, early0, early1, early2, early3, o_hbm, tok_hbm, cot_hbm, wo0, wo1, wo2, wo3, wg_hbm, wu_hbm, wd_hbm, gain_ref, bias_ref,
    h1_hbm, dh1_hbm, sums_ref, do_hbm, land_hbm, down0_hbm, down1_hbm, down2_hbm, down3_hbm, rows_hbm, *rest,
):
    chips = packs // 2
    piles = rest[: len(PILES)]
    (
        wo, wg, wu, wd, o_all, tok, cot, h1_all, hid, dgate, dup, part, from_x, from_y, last_x, last_y,
        a2_t, eb_t, acc, stage, do_own, db_own, h1_ref, dh1_ref, kept_sem, load_sem, tok_sem, cot_sem, own_sem, early_sem, stage_sem, put_sem, pile_sem,
        core_send, core_recv, send_sem, recv_sem,
    ) = rest[len(PILES) :]
    core, chip, other_core, _ = pack_neighbours(packs)
    steps, owners, block, width = o_all.shape
    share = width // packs
    feats = o_hbm.shape[-1]
    size = owners * block
    tiles = [pl.ds(at, TILE) for at in range(0, width, TILE)]
    early = early0.shape[1]
    some = owners
    sems = (send_sem, recv_sem)
    me, x, y, d = neighbours()
    row_total = owners * steps * block
    live_end = row_total - len_ref[0, len_ref.shape[1] - 1]

    loads = [(wg_hbm, wg), (wu_hbm, wu), (wd_hbm, wd)]
    for source, group in ((wo0, me), (wo1, x), (wo2, y), (wo3, d)):
        loads.append((source, wo.at[pl.ds(pl.multiple_of(group * feats, feats), feats)]))
    loads = [pltpu.make_async_copy(a, b, load_sem.at[i]) for i, (a, b) in enumerate(loads)]

    def fetch(step):
        slot = lax.rem(step, 2)
        return (
            pltpu.make_async_copy(tok_hbm.at[:, step], tok.at[slot], tok_sem.at[slot]),
            pltpu.make_async_copy(cot_hbm.at[:, step], cot.at[slot], cot_sem.at[slot]),
        )

    def lanes(group):
        return pl.ds(pl.multiple_of(group * feats, feats), feats)

    def early_copies(step):
        return [
            pltpu.make_async_copy(
                source.at[:, step], o_all.at[step, :, :, lanes(group)], early_sem.at[step, i]
            )
            for i, (source, group) in enumerate(
                ((early0, me), (early1, x), (early2, y), (early3, d))
            )
            if step < source.shape[1]
        ]

    def own_copy(step):
        return pltpu.make_async_copy(
            o_hbm.at[:, step - early], o_all.at[step, :, :, lanes(me)], own_sem.at[step]
        )

    def gather_own(step):
        source, target = o_hbm.at[:, step - early], o_all.at[step, :, :, lanes(me)]
        return [
            remote(source, target, sems, 0, step, x),
            remote(source, target, sems, 1, step, y),
        ]

    halfway = owners // 2

    def gather_relay(step):
        upper = o_all.at[step, pl.ds(0, halfway), :, lanes(x)]
        lower = o_all.at[step, pl.ds(halfway, halfway), :, lanes(y)]
        return [
            remote(upper, upper, sems, 2, step, y),
            remote(lower, lower, sems, 3, step, x),
        ]

    def relay(step):
        for copy, passed in zip(gather_own(step), gather_relay(step)):
            copy.wait_recv()
            passed.start()

    outgoing = (hid, dgate, dup)

    def to_core(kind):
        source = outgoing[kind] if kind < 3 else stage.at[steps % 2].reshape(size, width)
        return remote_pack(
            source, land_hbm.at[kind], core_send.at[kind], core_recv.at[kind], other_core
        )

    def landed(kind):
        return pltpu.make_async_copy(
            land_hbm.at[kind], tok.at[kind % 2].reshape(size, width), tok_sem.at[kind % 2]
        )

    def pile_copies(kind):
        summed = cot.at[kind % 2].reshape(size, width)
        return [
            pltpu.make_async_copy(
                summed.at[pl.ds(pl.multiple_of(chip_across(chip, bits) * share, share), share)],
                pile.at[i, kind - first],
                pile_sem.at[kind % 2, bits],
            )
            for pile, (places, first) in zip(piles, PILES)
            for i, bits in enumerate(places)
            if first <= kind < first + 2
        ]

    def sum_kind(kind):
        landed(kind).wait()
        if kind >= 2:
            for copy in pile_copies(kind - 2):
                copy.wait()
        theirs = tok[kind % 2].reshape(size, width)
        if kind < 3:
            mine = [
                acc[kind, pl.ds(pl.multiple_of((2 * z + core) * share, share), share), :]
                for z in range(chips)
            ]
            mine = jnp.concatenate(mine, axis=0)
        else:
            mine = h1_all[...].reshape(size, width)
        total = (mine + theirs.astype(F32)).astype(BF16)
        cot[kind % 2] = total.reshape(owners, block, width)
        for copy in pile_copies(kind):
            copy.start()

    def put_rows():
        slot = (steps - 1) % 2
        return [
            remote(stage.at[slot, target], rows_hbm.at[i], sems, 13 + i, 0, target)
            for i, target in enumerate((x, y))
        ]

    def put_do(step):
        return [
            remote(do_own.at[step, target], do_hbm.at[me, step], sems, 10 + i, step, target)
            for i, target in enumerate((x, y, d))
        ]

    def keep_rows(step):
        return [
            pltpu.make_async_copy(source.at[step], out.at[step], kept_sem.at[i, step])
            for i, (source, out) in enumerate(((h1_ref, h1_hbm), (dh1_ref, dh1_hbm)))
        ]

    def keep_do(step):
        return pltpu.make_async_copy(do_own.at[step, me], do_hbm.at[me, step], put_sem.at[step])

    for copy in fetch(0):
        copy.start()
    for copy in loads:
        copy.start()
    for step in range(early):
        for copy in early_copies(step):
            copy.start()
    group_barrier((x, y, d), (other_core,))

    def begin(step, _):
        for copy in gather_own(step):
            copy.start()
        own_copy(step).start()
        return 0

    lax.fori_loop(early, steps, begin, 0)
    acc[...] = jnp.zeros_like(acc)
    sums_ref[...] = jnp.zeros_like(sums_ref)
    for copy in loads:
        copy.wait()

    def step_body(step, _):
        slot = lax.rem(step, 2)
        now, before, older = [lax.rem(step + lag, 3) for lag in (0, 2, 1)]

        @pl.when(step + 1 < steps)
        def _():
            for copy in fetch(step + 1):
                copy.start()

        @pl.when((step + 1 < steps) & (step + 1 >= early))
        def _():
            relay(step + 1)

        for which in range(early):

            @pl.when(step == which)
            def _():
                if which == 0:
                    for copy in early_copies(0):
                        copy.wait()
                    for after in range(1, early):
                        for copy in early_copies(after):
                            copy.wait()
                        for copy in gather_relay(after):
                            copy.start()
                else:
                    for copy in gather_relay(which):
                        copy.wait_recv()

        @pl.when((step < steps) & (step >= early))
        def _():
            for copy in gather_relay(step):
                copy.wait_recv()
            own_copy(step).wait()

        @pl.when(step < steps)
        def _():
            for copy in fetch(step):
                copy.wait()
            def some_rows(turn, _):
                count = some * block
                who = pl.ds(turn * some, some)
                rows = pl.ds(pl.multiple_of(turn * count, count), count)
                position = lax.broadcasted_iota(jnp.int32, (some, block, 1), 1) + step * block
                position = position + (steps * block) * (
                    lax.broadcasted_iota(jnp.int32, (some, block, 1), 0) + turn * some
                )
                eb = jnp.where(position < live_end, cot[slot, who].astype(F32), 0.0).astype(BF16)
                cot[slot, who] = eb
                eb = eb.reshape(count, width)
                mixed = o_all[step, who].reshape(count, width)
                for cols in tiles:
                    h1 = tok[slot, who, :, cols].reshape(count, TILE).astype(F32)
                    h1 = h1 + mm(mixed, wo[:, cols])
                    h1_all[who, :, cols] = h1.reshape(some, block, TILE)
                hat, _ = norm_rows(h1_all[who].reshape(count, width))
                a2 = (hat * gain_ref[...] + bias_ref[...]).astype(BF16)

                def products(cols):
                    return mm(a2, wg[:, cols]), mm(a2, wu[:, cols]), mm_nt(eb, wd[cols, :])

                def hidden(cols, gate, up, back):
                    sig = 0.5 * jnp.tanh(0.5 * gate) + 0.5
                    act = gate * sig
                    hid[rows, cols] = (act * up).astype(BF16)
                    dgate[rows, cols] = (back * up * (sig + act * (1.0 - sig))).astype(BF16)
                    dup[rows, cols] = (back * act).astype(BF16)

                ready = products(tiles[0])
                a2_t[:, rows] = a2.T
                eb_t[:, rows] = eb.T
                for cols, ahead in zip(tiles, tiles[1:] + [None]):
                    coming = products(ahead) if ahead is not None else None
                    hidden(cols, *ready)
                    ready = coming
                for cols in tiles:
                    dc = mm_nt(dgate[rows, :], wg[cols, :]) + mm_nt(dup[rows, :], wu[cols, :])
                    part[now, who, :, :, cols] = dc.astype(BF16).reshape(some, 2, block // 2, TILE)
                return 0

            lax.fori_loop(0, owners // some, some_rows, 0)
            h1_ref[step] = h1_all[me]
            dh1_ref[step] = cot[slot, me].astype(F32)
            for copy in scatter_first(part, now, from_x, from_y, sems, 4, step):
                copy.start()

        @pl.when(step == steps)
        def _():
            for kind in range(3):
                for z in range(chips):
                    rows = pl.ds(pl.multiple_of((2 * z + 1 - core) * share, share), share)
                    outgoing[kind][z * share : (z + 1) * share, :] = acc[kind, rows, :].astype(BF16)
                to_core(kind).start()

        @pl.when((step >= 1) & (step <= steps))
        def _():
            scatter_middle(
                part, before, from_x, from_y, last_x, last_y, sems, 4, step - 1
            )

        @pl.when(step == steps)
        def _():
            for kind in range(2):
                to_core(kind).wait_recv()
                landed(kind).start()
            sum_kind(0)
            to_core(2).wait_recv()
            landed(2).start()
            sum_kind(1)
            sum_kind(2)

        def stage_copies(at, final):
            slot = lax.rem(at, 2)
            places = [(me, down0_hbm), (d, down3_hbm)]
            if not final:
                places += [(x, down1_hbm), (y, down2_hbm)]
            return [
                pltpu.make_async_copy(stage.at[slot, who], out.at[at], stage_sem.at[i, slot])
                for i, (who, out) in enumerate(places)
            ]

        @pl.when(step < steps)
        def _():
            @pl.when(step >= 2)
            def _():
                for copy in stage_copies(step - 2, False):
                    copy.wait()

            def some_output(turn, _):
                count = some * block
                who = pl.ds(turn * some, some)
                rows = pl.ds(pl.multiple_of(turn * count, count), count)
                for cols in tiles:
                    partial = mm(hid[rows, :], wd[:, cols]).astype(BF16)
                    stage[slot, who, :, cols] = partial.reshape(some, block, TILE)
                return 0

            lax.fori_loop(0, owners // some, some_output, 0)

            @pl.when(step < steps - 1)
            def _():
                for copy in stage_copies(step, False):
                    copy.start()

            @pl.when(step == steps - 1)
            def _():
                for copy in stage_copies(step, True):
                    copy.start()

            def some_grads(turn, _):
                rows = pl.ds(pl.multiple_of(turn * size, size), size)
                for cols in tiles:
                    acc[0, rows, cols] += mm(a2_t[rows, :], dgate[:, cols])
                    acc[1, rows, cols] += mm(a2_t[rows, :], dup[:, cols])
                    acc[2, rows, cols] += mm(eb_t[rows, :], hid[:, cols])
                return 0

            lax.fori_loop(0, width // size, some_grads, 0)

        @pl.when(step == steps)
        def _():
            for copy in stage_copies(steps - 2, False) + stage_copies(steps - 1, True):
                copy.wait()

        @pl.when(step >= 2)
        def _():
            prev = step - 2
            dc = scatter_last(part, older, from_x, from_y, last_x, last_y, sems, 4, prev)
            hat, scale = norm_rows(h1_ref[prev])
            sums_ref[0:1] += jnp.sum(dc * hat, axis=0, keepdims=True)
            sums_ref[1:2] += jnp.sum(dc, axis=0, keepdims=True)
            inner = dc * gain_ref[...]
            inner = inner - jnp.mean(inner, axis=-1, keepdims=True) - hat * jnp.mean(
                inner * hat, axis=-1, keepdims=True
            )
            dh1 = dh1_ref[prev] + scale * inner
            dh1_ref[prev] = dh1
            for copy in keep_rows(prev):
                copy.start()
            db = dh1.astype(BF16)
            db_own[prev] = db
            back = mm_nt(db, wo[...]).astype(BF16)
            for group in range(owners):
                do_own[prev, group] = back[:, group * feats : (group + 1) * feats]
            for copy in put_do(prev):
                copy.start()
            keep_do(prev).start()

        @pl.when(step == steps)
        def _():
            for copy in put_rows():
                copy.start()

        return 0

    lax.fori_loop(0, steps + 2, step_body, 0)

    o_mine = jnp.concatenate([o_all[step, me] for step in range(steps)], axis=0)
    for turn, which in enumerate((1 - core, core)):
        columns = [
            db_own[:, :, pl.ds(pl.multiple_of((2 * z + which) * share, share), share)].reshape(
                steps * block, share
            )
            for z in range(chips)
        ]
        values = mm_tn(jnp.concatenate(columns, axis=1), o_mine)
        if turn == 0:
            stage[steps % 2] = values.astype(BF16).reshape(owners, block, width)
            to_core(3).start()
        else:
            h1_all[...] = values.reshape(owners, block, width)

    to_core(3).wait_recv()
    landed(3).start()
    sum_kind(3)
    for kind in range(4):
        to_core(kind).wait_send()
    for copy in pile_copies(2) + pile_copies(3):
        copy.wait()

    for step in range(1, early):
        for copy in gather_relay(step):
            copy.wait_send()

    def sent(step, _):
        for copy in gather_own(step) + gather_relay(step):
            copy.wait_send()
        return 0

    lax.fori_loop(early, steps, sent, 0)

    for copy in put_rows():
        copy.wait()

    def finish(step, _):
        for copy in put_do(step) + keep_rows(step):
            copy.wait()
        keep_do(step).wait()
        return 0

    lax.fori_loop(0, steps, finish, 0)


def ffn(lengths, early, o, tokens, cotangent, wo, wg, wu, wd, gain, bias, steps, packs):
    rows, width = tokens.shape
    feats = o.shape[-1]
    owners = width // feats
    block = rows // (owners * steps)
    hidden = wg.shape[1]
    size = owners * block
    chips = packs // 2
    by_owner = lambda a: a.reshape(owners, steps, block, a.shape[1])
    own = jax.ShapeDtypeStruct((steps, block, width), F32)
    half = (steps, 2, block // 2, width)
    dma = pltpu.SemaphoreType.DMA
    flops = 2 * rows * width * (width + 9 * hidden)
    h1, dh1, sums, do, _, *rest = pl.pallas_call(
        functools.partial(ffn_kernel, packs),
        in_specs=[SMEM] + [ANY] * 14 + [VMEM, VMEM],
        out_specs=[ANY, ANY, VMEM] + [ANY] * (7 + len(PILES)),
        out_shape=[
            own,
            own,
            jax.ShapeDtypeStruct((2, width), F32),
            jax.ShapeDtypeStruct((owners, steps, block, feats), BF16),
            jax.ShapeDtypeStruct((4, size, width), BF16),
        ]
        + [
            jax.ShapeDtypeStruct((taken, block, width), BF16)
            for taken in (steps, steps - 1, steps - 1, steps, 2)
        ]
        + [jax.ShapeDtypeStruct((2, 2, width // packs, width), BF16)] * len(PILES),
        scratch_shapes=[
            pltpu.VMEM((width, width), BF16),
            pltpu.VMEM((width, hidden), BF16),
            pltpu.VMEM((width, hidden), BF16),
            pltpu.VMEM((hidden, width), BF16),
            pltpu.VMEM((steps, owners, block, width), BF16),
            pltpu.VMEM((2, owners, block, width), BF16),
            pltpu.VMEM((2, owners, block, width), BF16),
            pltpu.VMEM((owners, block, width), F32),
            pltpu.VMEM((size, hidden), BF16),
            pltpu.VMEM((size, hidden), BF16),
            pltpu.VMEM((size, hidden), BF16),
            pltpu.VMEM((3, owners, 2, block // 2, width), BF16),
            pltpu.VMEM(half, BF16),
            pltpu.VMEM(half, BF16),
            pltpu.VMEM((steps, block // 2, width), BF16),
            pltpu.VMEM((steps, block // 2, width), BF16),
            pltpu.VMEM((width, size), BF16),
            pltpu.VMEM((width, size), BF16),
            pltpu.VMEM((3, width, hidden), F32),
            pltpu.VMEM((2, owners, block, width), BF16),
            pltpu.VMEM((steps, owners, block, feats), BF16),
            pltpu.VMEM((steps, block, width), BF16),
            pltpu.VMEM(own.shape, F32),
            pltpu.VMEM(own.shape, F32),
            dma((2, steps)),
            dma((7,)),
            dma((2,)),
            dma((2,)),
            dma((steps,)),
            dma((early[0].shape[1], 4)),
            dma((4, 2)),
            dma((steps,)),
            dma((2, chips)),
            dma((4,)),
            dma((4,)),
            dma((15, steps)),
            dma((15, steps)),
        ],
        compiler_params=pltpu.CompilerParams(
            collective_id=0, has_side_effects=True, vmem_limit_bytes=VMEM_CAP
        ),
        cost_estimate=pl.CostEstimate(flops=flops, bytes_accessed=rows * width * 14, transcendentals=0),
        name="ffn",
    )(lengths, *early, o, by_owner(tokens), by_owner(cotangent), *wo, wg, wu, wd, gain, bias)
    return h1, dh1, sums, do.reshape(rows, feats), rest[:5], rest[5:]


def last_kernel(
    packs,
    grad_hbm, grad_t_hbm, a1_hbm, tok_hbm, dh1_hbm, h1_hbm, wq_hbm, wk_hbm, wv_hbm, gain_ref, sums2_ref, *rest,
):
    chips = packs // 2
    downs, rest = rest[:5], rest[5:]
    piles, rest = rest[: len(PILES)], rest[len(PILES) :]
    (
        out_hbm, tg_hbm, gq_hbm, gk_hbm, gv_hbm, gate_hbm, up_hbm, down_hbm, proj_hbm, norm_ref,
        out_ref, tg_ref, gq_ref, gk_ref, gv_ref, gate_ref, up_ref, down_ref, proj_ref, row_sem, result_sem,
        dh1_ref, wq_ref, wk_ref, wv_ref, weight_sem,
        grad, grad_t, a1, tok, part, from_x, from_y, last_x, last_y, h1, down, pile, pile_out, pile_in, sums1,
        full, core_out, core_in, chip_out, chip_in, proj_out, proj_in, norm_out, norm_in,
        grad_sem, tok_sem, load_sem, core_send, core_recv, chip_send, chip_recv, pile_send, pile_recv,
        small_send, small_recv, send_sem, recv_sem,
    ) = rest
    steps, owners, _, half, width = part.shape
    feats = wq_hbm.shape[1]
    size = owners * 2 * half
    share = width // packs
    tall = 3 * feats
    sems = (send_sem, recv_sem)
    me, x, y, d = neighbours()
    core, chip, other_core, next_chips = pack_neighbours(packs)

    def fetch(step):
        return [
            pltpu.make_async_copy(grad_hbm.at[:, step], grad.at[step], grad_sem.at[step]),
            pltpu.make_async_copy(tok_hbm.at[:, step], tok.at[step], tok_sem.at[step]),
        ]

    later = [(grad_t_hbm, grad_t), (a1_hbm, a1)]
    later += [(piles[i], pile.at[i]) for i in range(len(PILES))]
    later += [(h1_hbm, h1)]
    later += [(downs[i], down.at[i, pl.ds(0, downs[i].shape[0])]) for i in range(4)]
    later += [(downs[4], down.at[pl.ds(1, 2), steps - 1])]
    later = [pltpu.make_async_copy(a, b, load_sem.at[i]) for i, (a, b) in enumerate(later)]

    def to_core():
        return remote_pack(core_out, core_in, core_send, core_recv, other_core)

    def to_chips():
        return [
            remote_pack(
                chip_out.at[lax.rem(chip + i + 1, chips)], chip_in.at[i],
                chip_send.at[i], chip_recv.at[i], device,
            )
            for i, device in enumerate(next_chips)
        ]

    def pile_copies():
        index = lax.axis_index("dp")
        return [
            remote_pack(
                pile_out.at[i], pile_in.at[i], pile_send.at[i], pile_recv.at[i],
                index + 2 * (chip_across(chip, bits) - chip),
            )
            for i, bits in enumerate(reversed(PARTNERS))
        ]

    def small(kind, source, target):
        return [
            remote(source(device), target.at[i], (small_send, small_recv), kind, i, device)
            for i, device in enumerate((x, y, d))
        ]

    def proj_copies():
        return small(0, lambda device: proj_out.at[device], proj_in)

    def norm_copies():
        return small(1, lambda device: norm_out, norm_in)

    def begin(step, _):
        for copy in fetch(step):
            copy.start()
        return 0

    weights = ((wq_hbm, wq_ref), (wk_hbm, wk_ref), (wv_hbm, wv_ref), (dh1_hbm, dh1_ref))
    weights = [pltpu.make_async_copy(a, b, weight_sem.at[i]) for i, (a, b) in enumerate(weights)]
    for copy in weights[:3]:
        copy.start()
    lax.fori_loop(0, steps, begin, 0)
    for copy in later + weights[3:]:
        copy.start()
    group_barrier((x, y, d), [other_core] + next_chips)
    sums1[...] = jnp.zeros_like(sums1)

    for copy in weights[:3]:
        copy.wait()

    def first(step, _):
        for copy in fetch(step):
            copy.wait()
        rows = grad[step].reshape(size, tall)
        da = mm_nt(rows[:, :feats], wq_ref[...])
        da = da + mm_nt(rows[:, feats : 2 * feats], wk_ref[...])
        da = da + mm_nt(rows[:, 2 * feats :], wv_ref[...])
        part[step] = da.astype(BF16).reshape(owners, 2, half, width)
        for copy in scatter_first(part, step, from_x, from_y, sems, 0, step):
            copy.start()

        @pl.when(step == 0)
        def _():
            for copy in later[2 : 2 + len(PILES)]:
                copy.wait()
            for i in range(2):
                total = pile[2 * i, 1].astype(F32) + pile[2 * i + 1, 1].astype(F32)
                pile_out[i] = total.astype(BF16)
            for copy in pile_copies():
                copy.start()

        hat, _ = norm_rows(tok[step].reshape(size, width).astype(F32))
        sums1[0:1] += jnp.sum(da * hat, axis=0, keepdims=True)
        sums1[1:2] += jnp.sum(da, axis=0, keepdims=True)
        return 0

    lax.fori_loop(0, steps, first, 0)
    later[0].wait()
    later[1].wait()
    for kind in range(3):
        rows = pl.ds(kind * feats, feats)
        full[rows, :] = mm(grad_t[rows, :], a1[...])
    full[pl.ds(tall, 16), :] = jnp.concatenate(
        [sums1[...], sums2_ref[...], jnp.zeros((12, width), F32)], axis=0
    )
    for z in range(chips):
        columns = pl.ds(pl.multiple_of((2 * z + 1 - core) * share, share), share)
        core_out[z] = full[:, columns].astype(BF16)
    to_core().start()

    to_core().wait_recv()
    for z in range(chips):
        columns = pl.ds(pl.multiple_of((2 * z + core) * share, share), share)
        chip_out[z] = (full[:, columns] + core_in[z].astype(F32)).astype(BF16)
    for copy in to_chips():
        copy.start()
    for copy in later[2 + len(PILES) :]:
        copy.wait()

    def sum_piles():
        for copy in pile_copies():
            copy.wait_recv()
        for kind in range(4):
            half, at = kind // 2, kind % 2
            total = pile[2 * half, 0, at].astype(F32) + pile[2 * half + 1, 0, at].astype(F32)
            total = total + pile_in[half, at].astype(F32)
            if kind < 2:
                (gate_ref, up_ref)[kind][...] = total
            elif kind == 2:
                down_ref[...] = total.T
            else:
                for group in range(owners):
                    proj_out[group] = total[:, group * feats : (group + 1) * feats].astype(BF16)
                for copy in proj_copies():
                    copy.start()

    def row_copies(step):
        return [
            pltpu.make_async_copy(source.at[step], out.at[step], row_sem.at[i, step])
            for i, (source, out) in enumerate(((out_ref, out_hbm), (tg_ref, tg_hbm)))
        ]

    results = (
        (gq_ref, gq_hbm), (gk_ref, gk_hbm), (gv_ref, gv_hbm), (gate_ref, gate_hbm),
        (up_ref, up_hbm), (down_ref, down_hbm), (proj_ref, proj_hbm),
    )
    results = [
        pltpu.make_async_copy(source, out, result_sem.at[i])
        for i, (source, out) in enumerate(results)
    ]

    def finish(step):
        da = scatter_last(part, step, from_x, from_y, last_x, last_y, sems, 0, step)
        hat, scale = norm_rows(tok[step, me].astype(F32))
        inner = da * gain_ref[...]
        inner = inner - jnp.mean(inner, axis=-1, keepdims=True) - hat * jnp.mean(
            inner * hat, axis=-1, keepdims=True
        )
        tg_ref[step] = (dh1_ref[step] + scale * inner).astype(BF16)
        row_copies(step)[1].start()

    def second(step, _):
        scatter_middle(part, step, from_x, from_y, last_x, last_y, sems, 0, step)
        total = h1[step]
        for i in range(4):
            total = total + down[i, step].astype(F32)
        out_ref[step] = total.astype(BF16)
        row_copies(step)[0].start()
        return 0

    def third(step, _):
        finish(step)
        return 0

    weights[3].wait()
    lax.fori_loop(0, steps, second, 0)
    sum_piles()
    for copy in results[3:6]:
        copy.start()
    lax.fori_loop(0, steps - 2, third, 0)
    total = chip_out[chip].astype(F32)
    for i, copy in enumerate(to_chips()):
        copy.wait_recv()
        total = total + chip_in[i].astype(F32)
    norm_out[...] = total[tall : tall + 8]
    for copy in norm_copies():
        copy.start()
    finish(steps - 2)
    for kind, ref in enumerate((gq_ref, gk_ref, gv_ref)):
        ref[...] = total[kind * feats : (kind + 1) * feats].T
        results[kind].start()
    total = proj_out[me].astype(F32)
    for i, copy in enumerate(proj_copies()):
        copy.wait_recv()
        total = total + proj_in[i].astype(F32)
    proj_ref[...] = total.T
    results[6].start()
    finish(steps - 1)
    total = norm_out[...]
    for i, copy in enumerate(norm_copies()):
        copy.wait_recv()
        total = total + norm_in[i]
    norm_ref[...] = total
    for copy in results:
        copy.wait()
    for step in range(steps):
        for copy in row_copies(step):
            copy.wait()
    for copy in [to_core()] + to_chips() + pile_copies() + proj_copies() + norm_copies():
        copy.wait_send()


def last(grads, grads_t, a1, tokens, dh1, h1, wq, wk, wv, gain, sums2, downs, piles, packs):
    rows, width = tokens.shape
    steps, block, _ = dh1.shape
    owners = rows // (steps * block)
    feats = wq.shape[1]
    hidden = piles[0].shape[-1]
    chips = packs // 2
    share = width // packs
    tall = 3 * feats + 16
    by_owner = lambda a: a.reshape(owners, steps, block, a.shape[1])
    half = (steps, 2, block // 2, width)
    dma = pltpu.SemaphoreType.DMA
    own = jax.ShapeDtypeStruct((steps, block, width), BF16)
    f32 = lambda *shape: jax.ShapeDtypeStruct(shape, F32)
    out_shape = [own, own] + [f32(share, feats)] * 3
    out_shape += [f32(share, hidden)] * 2 + [f32(hidden, share), f32(feats, share), f32(8, share)]
    return pl.pallas_call(
        functools.partial(last_kernel, packs),
        in_specs=[ANY] * 9 + [VMEM] * 2 + [ANY] * (5 + len(piles)),
        out_specs=[ANY] * 9 + [VMEM],
        out_shape=out_shape,
        scratch_shapes=[pltpu.VMEM(a.shape, a.dtype) for a in out_shape[:9]]
        + [
            dma((2, steps)),
            dma((7,)),
            pltpu.VMEM((steps, block, width), F32),
            pltpu.VMEM((width, feats), BF16),
            pltpu.VMEM((width, feats), BF16),
            pltpu.VMEM((width, feats), BF16),
            dma((4,)),
            pltpu.VMEM((steps, owners, block, 3 * feats), BF16),
            pltpu.VMEM((3 * feats, rows), BF16),
            pltpu.VMEM((rows, width), BF16),
            pltpu.VMEM((steps, owners, block, width), BF16),
            pltpu.VMEM((steps, owners, 2, block // 2, width), BF16),
            pltpu.VMEM(half, BF16),
            pltpu.VMEM(half, BF16),
            pltpu.VMEM((steps, block // 2, width), BF16),
            pltpu.VMEM((steps, block // 2, width), BF16),
            pltpu.VMEM((steps, block, width), F32),
            pltpu.VMEM((4, steps, block, width), BF16),
            pltpu.VMEM((len(PILES), 2, 2, share, hidden), BF16),
            pltpu.VMEM((2, 2, share, hidden), BF16),
            pltpu.VMEM((2, 2, share, hidden), BF16),
            pltpu.VMEM((2, width), F32),
            pltpu.VMEM((tall, width), F32),
            pltpu.VMEM((chips, tall, share), BF16),
            pltpu.VMEM((chips, tall, share), BF16),
            pltpu.VMEM((chips, tall, share), BF16),
            pltpu.VMEM((chips - 1, tall, share), BF16),
            pltpu.VMEM((owners, share, feats), BF16),
            pltpu.VMEM((owners - 1, share, feats), BF16),
            pltpu.VMEM((8, share), F32),
            pltpu.VMEM((owners - 1, 8, share), F32),
            dma((steps,)),
            dma((steps,)),
            dma((8 + len(piles),)),
            dma,
            dma,
            dma((chips - 1,)),
            dma((chips - 1,)),
            dma((2,)),
            dma((2,)),
            dma((2, owners - 1)),
            dma((2, owners - 1)),
            dma((6, steps)),
            dma((6, steps)),
        ],
        compiler_params=pltpu.CompilerParams(
            collective_id=1, has_side_effects=True, vmem_limit_bytes=VMEM_CAP
        ),
        cost_estimate=pl.CostEstimate(
            flops=12 * rows * width * feats, bytes_accessed=rows * width * 20, transcendentals=0
        ),
        name="last",
    )(
        by_owner(grads), grads_t, a1, by_owner(tokens), dh1, h1, wq, wk, wv, gain, sums2, *downs, *piles
    )


def hand_out_kernel(count, *refs):
    sources, outs, held = refs[: count + 1], refs[count + 1 : 2 * count + 5], refs[2 * count + 5 : -2]
    in_sem, out_sem = refs[-2:]
    norm, vectors = held[count], held[count + 1 :]
    loads = [pltpu.make_async_copy(sources[i], held[i], in_sem.at[i]) for i in range(count + 1)]
    ready = list(held[:count]) + list(vectors)
    stores = [
        pltpu.make_async_copy(ready[i], outs[i], out_sem.at[i]) for i in range(count + 4)
    ]
    for copy in reversed(loads):
        copy.start()
    loads[count].wait()
    for i, vector in enumerate(vectors):
        vector[...] = norm[i]
        stores[count + i].start()
    for load, store in zip(loads[:count], stores):
        load.wait()
        store.start()
    for store in stores:
        store.wait()


def hand_out(arrays, norms):
    count = len(arrays)
    shape = lambda a: jax.ShapeDtypeStruct(a.shape, a.dtype)
    vectors = [jax.ShapeDtypeStruct(norms.shape[1:], F32)] * 4
    out_shape = [shape(a) for a in arrays] + vectors
    return pl.pallas_call(
        functools.partial(hand_out_kernel, count),
        in_specs=[ANY] * (count + 1),
        out_specs=[ANY] * (count + 4),
        out_shape=out_shape,
        scratch_shapes=[pltpu.VMEM(a.shape, a.dtype) for a in list(arrays) + [norms] + vectors]
        + [pltpu.SemaphoreType.DMA((count + 4,))] * 2,
        compiler_params=pltpu.CompilerParams(vmem_limit_bytes=VMEM_CAP),
        name="hand_out",
    )(*arrays, norms)


def local_square(
    tokens, lengths, cotangent, norm1_gain, norm1_bias, w_query, w_key, w_value, w_output,
    norm2_gain, norm2_bias, w_gate, w_up, w_down,
):
    rows, width = tokens.shape
    groups = lax.axis_size("mp")
    packs = lax.axis_size("dp")
    gain1, bias1 = norm1_gain[None, :], norm1_bias[None, :]
    exchange = lambda a, shift: lax.ppermute(a, "mp", [(i, i ^ shift) for i in range(groups)])
    w_outputs = [w_output] + [exchange(w_output, shift) for shift in range(1, groups)]
    a1, k, v, qt, kt, vt, cosine, sine = project(
        lengths, tokens, gain1, bias1, w_query, w_key, w_value
    )
    early, early_first, mixed_t, lse = attend(lengths, qt, k, vt, 0, EARLY, STEPS)
    early = [early, exchange(early, 1), exchange(early, 2), exchange(early_first, 3)]
    qt_late, *w_outputs = lax.optimization_barrier((qt, *w_outputs))
    mixed, mixed_t, lse = attend(lengths, qt_late, k, vt, EARLY, STEPS, STEPS, (mixed_t, lse))
    h1, dh1, sums2, mixed_grad, downs, piles = ffn(
        lengths, early, mixed, tokens, cotangent, w_outputs, w_gate, w_up, w_down,
        norm2_gain[None, :], norm2_bias[None, :], STEPS, packs,
    )
    downs[1:4] = [exchange(downs[shift], shift) for shift in range(1, groups)]
    for i, bits in enumerate(PARTNERS):
        perm = [(j, j ^ (2 * bits)) for j in range(packs)]
        piles[2 * i + 1] = lax.ppermute(piles[2 * i + 1], "dp", perm)
    grads, grads_t = attend_back(
        lengths, qt, k, kt, v, mixed_grad, mixed_t, lse, cosine, sine
    )
    *results, norms = last(
        grads, grads_t, a1, tokens, dh1, h1, w_query, w_key, w_value, gain1, sums2, downs, piles, packs
    )
    output, tokens_grad, grad_q, grad_k, grad_v, gate, up, down, proj, *sums = hand_out(
        results, norms
    )
    own_rows = (rows // groups, width)
    return (
        output.reshape(own_rows),
        tokens_grad.reshape(own_rows),
        grad_q,
        grad_k,
        grad_v,
        proj,
        gate,
        up,
        down,
        *sums,
    )


def layer_stats(row_values, gain_vec, bias_vec):
    normed, row_scale = norm_rows(row_values)
    return (normed * gain_vec + bias_vec, normed, row_scale)


def layer_back(gradient, normed, row_scale, gain_vec):
    inner_grad = gradient * gain_vec
    centred_grad = inner_grad - jnp.mean(inner_grad, axis=-1, keepdims=True)
    return row_scale * (
        centred_grad - normed * jnp.mean(inner_grad * normed, axis=-1, keepdims=True)
    )


def scatter_rows(partial, axis, dim=0):
    return lax.psum_scatter(
        partial.astype(BF16), axis, scatter_dimension=dim, tiled=True
    ).astype(F32)


def local(
    tokens, lengths, cotangent, norm1_gain, norm1_bias, w_query, w_key, w_value, w_output,
    norm2_gain, norm2_bias, w_gate, w_up, w_down,
):
    row_count, width = tokens.shape
    feats = w_query.shape[1]
    gain1, bias1 = norm1_gain[None, :], norm1_bias[None, :]
    a1, k, v, qt, kt, vt, cosine, sine = project(
        lengths, tokens, gain1, bias1, w_query, w_key, w_value
    )
    mixed, mixed_t, lse = attend(lengths, qt, k, vt, 0, 1, 1)
    mixed = mixed.reshape(row_count, feats)

    share_rows = row_count // lax.axis_size("mp")
    own_start = lax.axis_index("mp") * share_rows
    own = lambda a: lax.dynamic_slice_in_dim(a, own_start, share_rows, 0)
    live_end = row_count - lengths[0, lengths.shape[1] - 1]
    live = jnp.arange(row_count, dtype=jnp.int32)[:, None] < live_end
    out_grad = jnp.where(live, cotangent, jnp.zeros_like(cotangent))

    attn_rows = scatter_rows(mm(mixed, w_output), "mp")
    residual = own(tokens).astype(F32) + attn_rows
    normed_second, hat_second, scale_second = layer_stats(residual, norm2_gain, norm2_bias)
    inputs_second = lax.all_gather(normed_second.astype(BF16), "mp", axis=0, tiled=True)
    gate_pre = mm(inputs_second, w_gate)
    up_proj = mm(inputs_second, w_up)
    gate_sig = jax.nn.sigmoid(gate_pre)
    gate_act = gate_pre * gate_sig
    hidden = (gate_act * up_proj).astype(BF16)
    output_own = residual + scatter_rows(mm(hidden, w_down), "mp")
    down_w_grad = mm_tn(hidden, out_grad)
    hidden_grad = mm_nt(out_grad, w_down)
    gate_in_grad = (hidden_grad * up_proj * gate_sig * (1.0 + gate_pre * (1.0 - gate_sig))).astype(BF16)
    up_in_grad = (hidden_grad * gate_act).astype(BF16)
    gate_w_grad = mm_tn(inputs_second, gate_in_grad)
    up_w_grad = mm_tn(inputs_second, up_in_grad)
    ffn_sums = (
        scatter_rows(gate_w_grad, "dp"),
        scatter_rows(up_w_grad, "dp"),
        scatter_rows(down_w_grad, "dp", 1),
    )
    second_grad = scatter_rows(mm_nt(gate_in_grad, w_gate) + mm_nt(up_in_grad, w_up), "mp")
    residual_grad = own(out_grad).astype(F32) + layer_back(
        second_grad, hat_second, scale_second, norm2_gain
    )
    attn_grad = lax.all_gather(residual_grad.astype(BF16), "mp", axis=0, tiled=True)
    gain_second_grad = jnp.sum(second_grad * hat_second, axis=0)
    bias_second_grad = jnp.sum(second_grad, axis=0)
    output_w_grad = mm_tn(mixed, attn_grad)
    mixed_grad = mm_nt(attn_grad, w_output).astype(BF16)

    grads, grads_t = attend_back(
        lengths, qt, k, kt, v, mixed_grad, mixed_t, lse, cosine, sine
    )
    w_qkv = jnp.concatenate([w_query, w_key, w_value], axis=1)
    qkv_w_grad = mm(grads_t, a1)
    first_grad = scatter_rows(mm_nt(grads, w_qkv), "mp")
    hat_own, scale_own = norm_rows(own(tokens).astype(F32))
    tokens_grad = (residual_grad + layer_back(first_grad, hat_own, scale_own, norm1_gain)).astype(BF16)
    gain_parts = jnp.stack(
        [
            jnp.sum(first_grad * hat_own, axis=0),
            jnp.sum(first_grad, axis=0),
            gain_second_grad,
            bias_second_grad,
        ]
    )
    gain_parts = scatter_rows(lax.psum(gain_parts, "mp"), "dp", 1)
    attn_sums = scatter_rows(jnp.concatenate([qkv_w_grad, output_w_grad], axis=0), "dp", 1)
    return (
        output_own.astype(BF16),
        tokens_grad,
        attn_sums[:feats].T,
        attn_sums[feats : 2 * feats].T,
        attn_sums[2 * feats : 3 * feats].T,
        attn_sums[3 * feats :],
        ffn_sums[0],
        ffn_sums[1],
        ffn_sums[2],
        gain_parts[0],
        gain_parts[1],
        gain_parts[2],
        gain_parts[3],
    )


def solution(mesh):
    square = mesh.shape["mp"] == 4 and mesh.shape["dp"] == 2 * CHIPS
    rows, weight_in, weight_out = P("dp", None), P(None, "mp"), P("mp", None)
    row_out = P(("dp", "mp"), None)
    return jax.shard_map(
        local_square if square else local,
        mesh=mesh,
        in_specs=(rows, rows, rows, P(), P(), weight_in, weight_in, weight_in, weight_out)
        + (P(), P(), weight_in, weight_in, weight_out),
        out_specs=(row_out, row_out)
        + (P("dp", "mp"),) * 3
        + (P("mp", "dp"), P("dp", "mp"), P("dp", "mp"), P("mp", "dp"))
        + (P("dp"),) * 4,
        check_vma=False,
    )
```

```python
import functools
import math

import jax
import jax.numpy as jnp
import numpy as np
from jax import lax
from jax.experimental import pallas as pl
from jax.experimental.pallas import tpu as pltpu
from jax.sharding import PartitionSpec as P

HD = 64
HALF = HD // 2
PAIR = 2 * HD
QB = 128
KB = 256
EPS = 1e-05
BASE = 10000.0
NEG = -1e30
MOST = 1024
SCALE = HD**-0.5
VMEM = pl.BlockSpec(memory_space=pltpu.VMEM)
SMEM = pl.BlockSpec(memory_space=pltpu.SMEM)
ANY = pl.BlockSpec(memory_space=pl.ANY)
MESH = pl.DeviceIdType.MESH
STEPS = 5
EARLY = 2
MIDDLE = 2
TILE = 256
VMEM_CAP = 62 << 20
F32 = jnp.float32
BF16 = jnp.bfloat16


def mm(a, b):
    return jnp.dot(a, b, preferred_element_type=F32)


def mm_nt(a, b):
    return lax.dot_general(a, b, (((1,), (1,)), ((), ())), preferred_element_type=F32)


def mm_tn(a, b):
    return lax.dot_general(a, b, (((0,), (0,)), ((), ())), preferred_element_type=F32)


def window_bounds(len_ref, position):
    entries = len_ref.shape[1]
    start = jnp.zeros_like(position)
    end = jnp.zeros_like(position)
    edge = jnp.int32(0)
    for entry in range(entries):
        size = len_ref[0, entry]
        inside = position >= edge
        start = jnp.where(inside, edge, start)
        edge = edge + size
        end = jnp.where(inside, edge, end)
    return start, end


def norm_rows(rows):
    mean = jnp.mean(rows, axis=-1, keepdims=True)
    centred = rows - mean
    scale = lax.rsqrt(jnp.mean(centred * centred, axis=-1, keepdims=True) + EPS)
    return centred * scale, scale


def rotate_t(field, cosine, sine, direction):
    parts = []
    for head in range(field.shape[0] // HD):
        first = field[head * HD : head * HD + HALF]
        second = field[head * HD + HALF : (head + 1) * HD]
        parts.append(first * cosine - direction * (second * sine))
        parts.append(second * cosine + direction * (first * sine))
    return jnp.concatenate(parts, axis=0)


def qkv_kernel(
    len_ref, tok_ref, gain_ref, bias_ref, freq_ref, wq_ref, wk_ref, wv_ref,
    a1_ref, k_ref, v_ref, qt_ref, kt_ref, vt_ref, cos_ref, sin_ref,
):
    rows = tok_ref.shape[0]
    position = lax.broadcasted_iota(jnp.int32, (1, rows), 1) + pl.program_id(0) * rows
    start, _ = window_bounds(len_ref, position)
    offset = (position - start).astype(F32)
    theta = freq_ref[...] * offset
    cosine, sine = jnp.cos(theta), jnp.sin(theta)
    cos_ref[...] = cosine
    sin_ref[...] = sine
    parts = 2
    part = rows // parts
    spans = [pl.ds(i * part, part) for i in range(parts)]
    inputs = []
    for span in spans:
        hat, _ = norm_rows(tok_ref[span, :].astype(F32))
        a1 = (hat * gain_ref[...] + bias_ref[...]).astype(BF16)
        a1_ref[span, :] = a1
        inputs.append(a1)
    for i, (span, a1) in enumerate(zip(spans, inputs)):
        turn = slice(i * part, (i + 1) * part)
        for w_ref, out_ref, out_t_ref, scale in (
            (wq_ref, None, qt_ref, SCALE),
            (wk_ref, k_ref, kt_ref, None),
        ):
            field = mm(a1, w_ref[...]).T
            field = rotate_t(field, cosine[:, turn], sine[:, turn], 1.0).astype(BF16)
            if scale is not None:
                field = field * jnp.asarray(scale, BF16)
            out_t_ref[:, span] = field
            if out_ref is not None:
                out_ref[span, :] = field.T
        values = mm(a1, wv_ref[...]).astype(BF16)
        v_ref[span, :] = values
        vt_ref[:, span] = values.T


def project(lengths, tokens, gain, bias, wq, wk, wv):
    rows, width = tokens.shape
    feats = wq.shape[1]
    block = min(512, rows)
    freq = np.float32(BASE) ** (np.float32(-2.0 / HD) * np.arange(HALF, dtype=np.float32))
    freq = jnp.asarray(freq[:, None], F32)
    whole = lambda a: pl.BlockSpec(a.shape, lambda i: (0, 0))
    by_row = lambda cols: pl.BlockSpec((block, cols), lambda i: (i, 0))
    by_col = lambda size: pl.BlockSpec((size, block), lambda i: (0, i))
    nat = jax.ShapeDtypeStruct((rows, feats), BF16)
    trans = jax.ShapeDtypeStruct((feats, rows), BF16)
    table = jax.ShapeDtypeStruct((HALF, rows), F32)
    return pl.pallas_call(
        qkv_kernel,
        grid=(rows // block,),
        in_specs=[SMEM, by_row(width)] + [whole(a) for a in (gain, bias, freq, wq, wk, wv)],
        out_specs=[by_row(width)] + [by_row(feats)] * 2 + [by_col(feats)] * 3 + [by_col(HALF)] * 2,
        out_shape=[jax.ShapeDtypeStruct((rows, width), BF16)] + [nat] * 2 + [trans] * 3 + [table] * 2,
        compiler_params=pltpu.CompilerParams(vmem_limit_bytes=VMEM_CAP),
        cost_estimate=pl.CostEstimate(
            flops=6 * rows * width * feats, bytes_accessed=rows * width * 8, transcendentals=0
        ),
        name="qkv",
    )(lengths, tokens, gain, bias, freq, wq, wk, wv)


def block_diagonal_t(pair):
    head = lax.broadcasted_iota(jnp.int32, pair.shape, 0) < HD
    zero = jnp.zeros_like(pair)
    return jnp.concatenate([jnp.where(head, pair, zero), jnp.where(head, zero, pair)], axis=1)


def diagonal_blocks(product):
    return jnp.concatenate([product[:HD, :QB], product[HD:, QB:]], axis=1)


def key_range(len_ref, first):
    low, _ = window_bounds(len_ref, first)
    _, high = window_bounds(len_ref, first + (QB - 1))
    base = low // QB * QB
    return base, (high - base + (KB - 1)) // KB


def key_rows(at, rows):
    return pl.ds(pl.multiple_of(jnp.clip(at, 0, rows - KB), QB), KB)


def inside_window(start, end, at, rows):
    shift = jnp.minimum(at, rows - KB)
    key = lax.broadcasted_iota(jnp.int32, (KB, QB), 0)
    inside = (key >= jnp.maximum(start, at) - shift) & (key < end - shift)
    return jnp.concatenate([inside, inside], axis=1)


def fill_schedule(len_ref, sched, blocks, index_of, rows):
    def nothing(n):
        sched[0, n] = 0
        sched[1, n] = rows

    def one_query(turn, n):
        base, count = key_range(len_ref, index_of(turn) * QB)

        def one_key(kb, _):
            sched[0, n + kb] = turn
            sched[1, n + kb] = base + kb * KB
            return 0

        lax.fori_loop(0, count, one_key, 0)
        return n + count

    nothing(0)
    n = lax.fori_loop(0, blocks, one_query, jnp.int32(1))
    for extra in range(3):
        nothing(n + extra)
    return n - 1


def store_window(len_ref, window, turn, first):
    position = lax.broadcasted_iota(jnp.int32, (1, QB), 1) + first
    window[turn, 0:1], window[turn, 1:2] = window_bounds(len_ref, position)


def run_pipeline(count, pairs, inside, scores, soften, mix):
    def one_turn(n, buf):
        mask = inside(n)
        for p in pairs:
            mix(n - 1, 1 - buf, p)
            scores(n + 1, 1 - buf, p)
            soften(n, buf, p, mask)

    def two_turns(turn, _):
        one_turn(1 + 2 * turn, 0)
        one_turn(2 + 2 * turn, 1)
        return 0

    turns = (count + 1) // 2
    for p in pairs:
        scores(1, 0, p)
    lax.fori_loop(0, turns, two_turns, 0)
    for p in pairs:
        mix(2 * turns, 1, p)


def attend_kernel(begin, steps, len_ref, qt_ref, k_hbm, vt_hbm, *rest):
    if begin > 0:
        ot_before, lse_before, *rest = rest
    o_ref, *rest = rest
    first_ref = None
    if begin == 0 and steps > 1:
        first_ref, *rest = rest
    ot_ref, lse_ref, k_ref, vt_ref, load_sem, *rest = rest
    sched, window, diag, stat, acc, keep_buf, score_buf, prob_buf = rest
    loads = [
        pltpu.make_async_copy(k_hbm, k_ref, load_sem.at[0]),
        pltpu.make_async_copy(vt_hbm, vt_ref, load_sem.at[1]),
    ]
    for copy in loads:
        copy.start()
    if begin > 0:
        ot_ref[...] = ot_before[...]
        lse_ref[...] = lse_before[...]
    owners, taken = o_ref.shape[:2]
    feats, rows = qt_ref.shape
    pairs = range(feats // PAIR)
    feat = [pl.ds(p * PAIR, PAIR) for p in pairs]

    def index_of(turn):
        return turn // taken * steps + begin + lax.rem(turn, taken)

    def prepare(turn, _):
        first = index_of(turn) * QB
        cols = pl.ds(pl.multiple_of(first, QB), QB)
        store_window(len_ref, window, turn, first)
        for p in pairs:
            diag[turn, p] = block_diagonal_t(qt_ref[feat[p], cols])
            stat[turn, p : p + 1] = jnp.full((1, 2 * QB), NEG, F32)
            stat[turn, 4 + p : 5 + p] = jnp.zeros((1, 2 * QB), F32)
            acc[turn, p] = jnp.zeros((HD, 2 * QB), F32)
        return 0

    lax.fori_loop(0, owners * taken, prepare, 0)
    count = fill_schedule(len_ref, sched, owners * taken, index_of, rows)
    for copy in loads:
        copy.wait()

    def inside(n):
        turn = sched[0, n]
        return inside_window(window[turn, 0:1], window[turn, 1:2], sched[1, n], rows)

    def scores(n, buf, p):
        turn, keys = sched[0, n], key_rows(sched[1, n], rows)
        score_buf[buf, p] = mm(k_ref[keys, feat[p]], diag[turn, p])

    def soften(n, buf, p, mask):
        turn = sched[0, n]
        top, total = stat[turn, p : p + 1], stat[turn, 4 + p : 5 + p]
        values = jnp.where(mask, score_buf[buf, p], NEG)
        new_top = jnp.maximum(top, jnp.max(values, axis=0, keepdims=True))
        prob = jnp.exp(values - new_top)
        keep = jnp.exp(top - new_top)
        stat[turn, p : p + 1] = new_top
        stat[turn, 4 + p : 5 + p] = keep * total + jnp.sum(prob, axis=0, keepdims=True)
        keep_buf[buf, p : p + 1] = keep
        prob_buf[buf, p] = prob.astype(BF16)

    def mix(n, buf, p):
        turn, keys = sched[0, n], key_rows(sched[1, n], rows)
        mixed = diagonal_blocks(mm(vt_ref[feat[p], keys], prob_buf[buf, p]))
        acc[turn, p] = acc[turn, p] * keep_buf[buf, p : p + 1] + mixed

    prob_buf[1] = jnp.zeros_like(prob_buf[1])
    keep_buf[1] = jnp.ones_like(keep_buf[1])
    run_pipeline(count, pairs, inside, scores, soften, mix)

    def finish(turn, _):
        index = index_of(turn)
        cols = pl.ds(pl.multiple_of(index * QB, QB), QB)
        for p in pairs:
            top, total = stat[turn, p : p + 1], stat[turn, 4 + p : 5 + p]
            mixed = acc[turn, p] / total
            mixed = jnp.concatenate([mixed[:, :QB], mixed[:, QB:]], axis=0).astype(BF16)
            lse_ref[index, p : p + 1] = top + jnp.log(total)
            ot_ref[feat[p], cols] = mixed
            mixed = mixed.T
            o_ref[turn // taken, lax.rem(turn, taken), :, feat[p]] = mixed
            if first_ref is not None:

                @pl.when(lax.rem(turn, taken) == 0)
                def _():
                    first_ref[turn // taken, 0, :, feat[p]] = mixed

        return 0

    lax.fori_loop(0, owners * taken, finish, 0)


def schedule_size(blocks):
    return blocks * ((2 * MOST + 2 * QB) // KB + 1) + 4


def attend(lengths, qt, k, vt, begin, end, steps, before=()):
    feats, rows = qt.shape
    pairs = feats // PAIR
    owners = rows // (steps * QB)
    share = (end - begin) / steps
    blocks = owners * (end - begin)
    first = []
    if begin == 0 and steps > 1:
        first = [jax.ShapeDtypeStruct((owners, 1, QB, feats), BF16)]
    return pl.pallas_call(
        functools.partial(attend_kernel, begin, steps),
        in_specs=[SMEM, VMEM, ANY, ANY] + [VMEM] * len(before),
        out_specs=[VMEM] * (3 + len(first)),
        out_shape=[jax.ShapeDtypeStruct((owners, end - begin, QB, feats), BF16)]
        + first
        + [
            jax.ShapeDtypeStruct((feats, rows), BF16),
            jax.ShapeDtypeStruct((rows // QB, pairs, 2 * QB), F32),
        ],
        scratch_shapes=[
            pltpu.VMEM((rows, feats), BF16),
            pltpu.VMEM((feats, rows), BF16),
            pltpu.SemaphoreType.DMA((2,)),
            pltpu.SMEM((2, schedule_size(blocks)), jnp.int32),
            pltpu.VMEM((blocks, 8, QB), jnp.int32),
            pltpu.VMEM((blocks, pairs, PAIR, 2 * QB), BF16),
            pltpu.VMEM((blocks, 8, 2 * QB), F32),
            pltpu.VMEM((blocks, pairs, HD, 2 * QB), F32),
            pltpu.VMEM((2, 8, 2 * QB), F32),
            pltpu.VMEM((2, pairs, KB, 2 * QB), F32),
            pltpu.VMEM((2, pairs, KB, 2 * QB), BF16),
        ],
        compiler_params=pltpu.CompilerParams(vmem_limit_bytes=VMEM_CAP),
        cost_estimate=pl.CostEstimate(
            flops=int(8 * share * rows * rows * feats),
            bytes_accessed=rows * feats * 10,
            transcendentals=int(share * rows * rows),
        ),
        name="attend",
    )(lengths, qt, k, vt, *before)


def attend_back_kernel(
    len_ref, qt_ref, k_hbm, kt_hbm, v_hbm, do_ref, ot_ref, lse_ref, cos_hbm, sin_hbm,
    grad_hbm, grad_t_hbm, grad_ref, grad_t_ref, k_ref, kt_ref, v_ref, cos_ref, sin_ref, load_sem, out_sem, sched, window, q_diag, do_diag, stat, dq_acc, dk_acc, dv_acc,
    score_buf, prob_grad_buf, prob_buf, score_grad_buf,
):
    feats, rows = qt_ref.shape
    pairs = range(feats // PAIR)
    feat = [pl.ds(p * PAIR, PAIR) for p in pairs]
    loads = (
        (k_hbm, k_ref), (kt_hbm, kt_ref), (v_hbm, v_ref), (cos_hbm, cos_ref), (sin_hbm, sin_ref),
    )
    loads = [pltpu.make_async_copy(a, b, load_sem.at[i]) for i, (a, b) in enumerate(loads)]
    for copy in loads:
        copy.start()

    def store(turn):
        cols = pl.ds(pl.multiple_of(turn * QB, QB), QB)
        return [
            pltpu.make_async_copy(grad_ref.at[cols], grad_hbm.at[cols], out_sem.at[0, turn]),
            pltpu.make_async_copy(
                grad_t_ref.at[:, cols], grad_t_hbm.at[:, cols], out_sem.at[1, turn]
            ),
        ]

    dk_acc[...] = jnp.zeros_like(dk_acc)
    dv_acc[...] = jnp.zeros_like(dv_acc)
    dq_acc[...] = jnp.zeros_like(dq_acc)

    def prepare(turn, _):
        cols = pl.ds(pl.multiple_of(turn * QB, QB), QB)
        store_window(len_ref, window, turn, turn * QB)
        for p in pairs:
            do_t = do_ref[cols, feat[p]].T
            delta = do_t.astype(F32) * ot_ref[feat[p], cols].astype(F32)
            delta = [jnp.sum(part, axis=0, keepdims=True) for part in (delta[:HD], delta[HD:])]
            q_diag[turn, p] = block_diagonal_t(qt_ref[feat[p], cols])
            do_diag[turn, p] = block_diagonal_t(do_t)
            stat[turn, p : p + 1] = lse_ref[turn, p : p + 1]
            stat[turn, 4 + p : 5 + p] = jnp.concatenate(delta, axis=1)
        return 0

    lax.fori_loop(0, rows // QB, prepare, 0)
    count = fill_schedule(len_ref, sched, rows // QB, lambda turn: turn, rows)
    for copy in loads:
        copy.wait()

    def inside(n):
        turn = sched[0, n]
        return inside_window(window[turn, 0:1], window[turn, 1:2], sched[1, n], rows)

    def scores(n, buf, p):
        turn, keys = sched[0, n], key_rows(sched[1, n], rows)
        score_buf[buf, p] = mm(k_ref[keys, feat[p]], q_diag[turn, p])
        prob_grad_buf[buf, p] = mm(v_ref[keys, feat[p]], do_diag[turn, p])

    def soften(n, buf, p, mask):
        turn = sched[0, n]
        lse, delta = stat[turn, p : p + 1], stat[turn, 4 + p : 5 + p]
        prob = jnp.where(mask, jnp.exp(score_buf[buf, p] - lse), 0.0)
        prob_buf[buf, p] = prob.astype(BF16)
        score_grad_buf[buf, p] = (prob * (prob_grad_buf[buf, p] - delta)).astype(BF16)

    def mix(n, buf, p):
        turn, keys = sched[0, n], key_rows(sched[1, n], rows)
        dv_acc[feat[p], keys] += mm_nt(do_diag[turn, p], prob_buf[buf, p])
        dk_acc[feat[p], keys] += mm_nt(q_diag[turn, p], score_grad_buf[buf, p])
        dq_acc[turn, p] += diagonal_blocks(mm(kt_ref[feat[p], keys], score_grad_buf[buf, p]))

    prob_buf[1] = jnp.zeros_like(prob_buf[1])
    score_grad_buf[1] = jnp.zeros_like(score_grad_buf[1])
    run_pipeline(count, pairs, inside, scores, soften, mix)

    def finish(turn, _):
        cols = pl.ds(pl.multiple_of(turn * QB, QB), QB)
        cosine, sine = cos_ref[:, cols], sin_ref[:, cols]
        for p in pairs:
            dq = jnp.concatenate([dq_acc[turn, p, :, :QB], dq_acc[turn, p, :, QB:]], axis=0) * SCALE
            fields = (
                rotate_t(dq, cosine, sine, -1.0),
                rotate_t(dk_acc[feat[p], cols], cosine, sine, -1.0),
                dv_acc[feat[p], cols],
            )
            for kind, field in enumerate(fields):
                place = pl.ds(kind * feats + p * PAIR, PAIR)
                field = field.astype(BF16)
                grad_t_ref[place, cols] = field
                grad_ref[cols, place] = field.T
        for copy in store(turn):
            copy.start()
        return 0

    lax.fori_loop(0, rows // QB, finish, 0)

    def stored(turn, _):
        for copy in store(turn):
            copy.wait()
        return 0

    lax.fori_loop(0, rows // QB, stored, 0)


def attend_back(lengths, qt, k, kt, v, do, ot, lse, cosine, sine):
    feats, rows = qt.shape
    blocks = rows // QB
    return pl.pallas_call(
        attend_back_kernel,
        in_specs=[SMEM, VMEM] + [ANY] * 3 + [VMEM] * 3 + [ANY] * 2,
        out_specs=[ANY, ANY],
        out_shape=[
            jax.ShapeDtypeStruct((rows, 3 * feats), BF16),
            jax.ShapeDtypeStruct((3 * feats, rows), BF16),
        ],
        scratch_shapes=[
            pltpu.VMEM((rows, 3 * feats), BF16),
            pltpu.VMEM((3 * feats, rows), BF16),
            pltpu.VMEM((rows, feats), BF16),
            pltpu.VMEM((feats, rows), BF16),
            pltpu.VMEM((rows, feats), BF16),
            pltpu.VMEM(cosine.shape, F32),
            pltpu.VMEM(sine.shape, F32),
            pltpu.SemaphoreType.DMA((5,)),
            pltpu.SemaphoreType.DMA((2, blocks)),
            pltpu.SMEM((2, schedule_size(blocks)), jnp.int32),
            pltpu.VMEM((blocks, 8, QB), jnp.int32),
            pltpu.VMEM((blocks, feats // PAIR, PAIR, 2 * QB), BF16),
            pltpu.VMEM((blocks, feats // PAIR, PAIR, 2 * QB), BF16),
            pltpu.VMEM((blocks, 8, 2 * QB), F32),
            pltpu.VMEM((blocks, feats // PAIR, HD, 2 * QB), F32),
            pltpu.VMEM((feats, rows), F32),
            pltpu.VMEM((feats, rows), F32),
        ]
        + [pltpu.VMEM((2, feats // PAIR, KB, 2 * QB), kind) for kind in (F32, F32, BF16, BF16)],
        compiler_params=pltpu.CompilerParams(vmem_limit_bytes=VMEM_CAP),
        cost_estimate=pl.CostEstimate(
            flops=10 * rows * rows * feats, bytes_accessed=rows * feats * 28, transcendentals=rows * rows
        ),
        name="attend_back",
    )(lengths, qt, k, kt, v, do, ot, lse, cosine, sine)


def neighbours():
    me = lax.axis_index("mp")
    one = lax.rem(me, 2)
    across = me + 1 - 2 * one
    along = lax.rem(me + 2, 4)
    return me, across, along, lax.rem(across + 2, 4)


def remote(src, dst, sems, kind, step, device):
    send, recv = sems
    return pltpu.make_async_remote_copy(
        src_ref=src,
        dst_ref=dst,
        send_sem=send.at[kind, step],
        recv_sem=recv.at[kind, step],
        device_id={"mp": device},
        device_id_type=MESH,
    )


def pack_neighbours(packs):
    index = lax.axis_index("dp")
    core, chip = lax.rem(index, 2), index // 2
    chips = packs // 2
    return core, chip, index + 1 - 2 * core, [
        lax.rem(index + 2 * shift, packs) for shift in range(1, chips)
    ]


def chip_across(chip, bits):
    low, high = lax.rem(chip, 2), chip // 2
    low = 1 - low if bits % 2 else low
    high = 1 - high if bits // 2 else high
    return low + 2 * high


def remote_pack(src, dst, send, recv, device):
    return pltpu.make_async_remote_copy(
        src_ref=src, dst_ref=dst, send_sem=send, recv_sem=recv,
        device_id={"dp": device}, device_id_type=MESH,
    )


CHIPS = 4
PILES = (((0, 2), 0), ((1, 3), 0), ((0, 1), 2), ((2, 3), 2))
PARTNERS = (1, 2)


def group_barrier(devices, packs=()):
    barrier = pltpu.get_barrier_semaphore()
    for device in devices:
        pl.semaphore_signal(barrier, inc=1, device_id={"mp": device}, device_id_type=MESH)
    for device in packs:
        pl.semaphore_signal(barrier, inc=1, device_id={"dp": device}, device_id_type=MESH)
    pl.semaphore_wait(barrier, len(devices) + len(packs))


def scatter_first(part, slot, from_x, from_y, sems, kind, step):
    me, x, y, d = neighbours()
    return [
        remote(part.at[slot, x, 0], from_x.at[step, 0], sems, kind, step, x),
        remote(part.at[slot, y, 1], from_y.at[step, 0], sems, kind + 1, step, y),
        remote(part.at[slot, d, 0], from_x.at[step, 1], sems, kind + 2, step, x),
        remote(part.at[slot, d, 1], from_y.at[step, 1], sems, kind + 3, step, y),
    ]


def scatter_second(from_x, from_y, last_x, last_y, sems, kind, step):
    me, x, y, d = neighbours()
    return [
        remote(from_x.at[step, 1], last_y.at[step], sems, kind + 4, step, y),
        remote(from_y.at[step, 1], last_x.at[step], sems, kind + 5, step, x),
    ]


def scatter_middle(part, slot, from_x, from_y, last_x, last_y, sems, kind, step):
    me, x, y, d = neighbours()
    first = scatter_first(part, slot, from_x, from_y, sems, kind, step)
    second = scatter_second(from_x, from_y, last_x, last_y, sems, kind, step)
    first[2].wait_recv()
    total = from_x[step, 1].astype(F32) + part[slot, y, 0].astype(F32)
    from_x[step, 1] = total.astype(BF16)
    second[0].start()
    first[3].wait_recv()
    total = from_y[step, 1].astype(F32) + part[slot, x, 1].astype(F32)
    from_y[step, 1] = total.astype(BF16)
    second[1].start()


def scatter_last(part, slot, from_x, from_y, last_x, last_y, sems, kind, step):
    me, x, y, d = neighbours()
    first = scatter_first(part, slot, from_x, from_y, sems, kind, step)
    second = scatter_second(from_x, from_y, last_x, last_y, sems, kind, step)
    first[0].wait_recv()
    first[1].wait_recv()
    second[0].wait_recv()
    second[1].wait_recv()
    upper = part[slot, me, 0].astype(F32) + from_x[step, 0].astype(F32) + last_y[step].astype(F32)
    lower = part[slot, me, 1].astype(F32) + from_y[step, 0].astype(F32) + last_x[step].astype(F32)
    for copy in first + second:
        copy.wait_send()
    return jnp.concatenate([upper, lower], axis=0)


def ffn_kernel(
    packs,
    len_ref, early0, early1, early2, early3, o_hbm, tok_hbm, cot_hbm, wo0, wo1, wo2, wo3, wg_hbm, wu_hbm, wd_hbm, gain_ref, bias_ref,
    h1_hbm, dh1_hbm, sums_ref, do_hbm, land_hbm, down0_hbm, down1_hbm, down2_hbm, down3_hbm, rows_hbm, *rest,
):
    chips = packs // 2
    piles = rest[: len(PILES)]
    (
        wo, wg, wu, wd, o_all, tok, cot, h1_all, hid, dgate, dup, part, from_x, from_y, last_x, last_y,
        a2_t, eb_t, acc, stage, do_own, db_own, h1_ref, dh1_ref, kept_sem, load_sem, tok_sem, cot_sem, own_sem, early_sem, stage_sem, put_sem, pile_sem,
        core_send, core_recv, send_sem, recv_sem,
    ) = rest[len(PILES) :]
    core, chip, other_core, _ = pack_neighbours(packs)
    steps, owners, block, width = o_all.shape
    share = width // packs
    feats = o_hbm.shape[-1]
    size = owners * block
    tiles = [pl.ds(at, TILE) for at in range(0, width, TILE)]
    early = early0.shape[1]
    some = owners
    sems = (send_sem, recv_sem)
    me, x, y, d = neighbours()
    row_total = owners * steps * block
    live_end = row_total - len_ref[0, len_ref.shape[1] - 1]

    loads = [(wg_hbm, wg), (wu_hbm, wu), (wd_hbm, wd)]
    for source, group in ((wo0, me), (wo1, x), (wo2, y), (wo3, d)):
        loads.append((source, wo.at[pl.ds(pl.multiple_of(group * feats, feats), feats)]))
    loads = [pltpu.make_async_copy(a, b, load_sem.at[i]) for i, (a, b) in enumerate(loads)]

    def fetch(step):
        slot = lax.rem(step, 2)
        return (
            pltpu.make_async_copy(tok_hbm.at[:, step], tok.at[slot], tok_sem.at[slot]),
            pltpu.make_async_copy(cot_hbm.at[:, step], cot.at[slot], cot_sem.at[slot]),
        )

    def lanes(group):
        return pl.ds(pl.multiple_of(group * feats, feats), feats)

    def early_copies(step):
        return [
            pltpu.make_async_copy(
                source.at[:, step], o_all.at[step, :, :, lanes(group)], early_sem.at[step, i]
            )
            for i, (source, group) in enumerate(
                ((early0, me), (early1, x), (early2, y), (early3, d))
            )
            if step < source.shape[1]
        ]

    def own_copy(step):
        return pltpu.make_async_copy(
            o_hbm.at[:, step - early], o_all.at[step, :, :, lanes(me)], own_sem.at[step]
        )

    def gather_own(step):
        source, target = o_hbm.at[:, step - early], o_all.at[step, :, :, lanes(me)]
        return [
            remote(source, target, sems, 0, step, x),
            remote(source, target, sems, 1, step, y),
        ]

    halfway = owners // 2

    def gather_relay(step):
        upper = o_all.at[step, pl.ds(0, halfway), :, lanes(x)]
        lower = o_all.at[step, pl.ds(halfway, halfway), :, lanes(y)]
        return [
            remote(upper, upper, sems, 2, step, y),
            remote(lower, lower, sems, 3, step, x),
        ]

    def relay(step):
        for copy, passed in zip(gather_own(step), gather_relay(step)):
            copy.wait_recv()
            passed.start()

    outgoing = (hid, dgate, dup)

    def to_core(kind):
        source = outgoing[kind] if kind < 3 else stage.at[steps % 2].reshape(size, width)
        return remote_pack(
            source, land_hbm.at[kind], core_send.at[kind], core_recv.at[kind], other_core
        )

    def landed(kind):
        return pltpu.make_async_copy(
            land_hbm.at[kind], tok.at[kind % 2].reshape(size, width), tok_sem.at[kind % 2]
        )

    def pile_copies(kind):
        summed = cot.at[kind % 2].reshape(size, width)
        return [
            pltpu.make_async_copy(
                summed.at[pl.ds(pl.multiple_of(chip_across(chip, bits) * share, share), share)],
                pile.at[i, kind - first],
                pile_sem.at[kind % 2, bits],
            )
            for pile, (places, first) in zip(piles, PILES)
            for i, bits in enumerate(places)
            if first <= kind < first + 2
        ]

    def sum_kind(kind):
        landed(kind).wait()
        if kind >= 2:
            for copy in pile_copies(kind - 2):
                copy.wait()
        theirs = tok[kind % 2].reshape(size, width)
        if kind < 3:
            mine = [
                acc[kind, pl.ds(pl.multiple_of((2 * z + core) * share, share), share), :]
                for z in range(chips)
            ]
            mine = jnp.concatenate(mine, axis=0)
        else:
            mine = h1_all[...].reshape(size, width)
        total = (mine + theirs.astype(F32)).astype(BF16)
        cot[kind % 2] = total.reshape(owners, block, width)
        for copy in pile_copies(kind):
            copy.start()

    def put_middle_rows():
        return [
            remote(stage.at[MIDDLE % 2, target], rows_hbm.at[2 + i], sems, 15 + i, 0, target)
            for i, target in enumerate((x, y, d))
        ]

    def put_rows():
        slot = (steps - 1) % 2
        return [
            remote(stage.at[slot, target], rows_hbm.at[i], sems, 13 + i, 0, target)
            for i, target in enumerate((x, y))
        ]

    def put_do(step):
        return [
            remote(do_own.at[step, target], do_hbm.at[me, step], sems, 10 + i, step, target)
            for i, target in enumerate((x, y, d))
        ]

    def keep_rows(step):
        return [
            pltpu.make_async_copy(source.at[step], out.at[step], kept_sem.at[i, step])
            for i, (source, out) in enumerate(((h1_ref, h1_hbm), (dh1_ref, dh1_hbm)))
        ]

    def keep_do(step):
        return pltpu.make_async_copy(do_own.at[step, me], do_hbm.at[me, step], put_sem.at[step])

    for copy in fetch(0):
        copy.start()
    for copy in loads:
        copy.start()
    for step in range(early):
        for copy in early_copies(step):
            copy.start()
    group_barrier((x, y, d), (other_core,))

    def begin(step, _):
        for copy in gather_own(step):
            copy.start()
        own_copy(step).start()
        return 0

    lax.fori_loop(early, steps, begin, 0)
    acc[...] = jnp.zeros_like(acc)
    sums_ref[...] = jnp.zeros_like(sums_ref)
    for copy in loads:
        copy.wait()

    def step_body(step, _):
        slot = lax.rem(step, 2)
        now, before, older = [lax.rem(step + lag, 3) for lag in (0, 2, 1)]

        @pl.when(step + 1 < steps)
        def _():
            for copy in fetch(step + 1):
                copy.start()

        @pl.when((step + 1 < steps) & (step + 1 >= early))
        def _():
            relay(step + 1)

        for which in range(early):

            @pl.when(step == which)
            def _():
                if which == 0:
                    for copy in early_copies(0):
                        copy.wait()
                    for after in range(1, early):
                        for copy in early_copies(after):
                            copy.wait()
                        for copy in gather_relay(after):
                            copy.start()
                else:
                    for copy in gather_relay(which):
                        copy.wait_recv()

        @pl.when((step < steps) & (step >= early))
        def _():
            for copy in gather_relay(step):
                copy.wait_recv()
            own_copy(step).wait()

        @pl.when(step < steps)
        def _():
            for copy in fetch(step):
                copy.wait()
            def some_rows(turn, _):
                count = some * block
                who = pl.ds(turn * some, some)
                rows = pl.ds(pl.multiple_of(turn * count, count), count)
                position = lax.broadcasted_iota(jnp.int32, (some, block, 1), 1) + step * block
                position = position + (steps * block) * (
                    lax.broadcasted_iota(jnp.int32, (some, block, 1), 0) + turn * some
                )
                eb = jnp.where(position < live_end, cot[slot, who].astype(F32), 0.0).astype(BF16)
                cot[slot, who] = eb
                eb = eb.reshape(count, width)
                mixed = o_all[step, who].reshape(count, width)
                for cols in tiles:
                    h1 = tok[slot, who, :, cols].reshape(count, TILE).astype(F32)
                    h1 = h1 + mm(mixed, wo[:, cols])
                    h1_all[who, :, cols] = h1.reshape(some, block, TILE)
                hat, _ = norm_rows(h1_all[who].reshape(count, width))
                a2 = (hat * gain_ref[...] + bias_ref[...]).astype(BF16)

                def products(cols):
                    return mm(a2, wg[:, cols]), mm(a2, wu[:, cols]), mm_nt(eb, wd[cols, :])

                def hidden(cols, gate, up, back):
                    sig = 0.5 * jnp.tanh(0.5 * gate) + 0.5
                    act = gate * sig
                    hid[rows, cols] = (act * up).astype(BF16)
                    dgate[rows, cols] = (back * up * (sig + act * (1.0 - sig))).astype(BF16)
                    dup[rows, cols] = (back * act).astype(BF16)

                ready = products(tiles[0])
                a2_t[:, rows] = a2.T
                eb_t[:, rows] = eb.T
                for cols, ahead in zip(tiles, tiles[1:] + [None]):
                    coming = products(ahead) if ahead is not None else None
                    hidden(cols, *ready)
                    ready = coming
                for cols in tiles:
                    dc = mm_nt(dgate[rows, :], wg[cols, :]) + mm_nt(dup[rows, :], wu[cols, :])
                    part[now, who, :, :, cols] = dc.astype(BF16).reshape(some, 2, block // 2, TILE)
                return 0

            lax.fori_loop(0, owners // some, some_rows, 0)
            h1_ref[step] = h1_all[me]
            dh1_ref[step] = cot[slot, me].astype(F32)
            for copy in scatter_first(part, now, from_x, from_y, sems, 4, step):
                copy.start()

        @pl.when(step == steps)
        def _():
            for kind in range(3):
                for z in range(chips):
                    rows = pl.ds(pl.multiple_of((2 * z + 1 - core) * share, share), share)
                    outgoing[kind][z * share : (z + 1) * share, :] = acc[kind, rows, :].astype(BF16)
                to_core(kind).start()

        @pl.when((step >= 1) & (step <= steps))
        def _():
            scatter_middle(
                part, before, from_x, from_y, last_x, last_y, sems, 4, step - 1
            )

        @pl.when(step == steps)
        def _():
            for kind in range(2):
                to_core(kind).wait_recv()
                landed(kind).start()
            sum_kind(0)
            to_core(2).wait_recv()
            landed(2).start()
            sum_kind(1)
            sum_kind(2)

        def stage_copies(at, to_diagonal, to_neighbours):
            slot = lax.rem(at, 2)
            places = [(me, down0_hbm.at[at])]
            if to_diagonal:
                places.append((d, down3_hbm.at[at - at // 3]))
            if to_neighbours:
                places += [(x, down1_hbm.at[at - at // 3]), (y, down2_hbm.at[at - at // 3])]
            return [
                pltpu.make_async_copy(stage.at[slot, who], out, stage_sem.at[i, slot])
                for i, (who, out) in enumerate(places)
            ]

        @pl.when(step < steps)
        def _():
            @pl.when(step == MIDDLE + 2)
            def _():
                for copy in stage_copies(step - 2, False, False):
                    copy.wait()
                for copy in put_middle_rows():
                    copy.wait_send()

            @pl.when((step >= 2) & (step != MIDDLE + 2))
            def _():
                for copy in stage_copies(step - 2, True, True):
                    copy.wait()

            def some_output(turn, _):
                count = some * block
                who = pl.ds(turn * some, some)
                rows = pl.ds(pl.multiple_of(turn * count, count), count)
                for cols in tiles:
                    partial = mm(hid[rows, :], wd[:, cols]).astype(BF16)
                    stage[slot, who, :, cols] = partial.reshape(some, block, TILE)
                return 0

            lax.fori_loop(0, owners // some, some_output, 0)

            @pl.when(step == MIDDLE)
            def _():
                for copy in stage_copies(step, False, False) + put_middle_rows():
                    copy.start()

            @pl.when((step != MIDDLE) & (step < steps - 1))
            def _():
                for copy in stage_copies(step, True, True):
                    copy.start()

            @pl.when(step == steps - 1)
            def _():
                for copy in stage_copies(step, True, False):
                    copy.start()

            def some_grads(turn, _):
                rows = pl.ds(pl.multiple_of(turn * size, size), size)
                for cols in tiles:
                    acc[0, rows, cols] += mm(a2_t[rows, :], dgate[:, cols])
                    acc[1, rows, cols] += mm(a2_t[rows, :], dup[:, cols])
                    acc[2, rows, cols] += mm(eb_t[rows, :], hid[:, cols])
                return 0

            lax.fori_loop(0, width // size, some_grads, 0)

        @pl.when(step == steps)
        def _():
            for copy in stage_copies(steps - 2, True, True) + stage_copies(steps - 1, True, False):
                copy.wait()

        @pl.when(step >= 2)
        def _():
            prev = step - 2
            dc = scatter_last(part, older, from_x, from_y, last_x, last_y, sems, 4, prev)
            hat, scale = norm_rows(h1_ref[prev])
            sums_ref[0:1] += jnp.sum(dc * hat, axis=0, keepdims=True)
            sums_ref[1:2] += jnp.sum(dc, axis=0, keepdims=True)
            inner = dc * gain_ref[...]
            inner = inner - jnp.mean(inner, axis=-1, keepdims=True) - hat * jnp.mean(
                inner * hat, axis=-1, keepdims=True
            )
            dh1 = dh1_ref[prev] + scale * inner
            dh1_ref[prev] = dh1
            for copy in keep_rows(prev):
                copy.start()
            db = dh1.astype(BF16)
            db_own[prev] = db
            back = mm_nt(db, wo[...]).astype(BF16)
            for group in range(owners):
                do_own[prev, group] = back[:, group * feats : (group + 1) * feats]
            for copy in put_do(prev):
                copy.start()
            keep_do(prev).start()

        @pl.when(step == steps)
        def _():
            for copy in put_rows():
                copy.start()

        return 0

    lax.fori_loop(0, steps + 2, step_body, 0)

    o_mine = jnp.concatenate([o_all[step, me] for step in range(steps)], axis=0)
    for turn, which in enumerate((1 - core, core)):
        columns = [
            db_own[:, :, pl.ds(pl.multiple_of((2 * z + which) * share, share), share)].reshape(
                steps * block, share
            )
            for z in range(chips)
        ]
        values = mm_tn(jnp.concatenate(columns, axis=1), o_mine)
        if turn == 0:
            stage[steps % 2] = values.astype(BF16).reshape(owners, block, width)
            to_core(3).start()
        else:
            h1_all[...] = values.reshape(owners, block, width)

    to_core(3).wait_recv()
    landed(3).start()
    sum_kind(3)
    for kind in range(4):
        to_core(kind).wait_send()
    for copy in pile_copies(2) + pile_copies(3):
        copy.wait()

    for step in range(1, early):
        for copy in gather_relay(step):
            copy.wait_send()

    def sent(step, _):
        for copy in gather_own(step) + gather_relay(step):
            copy.wait_send()
        return 0

    lax.fori_loop(early, steps, sent, 0)

    for copy in put_rows():
        copy.wait()
    for copy in put_middle_rows():
        copy.wait_recv()

    def finish(step, _):
        for copy in put_do(step) + keep_rows(step):
            copy.wait()
        keep_do(step).wait()
        return 0

    lax.fori_loop(0, steps, finish, 0)


def ffn(lengths, early, o, tokens, cotangent, wo, wg, wu, wd, gain, bias, steps, packs):
    rows, width = tokens.shape
    feats = o.shape[-1]
    owners = width // feats
    block = rows // (owners * steps)
    hidden = wg.shape[1]
    size = owners * block
    chips = packs // 2
    by_owner = lambda a: a.reshape(owners, steps, block, a.shape[1])
    own = jax.ShapeDtypeStruct((steps, block, width), F32)
    half = (steps, 2, block // 2, width)
    dma = pltpu.SemaphoreType.DMA
    flops = 2 * rows * width * (width + 9 * hidden)
    h1, dh1, sums, do, _, *rest = pl.pallas_call(
        functools.partial(ffn_kernel, packs),
        in_specs=[SMEM] + [ANY] * 14 + [VMEM, VMEM],
        out_specs=[ANY, ANY, VMEM] + [ANY] * (7 + len(PILES)),
        out_shape=[
            own,
            own,
            jax.ShapeDtypeStruct((2, width), F32),
            jax.ShapeDtypeStruct((owners, steps, block, feats), BF16),
            jax.ShapeDtypeStruct((4, size, width), BF16),
        ]
        + [
            jax.ShapeDtypeStruct((taken, block, width), BF16)
            for taken in (steps, steps - 2, steps - 2, steps - 1, 5)
        ]
        + [jax.ShapeDtypeStruct((2, 2, width // packs, width), BF16)] * len(PILES),
        scratch_shapes=[
            pltpu.VMEM((width, width), BF16),
            pltpu.VMEM((width, hidden), BF16),
            pltpu.VMEM((width, hidden), BF16),
            pltpu.VMEM((hidden, width), BF16),
            pltpu.VMEM((steps, owners, block, width), BF16),
            pltpu.VMEM((2, owners, block, width), BF16),
            pltpu.VMEM((2, owners, block, width), BF16),
            pltpu.VMEM((owners, block, width), F32),
            pltpu.VMEM((size, hidden), BF16),
            pltpu.VMEM((size, hidden), BF16),
            pltpu.VMEM((size, hidden), BF16),
            pltpu.VMEM((3, owners, 2, block // 2, width), BF16),
            pltpu.VMEM(half, BF16),
            pltpu.VMEM(half, BF16),
            pltpu.VMEM((steps, block // 2, width), BF16),
            pltpu.VMEM((steps, block // 2, width), BF16),
            pltpu.VMEM((width, size), BF16),
            pltpu.VMEM((width, size), BF16),
            pltpu.VMEM((3, width, hidden), F32),
            pltpu.VMEM((2, owners, block, width), BF16),
            pltpu.VMEM((steps, owners, block, feats), BF16),
            pltpu.VMEM((steps, block, width), BF16),
            pltpu.VMEM(own.shape, F32),
            pltpu.VMEM(own.shape, F32),
            dma((2, steps)),
            dma((7,)),
            dma((2,)),
            dma((2,)),
            dma((steps,)),
            dma((early[0].shape[1], 4)),
            dma((4, 2)),
            dma((steps,)),
            dma((2, chips)),
            dma((4,)),
            dma((4,)),
            dma((18, steps)),
            dma((18, steps)),
        ],
        compiler_params=pltpu.CompilerParams(
            collective_id=0, has_side_effects=True, vmem_limit_bytes=VMEM_CAP
        ),
        cost_estimate=pl.CostEstimate(flops=flops, bytes_accessed=rows * width * 14, transcendentals=0),
        name="ffn",
    )(lengths, *early, o, by_owner(tokens), by_owner(cotangent), *wo, wg, wu, wd, gain, bias)
    return h1, dh1, sums, do.reshape(rows, feats), rest[:5], rest[5:]


def last_kernel(
    packs,
    grad_hbm, grad_t_hbm, a1_hbm, tok_hbm, dh1_hbm, h1_hbm, wq_hbm, wk_hbm, wv_hbm, gain_ref, sums2_ref, *rest,
):
    chips = packs // 2
    downs, rest = rest[:5], rest[5:]
    piles, rest = rest[: len(PILES)], rest[len(PILES) :]
    (
        out_hbm, tg_hbm, gq_hbm, gk_hbm, gv_hbm, gate_hbm, up_hbm, down_hbm, proj_hbm, norm_ref,
        out_ref, tg_ref, gq_ref, gk_ref, gv_ref, gate_ref, up_ref, down_ref, proj_ref, row_sem, result_sem,
        dh1_ref, wq_ref, wk_ref, wv_ref, weight_sem,
        grad, grad_t, a1, tok, part, from_x, from_y, last_x, last_y, h1, down, pile, pile_out, pile_in, sums1,
        full, core_out, core_in, chip_out, chip_in, proj_out, proj_in, norm_out, norm_in,
        grad_sem, tok_sem, load_sem, core_send, core_recv, chip_send, chip_recv, pile_send, pile_recv,
        small_send, small_recv, send_sem, recv_sem,
    ) = rest
    steps, owners, _, half, width = part.shape
    feats = wq_hbm.shape[1]
    size = owners * 2 * half
    share = width // packs
    tall = 3 * feats
    sems = (send_sem, recv_sem)
    me, x, y, d = neighbours()
    core, chip, other_core, next_chips = pack_neighbours(packs)

    def fetch(step):
        return [
            pltpu.make_async_copy(grad_hbm.at[:, step], grad.at[step], grad_sem.at[step]),
            pltpu.make_async_copy(tok_hbm.at[:, step], tok.at[step], tok_sem.at[step]),
        ]

    later = [(grad_t_hbm, grad_t), (a1_hbm, a1)]
    later += [(piles[i], pile.at[i]) for i in range(len(PILES))]
    later += [(h1_hbm, h1)]
    later += [(downs[0], down.at[0])]
    after = MIDDLE + 1
    for i in range(1, 4):
        left = downs[i].shape[0] - MIDDLE
        later += [(downs[i].at[pl.ds(0, MIDDLE)], down.at[i, pl.ds(0, MIDDLE)])]
        later += [(downs[i].at[pl.ds(MIDDLE, left)], down.at[i, pl.ds(after, left)])]
    later += [(downs[4].at[pl.ds(0, 2)], down.at[pl.ds(1, 2), steps - 1])]
    later += [(downs[4].at[pl.ds(2, 3)], down.at[pl.ds(1, 3), MIDDLE])]
    later = [pltpu.make_async_copy(a, b, load_sem.at[i]) for i, (a, b) in enumerate(later)]

    def to_core():
        return remote_pack(core_out, core_in, core_send, core_recv, other_core)

    def to_chips():
        return [
            remote_pack(
                chip_out.at[lax.rem(chip + i + 1, chips)], chip_in.at[i],
                chip_send.at[i], chip_recv.at[i], device,
            )
            for i, device in enumerate(next_chips)
        ]

    def pile_copies():
        index = lax.axis_index("dp")
        return [
            remote_pack(
                pile_out.at[i], pile_in.at[i], pile_send.at[i], pile_recv.at[i],
                index + 2 * (chip_across(chip, bits) - chip),
            )
            for i, bits in enumerate(reversed(PARTNERS))
        ]

    def small(kind, source, target):
        return [
            remote(source(device), target.at[i], (small_send, small_recv), kind, i, device)
            for i, device in enumerate((x, y, d))
        ]

    def proj_copies():
        return small(0, lambda device: proj_out.at[device], proj_in)

    def norm_copies():
        return small(1, lambda device: norm_out, norm_in)

    def begin(step, _):
        for copy in fetch(step):
            copy.start()
        return 0

    weights = ((wq_hbm, wq_ref), (wk_hbm, wk_ref), (wv_hbm, wv_ref), (dh1_hbm, dh1_ref))
    weights = [pltpu.make_async_copy(a, b, weight_sem.at[i]) for i, (a, b) in enumerate(weights)]
    for copy in weights[:3]:
        copy.start()
    lax.fori_loop(0, steps, begin, 0)
    for copy in later + weights[3:]:
        copy.start()
    group_barrier((x, y, d), [other_core] + next_chips)
    sums1[...] = jnp.zeros_like(sums1)

    for copy in weights[:3]:
        copy.wait()

    def first(step, _):
        for copy in fetch(step):
            copy.wait()
        rows = grad[step].reshape(size, tall)
        da = mm_nt(rows[:, :feats], wq_ref[...])
        da = da + mm_nt(rows[:, feats : 2 * feats], wk_ref[...])
        da = da + mm_nt(rows[:, 2 * feats :], wv_ref[...])
        part[step] = da.astype(BF16).reshape(owners, 2, half, width)
        for copy in scatter_first(part, step, from_x, from_y, sems, 0, step):
            copy.start()

        @pl.when(step == 0)
        def _():
            for copy in later[2 : 2 + len(PILES)]:
                copy.wait()
            for i in range(2):
                total = pile[2 * i, 1].astype(F32) + pile[2 * i + 1, 1].astype(F32)
                pile_out[i] = total.astype(BF16)
            for copy in pile_copies():
                copy.start()

        hat, _ = norm_rows(tok[step].reshape(size, width).astype(F32))
        sums1[0:1] += jnp.sum(da * hat, axis=0, keepdims=True)
        sums1[1:2] += jnp.sum(da, axis=0, keepdims=True)
        return 0

    lax.fori_loop(0, steps, first, 0)
    later[0].wait()
    later[1].wait()
    for kind in range(3):
        rows = pl.ds(kind * feats, feats)
        full[rows, :] = mm(grad_t[rows, :], a1[...])
    full[pl.ds(tall, 16), :] = jnp.concatenate(
        [sums1[...], sums2_ref[...], jnp.zeros((12, width), F32)], axis=0
    )
    for z in range(chips):
        columns = pl.ds(pl.multiple_of((2 * z + 1 - core) * share, share), share)
        core_out[z] = full[:, columns].astype(BF16)
    to_core().start()

    to_core().wait_recv()
    for z in range(chips):
        columns = pl.ds(pl.multiple_of((2 * z + core) * share, share), share)
        chip_out[z] = (full[:, columns] + core_in[z].astype(F32)).astype(BF16)
    for copy in to_chips():
        copy.start()
    for copy in later[2 + len(PILES) :]:
        copy.wait()

    def sum_piles():
        for copy in pile_copies():
            copy.wait_recv()
        for kind in range(4):
            half, at = kind // 2, kind % 2
            total = pile[2 * half, 0, at].astype(F32) + pile[2 * half + 1, 0, at].astype(F32)
            total = total + pile_in[half, at].astype(F32)
            if kind < 2:
                (gate_ref, up_ref)[kind][...] = total
            elif kind == 2:
                down_ref[...] = total.T
            else:
                for group in range(owners):
                    proj_out[group] = total[:, group * feats : (group + 1) * feats].astype(BF16)
                for copy in proj_copies():
                    copy.start()

    def row_copies(step):
        return [
            pltpu.make_async_copy(source.at[step], out.at[step], row_sem.at[i, step])
            for i, (source, out) in enumerate(((out_ref, out_hbm), (tg_ref, tg_hbm)))
        ]

    results = (
        (gq_ref, gq_hbm), (gk_ref, gk_hbm), (gv_ref, gv_hbm), (gate_ref, gate_hbm),
        (up_ref, up_hbm), (down_ref, down_hbm), (proj_ref, proj_hbm),
    )
    results = [
        pltpu.make_async_copy(source, out, result_sem.at[i])
        for i, (source, out) in enumerate(results)
    ]

    def finish(step):
        da = scatter_last(part, step, from_x, from_y, last_x, last_y, sems, 0, step)
        hat, scale = norm_rows(tok[step, me].astype(F32))
        inner = da * gain_ref[...]
        inner = inner - jnp.mean(inner, axis=-1, keepdims=True) - hat * jnp.mean(
            inner * hat, axis=-1, keepdims=True
        )
        tg_ref[step] = (dh1_ref[step] + scale * inner).astype(BF16)
        row_copies(step)[1].start()

    def second(step, _):
        scatter_middle(part, step, from_x, from_y, last_x, last_y, sems, 0, step)
        total = h1[step]
        for i in range(4):
            total = total + down[i, step].astype(F32)
        out_ref[step] = total.astype(BF16)
        row_copies(step)[0].start()
        return 0

    def third(step, _):
        finish(step)
        return 0

    weights[3].wait()
    lax.fori_loop(0, steps, second, 0)
    sum_piles()
    for copy in results[3:6]:
        copy.start()
    lax.fori_loop(0, steps - 2, third, 0)
    total = chip_out[chip].astype(F32)
    for i, copy in enumerate(to_chips()):
        copy.wait_recv()
        total = total + chip_in[i].astype(F32)
    norm_out[...] = total[tall : tall + 8]
    for copy in norm_copies():
        copy.start()
    finish(steps - 2)
    for kind, ref in enumerate((gq_ref, gk_ref, gv_ref)):
        ref[...] = total[kind * feats : (kind + 1) * feats].T
        results[kind].start()
    total = proj_out[me].astype(F32)
    for i, copy in enumerate(proj_copies()):
        copy.wait_recv()
        total = total + proj_in[i].astype(F32)
    proj_ref[...] = total.T
    results[6].start()
    finish(steps - 1)
    total = norm_out[...]
    for i, copy in enumerate(norm_copies()):
        copy.wait_recv()
        total = total + norm_in[i]
    norm_ref[...] = total
    for copy in results:
        copy.wait()
    for step in range(steps):
        for copy in row_copies(step):
            copy.wait()
    for copy in [to_core()] + to_chips() + pile_copies() + proj_copies() + norm_copies():
        copy.wait_send()


def last(grads, grads_t, a1, tokens, dh1, h1, wq, wk, wv, gain, sums2, downs, piles, packs):
    rows, width = tokens.shape
    steps, block, _ = dh1.shape
    owners = rows // (steps * block)
    feats = wq.shape[1]
    hidden = piles[0].shape[-1]
    chips = packs // 2
    share = width // packs
    tall = 3 * feats + 16
    by_owner = lambda a: a.reshape(owners, steps, block, a.shape[1])
    half = (steps, 2, block // 2, width)
    dma = pltpu.SemaphoreType.DMA
    own = jax.ShapeDtypeStruct((steps, block, width), BF16)
    f32 = lambda *shape: jax.ShapeDtypeStruct(shape, F32)
    out_shape = [own, own] + [f32(share, feats)] * 3
    out_shape += [f32(share, hidden)] * 2 + [f32(hidden, share), f32(feats, share), f32(8, share)]
    return pl.pallas_call(
        functools.partial(last_kernel, packs),
        in_specs=[ANY] * 9 + [VMEM] * 2 + [ANY] * (5 + len(piles)),
        out_specs=[ANY] * 9 + [VMEM],
        out_shape=out_shape,
        scratch_shapes=[pltpu.VMEM(a.shape, a.dtype) for a in out_shape[:9]]
        + [
            dma((2, steps)),
            dma((7,)),
            pltpu.VMEM((steps, block, width), F32),
            pltpu.VMEM((width, feats), BF16),
            pltpu.VMEM((width, feats), BF16),
            pltpu.VMEM((width, feats), BF16),
            dma((4,)),
            pltpu.VMEM((steps, owners, block, 3 * feats), BF16),
            pltpu.VMEM((3 * feats, rows), BF16),
            pltpu.VMEM((rows, width), BF16),
            pltpu.VMEM((steps, owners, block, width), BF16),
            pltpu.VMEM((steps, owners, 2, block // 2, width), BF16),
            pltpu.VMEM(half, BF16),
            pltpu.VMEM(half, BF16),
            pltpu.VMEM((steps, block // 2, width), BF16),
            pltpu.VMEM((steps, block // 2, width), BF16),
            pltpu.VMEM((steps, block, width), F32),
            pltpu.VMEM((4, steps, block, width), BF16),
            pltpu.VMEM((len(PILES), 2, 2, share, hidden), BF16),
            pltpu.VMEM((2, 2, share, hidden), BF16),
            pltpu.VMEM((2, 2, share, hidden), BF16),
            pltpu.VMEM((2, width), F32),
            pltpu.VMEM((tall, width), F32),
            pltpu.VMEM((chips, tall, share), BF16),
            pltpu.VMEM((chips, tall, share), BF16),
            pltpu.VMEM((chips, tall, share), BF16),
            pltpu.VMEM((chips - 1, tall, share), BF16),
            pltpu.VMEM((owners, share, feats), BF16),
            pltpu.VMEM((owners - 1, share, feats), BF16),
            pltpu.VMEM((8, share), F32),
            pltpu.VMEM((owners - 1, 8, share), F32),
            dma((steps,)),
            dma((steps,)),
            dma((12 + len(piles),)),
            dma,
            dma,
            dma((chips - 1,)),
            dma((chips - 1,)),
            dma((2,)),
            dma((2,)),
            dma((2, owners - 1)),
            dma((2, owners - 1)),
            dma((6, steps)),
            dma((6, steps)),
        ],
        compiler_params=pltpu.CompilerParams(
            collective_id=1, has_side_effects=True, vmem_limit_bytes=VMEM_CAP
        ),
        cost_estimate=pl.CostEstimate(
            flops=12 * rows * width * feats, bytes_accessed=rows * width * 20, transcendentals=0
        ),
        name="last",
    )(
        by_owner(grads), grads_t, a1, by_owner(tokens), dh1, h1, wq, wk, wv, gain, sums2, *downs, *piles
    )


def hand_out_kernel(count, *refs):
    sources, outs, held = refs[: count + 1], refs[count + 1 : 2 * count + 5], refs[2 * count + 5 : -2]
    in_sem, out_sem = refs[-2:]
    norm, vectors = held[count], held[count + 1 :]
    loads = [pltpu.make_async_copy(sources[i], held[i], in_sem.at[i]) for i in range(count + 1)]
    ready = list(held[:count]) + list(vectors)
    stores = [
        pltpu.make_async_copy(ready[i], outs[i], out_sem.at[i]) for i in range(count + 4)
    ]
    for copy in reversed(loads):
        copy.start()
    loads[count].wait()
    for i, vector in enumerate(vectors):
        vector[...] = norm[i]
        stores[count + i].start()
    for load, store in zip(loads[:count], stores):
        load.wait()
        store.start()
    for store in stores:
        store.wait()


def hand_out(arrays, norms):
    count = len(arrays)
    shape = lambda a: jax.ShapeDtypeStruct(a.shape, a.dtype)
    vectors = [jax.ShapeDtypeStruct(norms.shape[1:], F32)] * 4
    out_shape = [shape(a) for a in arrays] + vectors
    return pl.pallas_call(
        functools.partial(hand_out_kernel, count),
        in_specs=[ANY] * (count + 1),
        out_specs=[ANY] * (count + 4),
        out_shape=out_shape,
        scratch_shapes=[pltpu.VMEM(a.shape, a.dtype) for a in list(arrays) + [norms] + vectors]
        + [pltpu.SemaphoreType.DMA((count + 4,))] * 2,
        compiler_params=pltpu.CompilerParams(vmem_limit_bytes=VMEM_CAP),
        name="hand_out",
    )(*arrays, norms)


def local_square(
    tokens, lengths, cotangent, norm1_gain, norm1_bias, w_query, w_key, w_value, w_output,
    norm2_gain, norm2_bias, w_gate, w_up, w_down,
):
    rows, width = tokens.shape
    groups = lax.axis_size("mp")
    packs = lax.axis_size("dp")
    gain1, bias1 = norm1_gain[None, :], norm1_bias[None, :]
    exchange = lambda a, shift: lax.ppermute(a, "mp", [(i, i ^ shift) for i in range(groups)])
    w_outputs = [w_output] + [exchange(w_output, shift) for shift in range(1, groups)]
    a1, k, v, qt, kt, vt, cosine, sine = project(
        lengths, tokens, gain1, bias1, w_query, w_key, w_value
    )
    early, early_first, mixed_t, lse = attend(lengths, qt, k, vt, 0, EARLY, STEPS)
    early = [early, exchange(early, 1), exchange(early, 2), exchange(early_first, 3)]
    qt_late, *w_outputs = lax.optimization_barrier((qt, *w_outputs))
    mixed, mixed_t, lse = attend(lengths, qt_late, k, vt, EARLY, STEPS, STEPS, (mixed_t, lse))
    h1, dh1, sums2, mixed_grad, downs, piles = ffn(
        lengths, early, mixed, tokens, cotangent, w_outputs, w_gate, w_up, w_down,
        norm2_gain[None, :], norm2_bias[None, :], STEPS, packs,
    )
    downs[1:4] = [exchange(downs[shift], shift) for shift in range(1, groups)]
    for i, bits in enumerate(PARTNERS):
        perm = [(j, j ^ (2 * bits)) for j in range(packs)]
        piles[2 * i + 1] = lax.ppermute(piles[2 * i + 1], "dp", perm)
    grads, grads_t = attend_back(
        lengths, qt, k, kt, v, mixed_grad, mixed_t, lse, cosine, sine
    )
    *results, norms = last(
        grads, grads_t, a1, tokens, dh1, h1, w_query, w_key, w_value, gain1, sums2, downs, piles, packs
    )
    output, tokens_grad, grad_q, grad_k, grad_v, gate, up, down, proj, *sums = hand_out(
        results, norms
    )
    own_rows = (rows // groups, width)
    return (
        output.reshape(own_rows),
        tokens_grad.reshape(own_rows),
        grad_q,
        grad_k,
        grad_v,
        proj,
        gate,
        up,
        down,
        *sums,
    )


def layer_stats(row_values, gain_vec, bias_vec):
    normed, row_scale = norm_rows(row_values)
    return (normed * gain_vec + bias_vec, normed, row_scale)


def layer_back(gradient, normed, row_scale, gain_vec):
    inner_grad = gradient * gain_vec
    centred_grad = inner_grad - jnp.mean(inner_grad, axis=-1, keepdims=True)
    return row_scale * (
        centred_grad - normed * jnp.mean(inner_grad * normed, axis=-1, keepdims=True)
    )


def scatter_rows(partial, axis, dim=0):
    return lax.psum_scatter(
        partial.astype(BF16), axis, scatter_dimension=dim, tiled=True
    ).astype(F32)


def local(
    tokens, lengths, cotangent, norm1_gain, norm1_bias, w_query, w_key, w_value, w_output,
    norm2_gain, norm2_bias, w_gate, w_up, w_down,
):
    row_count, width = tokens.shape
    feats = w_query.shape[1]
    gain1, bias1 = norm1_gain[None, :], norm1_bias[None, :]
    a1, k, v, qt, kt, vt, cosine, sine = project(
        lengths, tokens, gain1, bias1, w_query, w_key, w_value
    )
    mixed, mixed_t, lse = attend(lengths, qt, k, vt, 0, 1, 1)
    mixed = mixed.reshape(row_count, feats)

    share_rows = row_count // lax.axis_size("mp")
    own_start = lax.axis_index("mp") * share_rows
    own = lambda a: lax.dynamic_slice_in_dim(a, own_start, share_rows, 0)
    live_end = row_count - lengths[0, lengths.shape[1] - 1]
    live = jnp.arange(row_count, dtype=jnp.int32)[:, None] < live_end
    out_grad = jnp.where(live, cotangent, jnp.zeros_like(cotangent))

    attn_rows = scatter_rows(mm(mixed, w_output), "mp")
    residual = own(tokens).astype(F32) + attn_rows
    normed_second, hat_second, scale_second = layer_stats(residual, norm2_gain, norm2_bias)
    inputs_second = lax.all_gather(normed_second.astype(BF16), "mp", axis=0, tiled=True)
    gate_pre = mm(inputs_second, w_gate)
    up_proj = mm(inputs_second, w_up)
    gate_sig = jax.nn.sigmoid(gate_pre)
    gate_act = gate_pre * gate_sig
    hidden = (gate_act * up_proj).astype(BF16)
    output_own = residual + scatter_rows(mm(hidden, w_down), "mp")
    down_w_grad = mm_tn(hidden, out_grad)
    hidden_grad = mm_nt(out_grad, w_down)
    gate_in_grad = (hidden_grad * up_proj * gate_sig * (1.0 + gate_pre * (1.0 - gate_sig))).astype(BF16)
    up_in_grad = (hidden_grad * gate_act).astype(BF16)
    gate_w_grad = mm_tn(inputs_second, gate_in_grad)
    up_w_grad = mm_tn(inputs_second, up_in_grad)
    ffn_sums = (
        scatter_rows(gate_w_grad, "dp"),
        scatter_rows(up_w_grad, "dp"),
        scatter_rows(down_w_grad, "dp", 1),
    )
    second_grad = scatter_rows(mm_nt(gate_in_grad, w_gate) + mm_nt(up_in_grad, w_up), "mp")
    residual_grad = own(out_grad).astype(F32) + layer_back(
        second_grad, hat_second, scale_second, norm2_gain
    )
    attn_grad = lax.all_gather(residual_grad.astype(BF16), "mp", axis=0, tiled=True)
    gain_second_grad = jnp.sum(second_grad * hat_second, axis=0)
    bias_second_grad = jnp.sum(second_grad, axis=0)
    output_w_grad = mm_tn(mixed, attn_grad)
    mixed_grad = mm_nt(attn_grad, w_output).astype(BF16)

    grads, grads_t = attend_back(
        lengths, qt, k, kt, v, mixed_grad, mixed_t, lse, cosine, sine
    )
    w_qkv = jnp.concatenate([w_query, w_key, w_value], axis=1)
    qkv_w_grad = mm(grads_t, a1)
    first_grad = scatter_rows(mm_nt(grads, w_qkv), "mp")
    hat_own, scale_own = norm_rows(own(tokens).astype(F32))
    tokens_grad = (residual_grad + layer_back(first_grad, hat_own, scale_own, norm1_gain)).astype(BF16)
    gain_parts = jnp.stack(
        [
            jnp.sum(first_grad * hat_own, axis=0),
            jnp.sum(first_grad, axis=0),
            gain_second_grad,
            bias_second_grad,
        ]
    )
    gain_parts = scatter_rows(lax.psum(gain_parts, "mp"), "dp", 1)
    attn_sums = scatter_rows(jnp.concatenate([qkv_w_grad, output_w_grad], axis=0), "dp", 1)
    return (
        output_own.astype(BF16),
        tokens_grad,
        attn_sums[:feats].T,
        attn_sums[feats : 2 * feats].T,
        attn_sums[2 * feats : 3 * feats].T,
        attn_sums[3 * feats :],
        ffn_sums[0],
        ffn_sums[1],
        ffn_sums[2],
        gain_parts[0],
        gain_parts[1],
        gain_parts[2],
        gain_parts[3],
    )


def solution(mesh):
    square = mesh.shape["mp"] == 4 and mesh.shape["dp"] == 2 * CHIPS
    rows, weight_in, weight_out = P("dp", None), P(None, "mp"), P("mp", None)
    row_out = P(("dp", "mp"), None)
    return jax.shard_map(
        local_square if square else local,
        mesh=mesh,
        in_specs=(rows, rows, rows, P(), P(), weight_in, weight_in, weight_in, weight_out)
        + (P(), P(), weight_in, weight_in, weight_out),
        out_specs=(row_out, row_out)
        + (P("dp", "mp"),) * 3
        + (P("mp", "dp"), P("dp", "mp"), P("dp", "mp"), P("mp", "dp"))
        + (P("dp"),) * 4,
        check_vma=False,
    )
```
